128 devices in a mesh: dp: 16 (over y, z_lo, core), mp: 8 (over z_hi, x).
Axes of the slice: x: 4, y: 4, z: 4 (z_hi: 2, z_lo: 2; z = z_hi * 2 + z_lo), core: 2. Of those that a mesh axis runs over, the one named last changes fastest.
Arguments:
- tokens: bfloat16 [16384, 2048], P(('dp', 'mp')), may hold values from -6 to 6
- cotangent: bfloat16 [16384, 2048], P(('dp', 'mp')), may hold values from -6 to 6
- attention_norm_scale: bfloat16 [2048], replicated, may hold values from 0.099609375 to 1.8984375
- attention_norm_bias: bfloat16 [2048], replicated, may hold values from -3 to 3
- query_projection: bfloat16 [2048, 2048], P('dp', 'mp'), may hold values from -0.125 to 0.125
- query_projection_bias: bfloat16 [2048], P('mp'), may hold values from -3 to 3
- keyvalue_projection: bfloat16 [2048, 256], P('dp'), may hold values from -0.125 to 0.125
- value_projection_bias: bfloat16 [128], replicated, may hold values from -3 to 3
- attention_output_weight: bfloat16 [2048, 2048], P('mp', 'dp'), may hold values from -0.5 to 0.5
- attention_output_bias: bfloat16 [2048], replicated, may hold values from -3 to 3
- feedforward_norm_scale: bfloat16 [2048], replicated, may hold values from 0.099609375 to 1.8984375
- feedforward_norm_bias: bfloat16 [2048], replicated, may hold values from -3 to 3
- up_projection_weight: bfloat16 [2048, 8192], P('dp', 'mp'), may hold values from -0.125 to 0.125
- up_projection_bias: bfloat16 [8192], P('mp'), may hold values from -3 to 3
- down_projection_weight: bfloat16 [8192, 2048], P('mp', 'dp'), may hold values from -0.0625 to 0.0625
- down_projection_bias: bfloat16 [2048], replicated, may hold values from -3 to 3
- sequence_adapter: int32 [16, 1], P('dp'), may hold values from 0 to 7
- query_adapter_input: bfloat16 [8, 2048, 16], replicated, may hold values from -0.125 to 0.125
- query_adapter_output: bfloat16 [8, 16, 2048], P(None, None, 'mp'), may hold values from -0.75 to 0.75
- keyvalue_adapter_input: bfloat16 [8, 2048, 16], replicated, may hold values from -0.125 to 0.125
- keyvalue_adapter_output: bfloat16 [8, 16, 256], replicated, may hold values from -0.75 to 0.75
- output_adapter_input: bfloat16 [8, 2048, 16], P(None, 'mp'), may hold values from -0.5 to 0.5
- output_adapter_output: bfloat16 [8, 16, 2048], replicated, may hold values from -0.75 to 0.75
- up_adapter_input: bfloat16 [8, 2048, 16], replicated, may hold values from -0.125 to 0.125
- up_adapter_output: bfloat16 [8, 16, 8192], P(None, None, 'mp'), may hold values from -0.75 to 0.75
- down_adapter_input: bfloat16 [8, 8192, 16], P(None, 'mp'), may hold values from -0.0625 to 0.0625
- down_adapter_output: bfloat16 [8, 16, 2048], replicated, may hold values from -0.75 to 0.75
Outputs:
- layer_output: bfloat16 [16384, 2048], P(('dp', 'mp'))
- grad_tokens: bfloat16 [16384, 2048], P(('dp', 'mp'))
- grad_query_lora_a: float32 [8, 2048, 16], replicated
- grad_query_lora_b: float32 [8, 16, 2048], replicated
- grad_keyval_lora_a: float32 [8, 2048, 16], replicated
- grad_keyval_lora_b: float32 [8, 16, 256], replicated
- grad_output_lora_a: float32 [8, 2048, 16], replicated
- grad_output_lora_b: float32 [8, 16, 2048], replicated
- grad_up_lora_a: float32 [8, 2048, 16], replicated
- grad_up_lora_b: float32 [8, 16, 8192], replicated
- grad_down_lora_a: float32 [8, 8192, 16], replicated
- grad_down_lora_b: float32 [8, 16, 2048], replicated
The draws below stay inside these ranges and needn't reach their ends.
Inputs may be any that keep to these rules, and one draw needn't show every extreme that they name: `sequence_adapter`: each of the 8 adapters is chosen by at least one sequence.
All inputs are finite; a program needn't handle non-finite values.
Results may differ from the reference program's by a relative error of at most 0.024.
Values may be sent and summed in bfloat16 or wider, within the bound.
No kernel may reach another device: no remote copies, remote signals or barrier semaphores. Data moves between devices by JAX's collectives and lax.ppermute only.
A program may use at most 192 MiB of HBM per device.

```python
import math
import jax
import jax.numpy as jnp
from jax import lax

MODEL_WIDTH = 2048
H = 16
HEAD_WIDTH = 128
FEED_HIDDEN = 8192
ADAPTER_RANK = 16
ADAPTER_COUNT = 8
BLOCK = 256
QROWS = 512
LEN = 1024
SEQS = 16
TOKENS = 16384


def level_of(rng, extent, pieces, low, largest):
    level = 1.0
    for position, parts in pieces:
        draws = jax.random.uniform(jax.random.fold_in(jax.random.fold_in(rng, 6), position), (parts,), jnp.float32, low / len(pieces), largest / len(pieces))
        level = level * jnp.repeat(jnp.exp(draws), extent[position] // parts).reshape((-1,) + (1,) * (len(extent) - 1 - position))
    return level


def picks_of(own_key, rows, number_of, top, lift):
    order = jax.random.permutation(jax.random.fold_in(own_key, 1), number_of)
    favour = order
    for power in range(3):
        favour = favour * favour // number_of
    favour = favour * lift // number_of
    lots = jax.random.randint(jax.random.fold_in(own_key, 2), (rows, number_of), 0, 4096) + favour
    fixed_rows = jax.random.permutation(jax.random.fold_in(own_key, 3), rows)[jnp.arange(number_of) % rows]
    lots = jnp.where(jnp.arange(rows)[:, None] == fixed_rows[None, :], 1 << 14, lots)
    priority = lots * number_of + jnp.arange(number_of)
    return lax.top_k(priority.astype(jnp.int32), top)[1].astype(jnp.int32)


def scatter_about(rng, dims, spread, reach, shards=(), kind=jnp.bfloat16):
    factor_of = level_of(rng, dims, shards, -0.22, 0.18) if shards else 1.0
    entries = jax.random.normal(rng, dims, jnp.float32) * spread * factor_of
    return jnp.minimum(jnp.maximum(entries, -reach), reach).astype(kind)


def setup_inputs(seed: int = 0) -> dict:
    key_of = jax.random.split(jax.random.key(seed), 28)
    return {
        "tokens": scatter_about(key_of[0], (TOKENS, MODEL_WIDTH), 1.0, 6.0, ((0, 128),)),
        "cotangent": scatter_about(key_of[1], (TOKENS, MODEL_WIDTH), 1.0, 6.0, ((0, 128),)),
        "attention_norm_scale": jnp.clip(1.0 + 0.18 * jax.random.normal(key_of[2], (MODEL_WIDTH,), jnp.float32), 0.099609375, 1.8984375).astype(jnp.bfloat16),
        "attention_norm_bias": scatter_about(key_of[3], (MODEL_WIDTH,), 0.3, 3.0),
        "query_projection": scatter_about(key_of[4], (MODEL_WIDTH, MODEL_WIDTH), MODEL_WIDTH ** -0.5, 0.125, ((0, 16), (1, 8))),
        "query_projection_bias": scatter_about(key_of[5], (MODEL_WIDTH,), 0.3, 3.0, ((0, 8),)),
        "keyvalue_projection": scatter_about(key_of[6], (MODEL_WIDTH, 2 * HEAD_WIDTH), MODEL_WIDTH ** -0.5, 0.125, ((0, 16),)),
        "value_projection_bias": scatter_about(key_of[7], (HEAD_WIDTH,), 0.3, 3.0),
        "attention_output_weight": scatter_about(key_of[8], (MODEL_WIDTH, MODEL_WIDTH), (MODEL_WIDTH // 16) ** -0.5, 0.5, ((0, 8), (1, 16))),
        "attention_output_bias": scatter_about(key_of[9], (MODEL_WIDTH,), 0.3, 3.0),
        "feedforward_norm_scale": jnp.clip(1.0 + 0.18 * jax.random.normal(key_of[10], (MODEL_WIDTH,), jnp.float32), 0.099609375, 1.8984375).astype(jnp.bfloat16),
        "feedforward_norm_bias": scatter_about(key_of[11], (MODEL_WIDTH,), 0.3, 3.0),
        "up_projection_weight": scatter_about(key_of[12], (MODEL_WIDTH, FEED_HIDDEN), MODEL_WIDTH ** -0.5, 0.125, ((0, 16), (1, 8))),
        "up_projection_bias": scatter_about(key_of[13], (FEED_HIDDEN,), 0.3, 3.0, ((0, 8),)),
        "down_projection_weight": scatter_about(key_of[14], (FEED_HIDDEN, MODEL_WIDTH), FEED_HIDDEN ** -0.5, 0.0625, ((0, 8), (1, 16))),
        "down_projection_bias": scatter_about(key_of[15], (MODEL_WIDTH,), 0.3, 3.0),
        "sequence_adapter": picks_of(key_of[16], SEQS, ADAPTER_COUNT, 1, 0),
        "query_adapter_input": scatter_about(key_of[17], (ADAPTER_COUNT, MODEL_WIDTH, ADAPTER_RANK), MODEL_WIDTH ** -0.5, 0.125),
        "query_adapter_output": scatter_about(key_of[18], (ADAPTER_COUNT, ADAPTER_RANK, MODEL_WIDTH), (4 * ADAPTER_RANK) ** -0.5, 0.75, ((2, 8),)),
        "keyvalue_adapter_input": scatter_about(key_of[19], (ADAPTER_COUNT, MODEL_WIDTH, ADAPTER_RANK), MODEL_WIDTH ** -0.5, 0.125),
        "keyvalue_adapter_output": scatter_about(key_of[20], (ADAPTER_COUNT, ADAPTER_RANK, 2 * HEAD_WIDTH), (4 * ADAPTER_RANK) ** -0.5, 0.75),
        "output_adapter_input": scatter_about(key_of[21], (ADAPTER_COUNT, MODEL_WIDTH, ADAPTER_RANK), (MODEL_WIDTH // 16) ** -0.5, 0.5, ((1, 8),)),
        "output_adapter_output": scatter_about(key_of[22], (ADAPTER_COUNT, ADAPTER_RANK, MODEL_WIDTH), (4 * ADAPTER_RANK) ** -0.5, 0.75),
        "up_adapter_input": scatter_about(key_of[23], (ADAPTER_COUNT, MODEL_WIDTH, ADAPTER_RANK), MODEL_WIDTH ** -0.5, 0.125),
        "up_adapter_output": scatter_about(key_of[24], (ADAPTER_COUNT, ADAPTER_RANK, FEED_HIDDEN), (4 * ADAPTER_RANK) ** -0.5, 0.75, ((2, 8),)),
        "down_adapter_input": scatter_about(key_of[25], (ADAPTER_COUNT, FEED_HIDDEN, ADAPTER_RANK), FEED_HIDDEN ** -0.5, 0.0625, ((1, 8),)),
        "down_adapter_output": scatter_about(key_of[26], (ADAPTER_COUNT, ADAPTER_RANK, MODEL_WIDTH), (4 * ADAPTER_RANK) ** -0.5, 0.75),
    }


@jax.custom_vjp
def lowrank_update(v):
    return lax.optimization_barrier(v.astype(jnp.bfloat16)).astype(jnp.float32)

@jax.custom_vjp
def lowrank_backward(v):
    return v

def low_keep(v):
    return (lowrank_update(v), None)

def low_pass(kept, grad):
    return (grad,)

def back_keep(v):
    return (v, None)

def back_low(kept, grad):
    return (lowrank_update(grad),)
lowrank_update.defvjp(low_keep, low_pass)
lowrank_backward.defvjp(back_keep, back_low)

def precise_product(left, right):
    return jnp.dot(left, right, precision=lax.Precision.HIGHEST)

def layer_norm(values, gain, shift):
    mean_value = lax.optimization_barrier(jnp.mean(values, axis=-1, keepdims=True))
    centred = values - mean_value
    variance = lax.optimization_barrier(jnp.mean(centred * centred, axis=-1, keepdims=True))
    return centred * lax.rsqrt(variance + 1e-05) * gain + shift

def gelu_tanh(values):
    inner_product = math.sqrt(2.0 / math.pi) * (values + 0.044715 * values * values * values)
    return 0.5 * values * (1.0 + jnp.tanh(inner_product))

def select_adapter(adapter_stack, adapter_position):
    return lax.dynamic_index_in_dim(adapter_stack, adapter_position, 0, keepdims=False)

def adapted_output(input_rows, weight_matrix, bias_vector, adapter_input_side, adapter_output_side):
    inner_product = lowrank_update(lowrank_backward(precise_product(input_rows, adapter_input_side)))
    return precise_product(input_rows, weight_matrix) + bias_vector + precise_product(inner_product, adapter_output_side)

def attend(query, keyval):
    keys = keyval[:, :HEAD_WIDTH]
    values = keyval[:, HEAD_WIDTH:]
    count = LEN // QROWS
    blocks = query.reshape(count, QROWS, H, HEAD_WIDTH)
    starts = jnp.arange(count, dtype=jnp.int32) * QROWS
    key_block = jnp.arange(LEN, dtype=jnp.int32) // BLOCK

    def one_block(element_item):
        rows_query, start = element_item
        scores = lowrank_backward(jnp.einsum('qhd,kd->qhk', rows_query, keys, precision=lax.Precision.HIGHEST) * HEAD_WIDTH ** (-0.5))
        query_block = (start + jnp.arange(QROWS, dtype=jnp.int32)) // BLOCK
        allowed = key_block[None, None, :] <= query_block[:, None, None]
        scores = jnp.where(allowed, scores, -1e+30)
        top = lax.optimization_barrier(jnp.max(scores, axis=-1, keepdims=True))
        expo = jnp.exp(scores - top)
        probs = lowrank_update(expo / lax.optimization_barrier(jnp.sum(expo, axis=-1, keepdims=True)))
        return jnp.einsum('qhk,kd->qhd', probs, values, precision=lax.Precision.HIGHEST)
    return lax.map(jax.checkpoint(one_block), (blocks, starts)).reshape(LEN, H * HEAD_WIDTH)

def sequence_layer(input_rows, adapter_position, frozen_weights, adapter_table):
    gain_one, shift_one, w_query, b_query, w_keyval, b_keyval, w_output, b_output, gain_two, shift_two, w_up, b_up, w_down, b_down = frozen_weights
    picked = [select_adapter(adapter_stack, adapter_position) for adapter_stack in adapter_table]
    normed = lowrank_update(layer_norm(input_rows, gain_one, shift_one))
    query = lowrank_update(lowrank_backward(adapted_output(normed, w_query, b_query, picked[0], picked[1])))
    keyval = lowrank_update(lowrank_backward(adapted_output(normed, w_keyval, b_keyval, picked[2], picked[3])))
    attended = lowrank_update(lowrank_backward(attend(query.reshape(LEN, H, HEAD_WIDTH), keyval)))
    middle = input_rows + lowrank_backward(adapted_output(attended, w_output, b_output, picked[4], picked[5]))
    normed_two = lowrank_update(layer_norm(middle, gain_two, shift_two))
    pre = lowrank_backward(adapted_output(normed_two, w_up, b_up, picked[6], picked[7]))
    act = lowrank_update(gelu_tanh(pre))
    return middle + lowrank_backward(adapted_output(act, w_down, b_down, picked[8], picked[9]))

def convert_float(value):
    return value.astype(jnp.float32)

def reference(tokens, cotangent, attention_norm_scale, attention_norm_bias, query_projection, query_projection_bias, keyvalue_projection, value_projection_bias, attention_output_weight, attention_output_bias, feedforward_norm_scale, feedforward_norm_bias, up_projection_weight, up_projection_bias, down_projection_weight, down_projection_bias, sequence_adapter, query_adapter_input, query_adapter_output, keyvalue_adapter_input, keyvalue_adapter_output, output_adapter_input, output_adapter_output, up_adapter_input, up_adapter_output, down_adapter_input, down_adapter_output):
    keyval_bias = jnp.concatenate([jnp.zeros((HEAD_WIDTH,), jnp.float32), convert_float(value_projection_bias)])
    frozen_weights = (convert_float(attention_norm_scale), convert_float(attention_norm_bias), convert_float(query_projection), convert_float(query_projection_bias), convert_float(keyvalue_projection), keyval_bias, convert_float(attention_output_weight), convert_float(attention_output_bias), convert_float(feedforward_norm_scale), convert_float(feedforward_norm_bias), convert_float(up_projection_weight), convert_float(up_projection_bias), convert_float(down_projection_weight), convert_float(down_projection_bias))
    adapter_table = tuple((convert_float(adapter_stack) for adapter_stack in (query_adapter_input, query_adapter_output, keyvalue_adapter_input, keyvalue_adapter_output, output_adapter_input, output_adapter_output, up_adapter_input, up_adapter_output, down_adapter_input, down_adapter_output)))
    seq_index = sequence_adapter[:, 0].astype(jnp.int32)

    def forward_pass(input_rows, adapter_pair):

        def step(loop_carry, element_item):
            return (loop_carry, sequence_layer(element_item[0], element_item[1], frozen_weights, adapter_pair))
        _, result = lax.scan(step, jnp.float32(0.0), (input_rows.reshape(SEQS, LEN, MODEL_WIDTH), seq_index))
        return result.reshape(TOKENS, MODEL_WIDTH)
    layer_output, backward_function = jax.vjp(forward_pass, convert_float(tokens), adapter_table)
    input_gradient, adapter_gradient = backward_function(convert_float(cotangent))
    return (layer_output.astype(jnp.bfloat16), input_gradient.astype(jnp.bfloat16), adapter_gradient[0], adapter_gradient[1], adapter_gradient[2], adapter_gradient[3], adapter_gradient[4], adapter_gradient[5], adapter_gradient[6], adapter_gradient[7], adapter_gradient[8], adapter_gradient[9])
```

```python
import math

import jax
import jax.numpy as jnp
from jax import lax
from jax.sharding import Mesh
from jax.sharding import PartitionSpec as P

MODEL_WIDTH = 2048
H = 16
HEAD_WIDTH = 128
FEED_HIDDEN = 8192
ADAPTER_RANK = 16
ADAPTER_COUNT = 8
BLOCK = 256

AXES = ("y", "zl", "core", "zh", "x")
SIZES = (4, 2, 2, 2, 4)
DP = ("y", "zl", "core")
MP = ("zh", "x")
PLACES = (0, 3, 1, 2)
Z_RING = (0, 2, 1, 3)
ROWS = 128
RIDE = 128

f32 = jnp.float32
bf16 = jnp.bfloat16


def ring_x(a, step):
    return lax.ppermute(a, "x", [(i, (i + step) % 4) for i in range(4)])


def ring_y(a, step):
    return lax.ppermute(a, "y", [(i, (i + step) % 4) for i in range(4)])


def ring_z(a, step):
    return lax.ppermute(a, ("zl", "zh"), [(Z_RING[i], Z_RING[(i + step) % 4]) for i in range(4)])


def other_core(a):
    return lax.ppermute(a, "core", [(0, 1), (1, 0)])


def other_half(a):
    return lax.ppermute(a, "zh", [(0, 1), (1, 0)])


def turn(a):
    return lax.ppermute(a, ("core", "zh"), [(0, 0), (1, 2), (2, 1), (3, 3)])


def gather_row(a):
    half = a.shape[0] // 2
    left, right = ring_x(a, 1), ring_x(a, -1)
    near = other_core(a)
    far = jnp.concatenate([ring_x(left[:half], 1), ring_x(right[half:], -1)], axis=0)
    sides = other_core(jnp.concatenate([left, right], axis=0))
    far_other = other_core(far)
    n = a.shape[0]
    return jnp.stack(
        [
            jnp.stack([a, near]),
            jnp.stack([left, sides[:n]]),
            jnp.stack([right, sides[n:]]),
            jnp.stack([far, far_other]),
        ]
    )


def scatter_row(parts):
    parts = parts.astype(bf16)
    mine, theirs = parts[:, 0], parts[:, 1]
    half = parts.shape[2] // 2
    far = (mine[3].astype(f32) + other_core(theirs[3]).astype(f32)).astype(bf16)
    up, down = ring_x(far[:half], 1), ring_x(far[half:], -1)
    rest = mine[:3].astype(f32) + other_core(theirs[:3]).astype(f32)
    to_right = jnp.concatenate([rest[2, :half] + up.astype(f32), rest[2, half:]]).astype(bf16)
    to_left = jnp.concatenate([rest[1, :half], rest[1, half:] + down.astype(f32)]).astype(bf16)
    return rest[0] + ring_x(to_right, 1).astype(f32) + ring_x(to_left, -1).astype(f32)


def rolled(blocks, me):
    both = jnp.concatenate([blocks, blocks], axis=0)
    return lax.dynamic_slice_in_dim(both, lax.rem(4 - me, 4), 4, 0)


def gather_ring(a, ring, me):
    half = a.shape[-2] // 2
    left, right = ring(a, 1), ring(a, -1)
    far = jnp.concatenate(
        [ring(left[..., :half, :], 1), ring(right[..., half:, :], -1)], axis=-2
    )
    return rolled(jnp.stack([a, right, far, left]), me)


def gather_plane(a, y, z):
    half = a.shape[0] // 2
    first = gather_ring(gather_ring(a[:half], ring_y, y), ring_z, z)
    second = gather_ring(gather_ring(a[half:], ring_z, z), ring_y, y)
    return jnp.concatenate([jnp.moveaxis(first, 0, 1), second], axis=2)


def layer_norm(values, gain, shift):
    mean_value = jnp.mean(values, axis=-1, keepdims=True)
    centred = values - mean_value
    variance = jnp.mean(centred * centred, axis=-1, keepdims=True)
    return centred * lax.rsqrt(variance + 1e-05) * gain + shift


def gelu_tanh(values):
    inner_product = math.sqrt(2.0 / math.pi) * (values + 0.044715 * values * values * values)
    return 0.5 * values * (1.0 + jnp.tanh(inner_product))


def pick(adapter_stack, position):
    return lax.dynamic_index_in_dim(adapter_stack, position, 0, keepdims=False)


def dot(left, right):
    return jnp.dot(left, right, preferred_element_type=f32)


def dot_t(left, right):
    return lax.dot_general(left, right, (((1,), (1,)), ((), ())), preferred_element_type=f32)


def tdot(left, right):
    return lax.dot_general(left, right, (((0,), (0,)), ((), ())), preferred_element_type=f32)


def shards(
    tokens,
    cotangent,
    attention_norm_scale,
    attention_norm_bias,
    query_projection,
    query_projection_bias,
    keyvalue_projection,
    value_projection_bias,
    attention_output_weight,
    attention_output_bias,
    feedforward_norm_scale,
    feedforward_norm_bias,
    up_projection_weight,
    up_projection_bias,
    down_projection_weight,
    down_projection_bias,
    sequence_adapter,
    query_adapter_input,
    query_adapter_output,
    keyvalue_adapter_input,
    keyvalue_adapter_output,
    output_adapter_input,
    output_adapter_output,
    up_adapter_input,
    up_adapter_output,
    down_adapter_input,
    down_adapter_output,
):
    y, core, zl, zh, x = (lax.axis_index(n) for n in ("y", "core", "zl", "zh", "x"))
    z = zh * 2 + zl
    scale = HEAD_WIDTH ** (-0.5)
    local = (ROWS, MODEL_WIDTH)
    gain_one, shift_one = attention_norm_scale.astype(f32), attention_norm_bias.astype(f32)
    gain_two, shift_two = feedforward_norm_scale.astype(f32), feedforward_norm_bias.astype(f32)

    mine = sequence_adapter[0, 0]
    theirs = other_core(sequence_adapter)[0, 0]
    picks = (mine, theirs)
    low = jnp.where(core == 0, mine, theirs)
    high = jnp.where(core == 0, theirs, mine)

    def ordered(stack):
        return jnp.concatenate([pick(stack, low), pick(stack, high)], axis=0)

    small = jnp.concatenate(
        [
            ordered(query_adapter_output),
            ordered(jnp.swapaxes(output_adapter_input, 1, 2)),
            ordered(up_adapter_output),
            ordered(jnp.swapaxes(down_adapter_input, 1, 2)),
        ],
        axis=1,
    )
    biases = jnp.concatenate(
        [
            query_projection_bias,
            jnp.zeros((256,), bf16),
            up_projection_bias,
            jnp.zeros((1024,), bf16),
        ]
    )
    small = turn(
        jnp.concatenate([small, biases[None], jnp.zeros((15, 2560), bf16)], axis=0)
    )
    by_core = small[:32].reshape(2, ADAPTER_RANK, 2560)
    by_core = jnp.where(core == 0, by_core, by_core[::-1])
    q_out, o_in, u_out, d_in = (
        by_core[:, :, :256],
        by_core[:, :, 256:512],
        by_core[:, :, 512:1536],
        by_core[:, :, 1536:],
    )
    q_bias, u_bias = small[32, :256].astype(f32), small[32, 512:1536].astype(f32)

    def both(stack):
        return jnp.stack([pick(stack, p) for p in picks])

    attention_shard = turn(
        jnp.concatenate(
            [query_projection, keyvalue_projection, attention_output_weight.T], axis=1
        )
    )
    plane = gather_plane(attention_shard, y, z)
    plane = plane.reshape(4, 2, 2, ROWS, 768)
    plane = jnp.swapaxes(plane, 1, 2).reshape(MODEL_WIDTH, 768)
    w_query, w_keyval, w_output = plane[:, :256], plane[:, 256:512], plane[:, 512:]

    feed_shard = jnp.concatenate([up_projection_weight, down_projection_weight.T], axis=1)
    feed = lax.all_gather(feed_shard, DP + ("zh",), axis=0, tiled=True)
    feed = feed.reshape(16, 2, ROWS, 2048)
    feed = lax.dynamic_index_in_dim(feed, core, 1, keepdims=False).reshape(MODEL_WIDTH, 2048)
    w_up, w_down = feed[:, :1024], feed[:, 1024:]

    cot_all = lax.all_gather(cotangent, ("core", "x"), axis=0, tiled=True)
    cot_all = cot_all.reshape(2, 4, *local)
    cot_all = jnp.where(core == 0, cot_all, cot_all[::-1])
    cot_all = rolled(jnp.swapaxes(cot_all, 0, 1), lax.rem(4 - x, 4))
    cot_all = jnp.stack([cot_all[p] for p in PLACES])

    input_rows = tokens.astype(f32)
    normed = layer_norm(input_rows, gain_one, shift_one).astype(bf16)
    normed_all = gather_row(normed)

    kv_in, kv_out = pick(keyvalue_adapter_input, mine), pick(keyvalue_adapter_output, mine)
    keyval_inner = dot(normed, kv_in).astype(bf16)
    keyval_bias = jnp.concatenate(
        [jnp.zeros((HEAD_WIDTH,), f32), value_projection_bias.astype(f32)]
    )
    keyval = (dot(normed, w_keyval) + keyval_bias + dot(keyval_inner, kv_out)).astype(bf16)
    keyval_all = gather_row(jnp.concatenate([keyval, other_half(keyval)], axis=1))
    keyval_all = keyval_all.reshape(4, 2, ROWS, 2, 256).transpose(1, 3, 0, 2, 4)
    keyval_all = keyval_all.reshape(2, 1024, 256)
    keys, values = keyval_all[..., :HEAD_WIDTH], keyval_all[..., HEAD_WIDTH:]

    def per_sequence(a):
        return jnp.swapaxes(a, 0, 1).reshape(2, 4 * ROWS, a.shape[-1])

    def per_place(a):
        return jnp.swapaxes(a.reshape(2, 4, ROWS, a.shape[-1]), 0, 1)

    def low_in(a, sides):
        return jnp.einsum("stw,swr->str", a, sides, preferred_element_type=f32)

    def low_in_t(a, sides):
        return jnp.einsum("stw,srw->str", a, sides, preferred_element_type=f32)

    normed_seq = per_sequence(normed_all)
    query_inner = low_in(normed_seq, both(query_adapter_input)).astype(bf16)
    query = (
        jnp.einsum("stw,wn->stn", normed_seq, w_query, preferred_element_type=f32)
        + q_bias
        + jnp.einsum("str,srn->stn", query_inner, q_out, preferred_element_type=f32)
    ).astype(bf16)

    place_x = jnp.stack([lax.rem(x + p, 4) for p in PLACES])
    own_block = jnp.repeat(place_x // 2, ROWS)
    allowed = jnp.concatenate(
        [
            own_block[None, :] <= own_block[:, None],
            jnp.broadcast_to(zh == 1, (4 * ROWS, 4 * ROWS)),
        ],
        axis=1,
    )
    heads = query.reshape(2, 4 * ROWS, 2, HEAD_WIDTH)

    def scores_of():
        raw = jnp.einsum("sqhd,skd->shqk", heads, keys, preferred_element_type=f32) * scale
        return jnp.where(allowed, raw, -1e30)

    scores = scores_of()
    top = jnp.max(scores, axis=-1, keepdims=True)
    expo = jnp.exp(scores - top)
    total = jnp.sum(expo, axis=-1, keepdims=True)
    probs_low = (expo / total).astype(bf16)
    log_total = top + jnp.log(total)
    attended = jnp.einsum("shqk,skd->sqhd", probs_low, values, preferred_element_type=f32)
    attended = attended.reshape(2, 4 * ROWS, 256).astype(bf16)

    def ride(main, *extra):
        width = sum(e.shape[-1] for e in extra)
        pad = jnp.zeros((*main.shape[:-1], -width % RIDE), f32)
        return per_place(jnp.concatenate([main, *extra, pad], axis=-1))

    out_part = ride(
        jnp.einsum("stw,nw->stn", attended, w_output, preferred_element_type=f32),
        low_in_t(attended, o_in),
    )
    out_sum = scatter_row(out_part)
    output_inner = out_sum[:, 2048:2064].astype(bf16)
    middle = (
        input_rows
        + out_sum[:, :2048]
        + attention_output_bias.astype(f32)
        + dot(output_inner, pick(output_adapter_output, mine))
    )
    normed_two = layer_norm(middle, gain_two, shift_two).astype(bf16)
    normed_two_seq = per_sequence(gather_row(normed_two))
    up_inner = low_in(normed_two_seq, both(up_adapter_input)).astype(bf16)
    pre = (
        jnp.einsum("stw,wn->stn", normed_two_seq, w_up, preferred_element_type=f32)
        + u_bias
        + jnp.einsum("str,srn->stn", up_inner, u_out, preferred_element_type=f32)
    )
    act = gelu_tanh(pre).astype(bf16)
    down_sum = scatter_row(
        ride(
            jnp.einsum("stw,nw->stn", act, w_down, preferred_element_type=f32),
            low_in_t(act, d_in),
        )
    )
    down_inner = down_sum[:, 2048:2064].astype(bf16)
    layer_output = (
        middle
        + down_sum[:, :2048]
        + down_projection_bias.astype(f32)
        + dot(down_inner, pick(down_adapter_output, mine))
    ).astype(bf16)

    cot_seq = per_sequence(cot_all)
    grad_down_b = tdot(down_inner, cotangent)
    down_back = low_in_t(cot_seq, both(down_adapter_output)).astype(bf16)
    grad_down_a = jnp.einsum("stw,str->srw", act, down_back, preferred_element_type=f32)
    grad_act = jnp.einsum(
        "stn,nw->stw", cot_seq, w_down, preferred_element_type=f32
    ) + jnp.einsum("str,srw->stw", down_back, d_in, preferred_element_type=f32)
    _, gelu_back = jax.vjp(gelu_tanh, pre)
    grad_pre = gelu_back(grad_act)[0].astype(bf16)
    grad_up_b = jnp.einsum("str,stw->srw", up_inner, grad_pre, preferred_element_type=f32)
    up_sum = scatter_row(
        ride(
            jnp.einsum("stw,nw->stn", grad_pre, w_up, preferred_element_type=f32),
            low_in_t(grad_pre, u_out),
        )
    )
    up_back = up_sum[:, 2048:2064].astype(bf16)
    grad_up_a = tdot(up_back, normed_two)
    grad_normed_two = up_sum[:, :2048] + dot_t(up_back, pick(up_adapter_input, mine))
    _, norm_two_back = jax.vjp(lambda v: layer_norm(v, gain_two, shift_two), middle)
    grad_middle = cotangent.astype(f32) + norm_two_back(grad_normed_two)[0]
    grad_branch = grad_middle.astype(bf16)

    branch_seq = per_sequence(gather_row(grad_branch))
    grad_output_b = tdot(output_inner, grad_branch)
    output_back = low_in_t(branch_seq, both(output_adapter_output)).astype(bf16)
    grad_output_a = jnp.einsum("stw,str->srw", attended, output_back, preferred_element_type=f32)
    grad_attended = (
        jnp.einsum("stn,nw->stw", branch_seq, w_output, preferred_element_type=f32)
        + jnp.einsum("str,srw->stw", output_back, o_in, preferred_element_type=f32)
    ).astype(bf16)
    grad_heads = grad_attended.reshape(2, 4 * ROWS, 2, HEAD_WIDTH)
    probs = jnp.exp(scores_of() - log_total)
    grad_probs = jnp.einsum("sqhd,skd->shqk", grad_heads, values, preferred_element_type=f32)
    grad_scores = (
        probs * (grad_probs - jnp.sum(probs * grad_probs, axis=-1, keepdims=True))
    ).astype(bf16)
    grad_query = (
        jnp.einsum("shqk,skd->sqhd", grad_scores, keys, preferred_element_type=f32) * scale
    )
    grad_query = grad_query.reshape(2, 4 * ROWS, 256).astype(bf16)
    grad_keys = jnp.einsum("shqk,sqhd->skd", grad_scores, heads, preferred_element_type=f32) * scale
    grad_values = jnp.einsum(
        "shqk,sqhd->skd", probs.astype(bf16), grad_heads, preferred_element_type=f32
    )
    grad_query_b = jnp.einsum("str,stw->srw", query_inner, grad_query, preferred_element_type=f32)
    grad_kv = jnp.concatenate([grad_keys, grad_values], axis=-1).reshape(2, 2, 4 * ROWS, 256)
    query_sum = scatter_row(
        ride(
            jnp.einsum("stw,nw->stn", grad_query, w_query, preferred_element_type=f32),
            grad_kv[:, 0],
            grad_kv[:, 1],
            low_in_t(grad_query, q_out),
        )
    )
    grad_keyval = (
        query_sum[:, 2048:2304] + other_half(query_sum[:, 2304:2560].astype(bf16)).astype(f32)
    ).astype(bf16)
    query_back = query_sum[:, 2560:2576].astype(bf16)
    grad_query_a = tdot(query_back, normed)
    grad_keyval_b = tdot(keyval_inner, grad_keyval)
    keyval_back = dot_t(grad_keyval, kv_out).astype(bf16)
    grad_keyval_a = tdot(keyval_back, normed)
    grad_normed = (
        query_sum[:, :2048]
        + dot_t(query_back, pick(query_adapter_input, mine))
        + dot_t(grad_keyval, w_keyval)
        + dot_t(keyval_back, kv_in)
    )
    _, norm_one_back = jax.vjp(lambda v: layer_norm(v, gain_one, shift_one), input_rows)
    grad_tokens = (grad_middle + norm_one_back(grad_normed)[0]).astype(bf16)

    ids = jnp.arange(ADAPTER_COUNT, dtype=jnp.int32)
    hot_mine = (ids == mine).astype(f32)[:, None, None]
    hot_theirs = (ids == theirs).astype(f32)[:, None, None]

    def whole(piece):
        return (hot_mine * piece[None]).astype(bf16)

    def placed(pair, width):
        stacked = (hot_mine * pair[0][None] + hot_theirs * pair[1][None]).astype(bf16)
        here = (core * 4 + x) * pair.shape[-1]
        return lax.dynamic_update_slice_in_dim(
            jnp.zeros((ADAPTER_COUNT, ADAPTER_RANK, width), bf16), stacked, here, 2
        )

    feed_grads = jnp.concatenate(
        [
            whole(grad_up_a),
            placed(grad_up_b, FEED_HIDDEN),
            placed(grad_down_a, FEED_HIDDEN),
            whole(grad_down_b),
        ],
        axis=2,
    )
    feed_grads = lax.psum(feed_grads, AXES).astype(f32)
    up_a, up_b, down_a, down_b = jnp.split(feed_grads, (2048, 10240, 18432), axis=2)
    rest_grads = jnp.concatenate(
        [
            whole(grad_query_a),
            placed(grad_query_b, MODEL_WIDTH),
            whole(grad_keyval_a),
            whole(grad_keyval_b),
            placed(grad_output_a, MODEL_WIDTH),
            whole(grad_output_b),
        ],
        axis=2,
    )
    rest_grads = lax.psum(rest_grads, AXES).astype(f32)
    query_a, query_b, keyval_a, keyval_b, output_a, output_b = jnp.split(
        rest_grads, (2048, 4096, 6144, 6400, 8448), axis=2
    )

    def side_in(a):
        return jnp.swapaxes(a, 1, 2)

    return (
        layer_output,
        grad_tokens,
        side_in(query_a),
        query_b,
        side_in(keyval_a),
        keyval_b,
        side_in(output_a),
        output_b,
        side_in(up_a),
        up_b,
        side_in(down_a),
        down_b,
    )


def solution(mesh):
    fine = Mesh(mesh.devices.reshape(SIZES), AXES)
    in_specs = (
        P(AXES, None),
        P(AXES, None),
        P(),
        P(),
        P(DP, MP),
        P(MP),
        P(DP, None),
        P(),
        P(MP, DP),
        P(),
        P(),
        P(),
        P(DP, MP),
        P(MP),
        P(MP, DP),
        P(),
        P(DP, None),
        P(),
        P(None, None, MP),
        P(),
        P(),
        P(None, MP, None),
        P(),
        P(),
        P(None, None, MP),
        P(None, MP, None),
        P(),
    )
    out_specs = (P(AXES, None), P(AXES, None)) + (P(),) * 10
    return jax.shard_map(shards, mesh=fine, in_specs=in_specs, out_specs=out_specs, check_vma=False)
```

```python
import functools
import math

import jax
import jax.numpy as jnp
from jax import lax
from jax.experimental import pallas as pl
from jax.experimental.pallas import tpu as pltpu
from jax.sharding import Mesh
from jax.sharding import PartitionSpec as P

MODEL_WIDTH = 2048
H = 16
HEAD_WIDTH = 128
FEED_HIDDEN = 8192
ADAPTER_RANK = 16
ADAPTER_COUNT = 8
BLOCK = 256

AXES = ("y", "zl", "core", "zh", "x")
SIZES = (4, 2, 2, 2, 4)
DP = ("y", "zl", "core")
MP = ("zh", "x")
PLACES = (0, 3, 1, 2)
Z_RING = (0, 2, 1, 3)
ROWS = 128
RIDE = 128

f32 = jnp.float32
bf16 = jnp.bfloat16


def ring_x(a, step):
    return lax.ppermute(a, "x", [(i, (i + step) % 4) for i in range(4)])


def ring_y(a, step):
    return lax.ppermute(a, "y", [(i, (i + step) % 4) for i in range(4)])


def ring_z(a, step):
    return lax.ppermute(a, ("zl", "zh"), [(Z_RING[i], Z_RING[(i + step) % 4]) for i in range(4)])


def other_core(a):
    return lax.ppermute(a, "core", [(0, 1), (1, 0)])


def other_half(a):
    return lax.ppermute(a, "zh", [(0, 1), (1, 0)])


def turn(a):
    return lax.ppermute(a, ("core", "zh"), [(0, 0), (1, 2), (2, 1), (3, 3)])


def gather_row(a):
    half = a.shape[0] // 2
    left, right = ring_x(a, 1), ring_x(a, -1)
    near = other_core(a)
    top, bottom = ring_x(left[:half], 1), ring_x(right[half:], -1)
    left_other, right_other = other_core(left), other_core(right)
    return (
        (a, near),
        (left, left_other),
        (right, right_other),
        (top, bottom, other_core(top), other_core(bottom)),
    )


def scatter_row(mine, theirs):
    half = mine[0].shape[0] // 2
    far = mine[3].astype(f32) + other_core(theirs[3]).astype(f32)
    up = ring_x(far[:half].astype(bf16), 1)
    down = ring_x(far[half:].astype(bf16), -1)
    right = mine[2].astype(f32) + other_core(theirs[2]).astype(f32)
    left = mine[1].astype(f32) + other_core(theirs[1]).astype(f32)
    near = mine[0].astype(f32) + other_core(theirs[0]).astype(f32)
    right = jnp.concatenate([right[:half] + up.astype(f32), right[half:]]).astype(bf16)
    left = jnp.concatenate([left[:half], left[half:] + down.astype(f32)]).astype(bf16)
    return near + ring_x(right, 1).astype(f32) + ring_x(left, -1).astype(f32)


def gather_ring(a, ring):
    half = a.shape[-2] // 2
    left, right = ring(a, 1), ring(a, -1)
    return a, left, right, ring(left[..., :half, :], 1), ring(right[..., half:, :], -1)


def stacked_ring(pieces):
    own, left, right, top, bottom = pieces
    return jnp.stack([own, right, jnp.concatenate([top, bottom], axis=-2), left])


def rolled(blocks, me):
    both = jnp.concatenate([blocks, blocks], axis=0)
    return lax.dynamic_slice_in_dim(both, lax.rem(4 - me, 4), 4, 0)


def own_slice(pair, zh):
    kept = jnp.where(zh == 0, pair[:16], pair[16:])
    sent = jnp.where(zh == 0, pair[16:], pair[:16])
    total = kept + other_half(sent.astype(bf16)).astype(f32)
    return turn(total.astype(bf16))


def scatter_sequence(slices, zh, x):
    kept = lax.dynamic_index_in_dim(slices, zh, 0, keepdims=False)
    sent = lax.dynamic_index_in_dim(slices, 1 - zh, 0, keepdims=False)
    total = kept + other_half(sent.astype(bf16)).astype(f32)
    both = jnp.concatenate([total, total], axis=0)
    near = lax.dynamic_slice_in_dim(both, x, 4, 0)
    low = near.astype(bf16)
    return (
        near[0]
        + ring_x(low[1], 1).astype(f32)
        + ring_x(low[3], -1).astype(f32)
        + ring_x(low[2], 2).astype(f32)
    )


def gather_sequences(piece, zh, x):
    other = other_half(piece)
    pair = jnp.where(zh == 0, jnp.stack([piece, other]), jnp.stack([other, piece]))
    row = rolled(jnp.stack([pair, ring_x(pair, -1), ring_x(pair, 2), ring_x(pair, 1)]), x)
    return lax.all_gather(row, DP, axis=0)


def layer_norm(values, gain, shift):
    mean_value = jnp.mean(values, axis=-1, keepdims=True)
    centred = values - mean_value
    variance = jnp.mean(centred * centred, axis=-1, keepdims=True)
    return centred * lax.rsqrt(variance + 1e-05) * gain + shift


def gelu_tanh(values):
    inner_product = math.sqrt(2.0 / math.pi) * (values + 0.044715 * values * values * values)
    return 0.5 * values * (1.0 + jnp.tanh(inner_product))


def pick(adapter_stack, position):
    return lax.dynamic_index_in_dim(adapter_stack, position, 0, keepdims=False)


def dot(left, right):
    return jnp.dot(left, right, preferred_element_type=f32)


def dot_t(left, right):
    return lax.dot_general(left, right, (((1,), (1,)), ((), ())), preferred_element_type=f32)


def tdot(left, right):
    return lax.dot_general(left, right, (((0,), (0,)), ((), ())), preferred_element_type=f32)


def lane_owner(rows, row_core):
    lane = lax.broadcasted_iota(jnp.int32, (rows, RIDE), 1)
    return (lane // ADAPTER_RANK) == row_core


def place_mask(core):
    row = lax.broadcasted_iota(jnp.int32, (2 * ROWS, RIDE), 0)
    return lane_owner(2 * ROWS, jnp.where(row < ROWS, core, 1 - core))


def copy(source, target, sem):
    pltpu.make_async_copy(source, target, sem).start()


def wait(target, sem):
    pltpu.make_async_copy(target, target, sem).wait()


def copy_place(pieces, target_mine, target_theirs, sem):
    half = ROWS // 2
    if len(pieces) == 2:
        copy(pieces[0], target_mine, sem)
        copy(pieces[1], target_theirs, sem)
    else:
        copy(pieces[0], target_mine.at[pl.ds(0, half)], sem)
        copy(pieces[1], target_mine.at[pl.ds(half, half)], sem)
        copy(pieces[2], target_theirs.at[pl.ds(0, half)], sem)
        copy(pieces[3], target_theirs.at[pl.ds(half, half)], sem)


def split_pieces(refs):
    return (refs[0:2], refs[2:4], refs[4:6], refs[6:10])


def assemble_kernel(at, *refs):
    pieces, (out, sem) = refs[:10], refs[10:]
    y, z = at[3], at[4]
    half = ROWS // 2
    for which in range(2):
        group = pieces[5 * which : 5 * which + 5]
        for piece, step, first, count in (
            (group[0], 0, 0, half),
            (group[1], 3, 0, half),
            (group[2], 1, 0, half),
            (group[3], 2, 0, half // 2),
            (group[4], 2, half // 2, half // 2),
        ):
            for k in range(4):
                if which == 0:
                    to_y, to_z = lax.rem(y + k, 4), lax.rem(z + step, 4)
                else:
                    to_y, to_z = lax.rem(y + step, 4), lax.rem(z + k, 4)
                shard = (to_y * 2 + lax.rem(to_z, 2)) * 2 + to_z // 2
                row = pl.multiple_of(shard * ROWS + which * half + first, 32)
                copy(piece.at[k], out.at[pl.ds(row, count)], sem)
    wait(out, sem)


def pack_kernel(at, query, keyval, output, up, down, attention_out, feed_out):
    attention_out[:, :256] = query[...]
    attention_out[:, 256:512] = keyval[...]
    attention_out[:, 512:] = output[...].astype(f32).T.astype(bf16)
    feed_out[:, :1024] = up[...]
    feed_out[:, 1024:] = down[...].astype(f32).T.astype(bf16)


def finish_kernel(widths, ids, gathered, *outs):
    first = 0
    for out, width in zip(outs, widths):
        out[...] = jnp.zeros_like(out)
        for s in range(16):
            out[ids[s]] += gathered[s, 0, 0, :, first : first + width].astype(f32)
        first += width


def attention_kernel(at, *refs):
    rows_in = split_pieces(refs[:10])
    kv_in = refs[10:14]
    w, q_in, q_out, o_in, q_bias, bias = refs[14:20]
    inner_out, query_out, kv_all, lse_out, att_out = refs[20:25]
    parts = (refs[25:29], refs[29:33])
    rows, kvs, ws, sems = refs[33:]
    s = pl.program_id(0)
    core = at[0]

    @pl.when(s == 0)
    def _():
        copy(w, ws, sems.at[2])
        for p in range(4):
            here = pl.ds(p * ROWS, ROWS)
            copy_place(rows_in[p], rows.at[0, here], rows.at[1, here], sems.at[0])
            for q in range(2):
                for half in range(2):
                    copy(
                        kv_in[p].at[pl.ds(q * ROWS, ROWS), pl.ds(half * 256, 256)],
                        kvs.at[q, half * 4 + p],
                        sems.at[1],
                    )
        wait(rows, sems.at[0])
        wait(ws, sems.at[2])
        wait(kvs, sems.at[1])

    owner = lane_owner(4 * ROWS, jnp.where(s == 0, core, 1 - core))
    x = rows[s]
    inner = jnp.where(owner, dot_t(x, q_in[...]), 0.0).astype(bf16)
    inner_out[0] = inner
    query = (dot(x, ws[:, :256]) + q_bias[...] + dot(inner, q_out[...])).astype(bf16)
    query_out[0] = query
    kv = kvs[s]
    kv_all[0] = kv
    keys = kv[:, :, :HEAD_WIDTH].reshape(8 * ROWS, HEAD_WIDTH)
    values_t = kv[:, :, HEAD_WIDTH:].reshape(8 * ROWS, HEAD_WIDTH).astype(f32).T.astype(bf16)
    columns = []
    for h in range(2):
        chunks = []
        for c in range(2):
            lanes = slice(c * 256, c * 256 + 256)
            q = query[lanes, h * HEAD_WIDTH : (h + 1) * HEAD_WIDTH]
            scores = dot_t(keys, q) * (HEAD_WIDTH**-0.5)
            scores = scores.reshape(8, ROWS, 256) + bias[:, lanes][:, None, :]
            scores = scores.reshape(8 * ROWS, 256)
            top = jnp.max(scores, axis=0, keepdims=True)
            expo = jnp.exp(scores - top)
            total = jnp.sum(expo, axis=0, keepdims=True)
            probs = (expo * (1.0 / total)).astype(bf16)
            lse_out[0, h : h + 1, lanes] = top + jnp.log(total)
            chunks.append(dot(values_t, probs).T)
        columns.append(jnp.concatenate(chunks, axis=0))
    attended = jnp.concatenate(columns, axis=1).astype(bf16)
    att_out[0] = attended
    low = jnp.where(owner, dot_t(attended, o_in[...]), 0.0).astype(bf16)
    for which in range(2):

        @pl.when(s == which)
        def _(which=which):
            for p in range(4):
                here = slice(p * ROWS, (p + 1) * ROWS)
                parts[which][p][:, :MODEL_WIDTH] = dot_t(attended[here], ws[:, 512:]).astype(bf16)
                parts[which][p][:, MODEL_WIDTH:] = low[here]


def feed_kernel(at, *refs):
    rows_in = split_pieces(refs[:10])
    feed, u_in, u_out, d_in, u_bias = refs[10:15]
    inner_out, pre_out, act_out = refs[15:18]
    parts = (refs[18:22], refs[22:26])
    rows, up, down, sems = refs[26:]
    p = pl.program_id(0)
    core = at[0]

    @pl.when(p == 0)
    def _():
        copy(feed.at[:, core, :, pl.ds(0, 1024)], up, sems.at[4])
        for k in range(4):
            copy_place(
                rows_in[k], rows.at[k, pl.ds(0, ROWS)], rows.at[k, pl.ds(ROWS, ROWS)], sems.at[k]
            )
        copy(feed.at[:, core, :, pl.ds(1024, 1024)], down, sems.at[5])
        wait(up, sems.at[4])

    wait(rows.at[p], sems.at[p])
    mask = place_mask(core)
    x = rows[p]
    inner = jnp.where(mask, dot_t(x, u_in[...]), 0.0).astype(bf16)
    inner_out[0] = inner
    pre = dot(x, up[...].reshape(MODEL_WIDTH, 1024)) + u_bias[...] + dot(inner, u_out[...])
    pre_out[0] = pre
    act = gelu_tanh(pre).astype(bf16)
    act_out[0] = act

    @pl.when(p == 0)
    def _():
        wait(down, sems.at[5])

    low = jnp.where(mask, dot_t(act, d_in[...]), 0.0).astype(bf16)
    out = dot_t(act, down[...].reshape(MODEL_WIDTH, 1024)).astype(bf16)
    for k in range(4):

        @pl.when(p == k)
        def _(k=k):
            for which in range(2):
                here = slice(which * ROWS, (which + 1) * ROWS)
                parts[which][k][:, :MODEL_WIDTH] = out[here]
                parts[which][k][:, MODEL_WIDTH:] = low[here]


def feed_back_kernel(at, *refs):
    cot, feed, pre_in, act_in, inner_in, d_out, d_in, u_out = refs[:8]
    up_b, down_a = refs[8:10]
    parts = (refs[10:14], refs[14:18])
    rows, up, down, sems = refs[18:]
    p = pl.program_id(0)
    core, x = at[0], at[1]

    @pl.when(p == 0)
    def _():
        copy(feed.at[:, core, :, pl.ds(1024, 1024)], down, sems.at[5])
        for k in range(4):
            there = lax.rem(x + PLACES[k], 4)
            copy(cot.at[core, there], rows.at[k, pl.ds(0, ROWS)], sems.at[k])
            copy(cot.at[1 - core, there], rows.at[k, pl.ds(ROWS, ROWS)], sems.at[k])
        copy(feed.at[:, core, :, pl.ds(0, 1024)], up, sems.at[4])
        up_b[...] = jnp.zeros_like(up_b)
        down_a[...] = jnp.zeros_like(down_a)
        wait(down, sems.at[5])

    wait(rows.at[p], sems.at[p])
    mask = place_mask(core)
    grad = rows[p]
    back = jnp.where(mask, dot_t(grad, d_out[...]), 0.0)
    back_t = back.T[:32].astype(bf16)
    act = act_in[0]
    down_a[...] += dot(back_t, act)
    grad_act = dot(grad, down[...].reshape(MODEL_WIDTH, 1024)) + dot(back.astype(bf16), d_in[...])
    pre = pre_in[0]
    k0 = math.sqrt(2.0 / math.pi)
    square = pre * pre
    bend = jnp.tanh(k0 * (pre + 0.044715 * square * pre))
    slope = 0.5 * (1.0 + bend) + 0.5 * pre * (1.0 - bend * bend) * (
        k0 * (1.0 + 3.0 * 0.044715 * square)
    )
    grad_pre = (grad_act * slope).astype(bf16)
    inner_t = inner_in[0].astype(f32).T[:32].astype(bf16)
    up_b[...] += dot(inner_t, grad_pre)
    low = jnp.where(mask, dot_t(grad_pre, u_out[...]), 0.0).astype(bf16)

    @pl.when(p == 0)
    def _():
        wait(up, sems.at[4])

    out = dot_t(grad_pre, up[...].reshape(MODEL_WIDTH, 1024)).astype(bf16)
    for k in range(4):

        @pl.when(p == k)
        def _(k=k):
            for which in range(2):
                here = slice(which * ROWS, (which + 1) * ROWS)
                parts[which][k][:, :MODEL_WIDTH] = out[here]
                parts[which][k][:, MODEL_WIDTH:] = low[here]


def attention_back_kernel(at, *refs):
    rows_in = split_pieces(refs[:10])
    w, inner_in, query_in, kv_in, lse_in, att_in, o_out, o_in, q_out, bias = refs[10:20]
    query_b, output_a = refs[20:22]
    parts = (refs[22:26], refs[26:30])
    rows, ws, grad_k, grad_v, sems = refs[30:]
    s = pl.program_id(0)
    core = at[0]

    @pl.when(s == 0)
    def _():
        copy(w, ws, sems.at[1])
        for p in range(4):
            here = pl.ds(p * ROWS, ROWS)
            copy_place(rows_in[p], rows.at[0, here], rows.at[1, here], sems.at[0])
        query_b[...] = jnp.zeros_like(query_b)
        output_a[...] = jnp.zeros_like(output_a)
        wait(rows, sems.at[0])
        wait(ws, sems.at[1])

    owner = lane_owner(4 * ROWS, jnp.where(s == 0, core, 1 - core))
    scale = HEAD_WIDTH**-0.5
    x = rows[s]
    back = jnp.where(owner, dot_t(x, o_out[...]), 0.0)
    output_a[...] += dot(back.T[:32].astype(bf16), att_in[0])
    grad_att = (dot(x, ws[:, 512:]) + dot(back.astype(bf16), o_in[...])).astype(bf16)
    query = query_in[0]
    kv = kv_in[0]
    keys = kv[:, :, :HEAD_WIDTH].reshape(8 * ROWS, HEAD_WIDTH)
    values = kv[:, :, HEAD_WIDTH:].reshape(8 * ROWS, HEAD_WIDTH)
    keys_t = keys.astype(f32).T.astype(bf16)
    columns = []
    for h in range(2):
        chunks = []
        for c in range(2):
            lanes = slice(c * 256, c * 256 + 256)
            head = slice(h * HEAD_WIDTH, (h + 1) * HEAD_WIDTH)
            q, g = query[lanes, head], grad_att[lanes, head]
            scores = dot_t(keys, q) * scale
            scores = scores.reshape(8, ROWS, 256) + bias[:, lanes][:, None, :]
            probs = jnp.exp(scores.reshape(8 * ROWS, 256) - lse_in[0, h : h + 1, lanes])
            grad_probs = dot_t(values, g)
            delta = jnp.sum(probs * grad_probs, axis=0, keepdims=True)
            grad_scores = (probs * (grad_probs - delta)).astype(bf16)
            chunks.append((dot(keys_t, grad_scores) * scale).T)
            more_k = dot(grad_scores, q) * scale
            more_v = dot(probs.astype(bf16), g)
            if h == 0 and c == 0:
                grad_k[...] = more_k
                grad_v[...] = more_v
            else:
                grad_k[...] += more_k
                grad_v[...] += more_v
        columns.append(jnp.concatenate(chunks, axis=0))
    grad_query = jnp.concatenate(columns, axis=1).astype(bf16)
    query_b[...] += dot(inner_in[0].astype(f32).T[:32].astype(bf16), grad_query)
    low = jnp.where(owner, dot_t(grad_query, q_out[...]), 0.0).astype(bf16)
    for which in range(2):

        @pl.when(s == which)
        def _(which=which):
            for p in range(4):
                here = slice(p * ROWS, (p + 1) * ROWS)
                part = parts[which][p]
                part[:, :2048] = dot_t(grad_query[here], ws[:, :256]).astype(bf16)
                part[:, 2048:2176] = grad_k[here].astype(bf16)
                part[:, 2176:2304] = grad_v[here].astype(bf16)
                after = slice((p + 4) * ROWS, (p + 5) * ROWS)
                part[:, 2304:2432] = grad_k[after].astype(bf16)
                part[:, 2432:2560] = grad_v[after].astype(bf16)
                part[:, 2560:] = low[here]


VMEM_LIMIT = 56 * 1024 * 1024
ANY = pl.BlockSpec(memory_space=pl.ANY)


def whole_block(shape):
    return pl.BlockSpec(shape, lambda i, at: (0,) * len(shape))


def step_block(shape):
    return pl.BlockSpec((1, *shape), lambda i, at: (i,) + (0,) * len(shape))


def call(kernel, steps, at, ins, outs, scratch, name, flops=0):
    arrays = [a for a, _ in ins]
    in_specs = [whole_block(a.shape) if b is None else b for a, b in ins]
    out_specs = [whole_block(s) if b is None else b for s, _, b in outs]
    return pl.pallas_call(
        kernel,
        out_shape=[jax.ShapeDtypeStruct(s, d) for s, d, _ in outs],
        grid_spec=pltpu.PrefetchScalarGridSpec(
            num_scalar_prefetch=1,
            grid=(steps,),
            in_specs=in_specs,
            out_specs=out_specs,
            scratch_shapes=scratch,
        ),
        compiler_params=pltpu.CompilerParams(vmem_limit_bytes=VMEM_LIMIT),
        cost_estimate=pl.CostEstimate(
            flops=flops,
            bytes_accessed=sum(a.size * a.dtype.itemsize for a in arrays)
            + sum(math.prod(s) * 4 for s, _, _ in outs),
            transcendentals=0,
        ),
        name=name,
    )(at, *arrays)


def flat(places):
    return [(piece, ANY) for place in places for piece in place]


def part_outs(width):
    return [((ROWS, width), bf16, None)] * 8


def dma(n):
    return pltpu.SemaphoreType.DMA((n,))


def finish(gathered, ids, widths):
    total = gathered.shape[-1]
    return pl.pallas_call(
        functools.partial(finish_kernel, widths),
        out_shape=[
            jax.ShapeDtypeStruct((ADAPTER_COUNT, ADAPTER_RANK, 8 * w), f32) for w in widths
        ],
        grid_spec=pltpu.PrefetchScalarGridSpec(
            num_scalar_prefetch=1,
            grid=(4, 2),
            in_specs=[
                pl.BlockSpec((16, 1, 1, ADAPTER_RANK, total), lambda i, j, ids: (0, i, j, 0, 0))
            ],
            out_specs=[
                pl.BlockSpec((ADAPTER_COUNT, ADAPTER_RANK, w), lambda i, j, ids: (0, 0, j * 4 + i))
                for w in widths
            ],
        ),
        compiler_params=pltpu.CompilerParams(vmem_limit_bytes=VMEM_LIMIT),
        name="finish",
    )(ids, gathered)


def shards(
    tokens,
    cotangent,
    attention_norm_scale,
    attention_norm_bias,
    query_projection,
    query_projection_bias,
    keyvalue_projection,
    value_projection_bias,
    attention_output_weight,
    attention_output_bias,
    feedforward_norm_scale,
    feedforward_norm_bias,
    up_projection_weight,
    up_projection_bias,
    down_projection_weight,
    down_projection_bias,
    sequence_adapter,
    query_adapter_input,
    query_adapter_output,
    keyvalue_adapter_input,
    keyvalue_adapter_output,
    output_adapter_input,
    output_adapter_output,
    up_adapter_input,
    up_adapter_output,
    down_adapter_input,
    down_adapter_output,
):
    y, core, zl, zh, x = (lax.axis_index(n) for n in ("y", "core", "zl", "zh", "x"))
    z = zh * 2 + zl
    at = jnp.stack([core, x, zh, y, z]).astype(jnp.int32)
    gain_one, shift_one = attention_norm_scale.astype(f32), attention_norm_bias.astype(f32)
    gain_two, shift_two = feedforward_norm_scale.astype(f32), feedforward_norm_bias.astype(f32)

    attention_shard, feed_shard = call(
        pack_kernel,
        1,
        at,
        [
            (query_projection, None),
            (keyvalue_projection, None),
            (attention_output_weight, None),
            (up_projection_weight, None),
            (down_projection_weight, None),
        ],
        [((ROWS, 768), bf16, None), ((ROWS, 2048), bf16, None)],
        [],
        "pack",
    )
    feed = lax.all_gather(feed_shard, DP + ("zh",), axis=0, tiled=True)
    feed = feed.reshape(16, 2, ROWS, 2048)
    late_cotangent, late_ids, _ = lax.optimization_barrier((cotangent, sequence_adapter, feed))
    cot_all = lax.all_gather(late_cotangent, ("core", "x"), axis=0, tiled=True)
    cot_all = cot_all.reshape(2, 4, ROWS, MODEL_WIDTH)
    all_ids = lax.all_gather(late_ids, DP, axis=0, tiled=True)[:, 0]

    attention_shard = turn(attention_shard)
    half = ROWS // 2
    along_y = stacked_ring(gather_ring(attention_shard[:half], ring_y))
    along_z = stacked_ring(gather_ring(attention_shard[half:], ring_z))
    pieces = (*gather_ring(along_y, ring_z), *gather_ring(along_z, ring_y))
    (w,) = call(
        assemble_kernel,
        1,
        at,
        [(piece, ANY) for piece in pieces],
        [((MODEL_WIDTH, 768), bf16, None)],
        [pltpu.SemaphoreType.DMA],
        "assemble",
    )

    mine = sequence_adapter[0, 0]
    theirs = other_core(sequence_adapter)[0, 0]
    low = jnp.where(core == 0, mine, theirs)
    high = jnp.where(core == 0, theirs, mine)

    def ordered(stack):
        return jnp.concatenate([pick(stack, low), pick(stack, high)], axis=0)

    def ordered_t(stack):
        return ordered(jnp.swapaxes(stack, 1, 2))

    def padded(pair):
        return jnp.concatenate([pair, jnp.zeros((RIDE - 32, pair.shape[1]), bf16)], axis=0)

    small = jnp.concatenate(
        [
            ordered(query_adapter_output),
            ordered_t(output_adapter_input),
            ordered(up_adapter_output),
            ordered_t(down_adapter_input),
        ],
        axis=1,
    )
    biases = jnp.concatenate(
        [
            query_projection_bias,
            jnp.zeros((256,), bf16),
            up_projection_bias,
            jnp.zeros((1024,), bf16),
        ]
    )
    small = turn(jnp.concatenate([small, biases[None], jnp.zeros((15, 2560), bf16)], axis=0))
    q_bias, u_bias = small[32:33, :256].astype(f32), small[32:33, 512:1536].astype(f32)
    small = padded(small[:32])
    q_out, o_in, u_out, d_in = (
        small[:, :256],
        small[:, 256:512],
        small[:, 512:1536],
        small[:, 1536:],
    )
    q_in, u_in = padded(ordered_t(query_adapter_input)), padded(ordered_t(up_adapter_input))
    o_out, d_out = padded(ordered(output_adapter_output)), padded(ordered(down_adapter_output))

    input_rows = tokens.astype(f32)
    normed = layer_norm(input_rows, gain_one, shift_one).astype(bf16)
    normed_places = gather_row(normed)

    kv_in, kv_out = pick(keyvalue_adapter_input, mine), pick(keyvalue_adapter_output, mine)
    keyval_inner = dot(normed, kv_in).astype(bf16)
    keyval_bias = jnp.concatenate(
        [jnp.zeros((HEAD_WIDTH,), f32), value_projection_bias.astype(f32)]
    )
    keyval = (dot(normed, w[:, 256:512]) + keyval_bias + dot(keyval_inner, kv_out)).astype(bf16)
    keyval = jnp.concatenate([keyval, other_half(keyval)], axis=1)
    keyval = jnp.concatenate([keyval, other_core(keyval)], axis=0)
    keyval_places = (keyval, ring_x(keyval, 1), ring_x(keyval, -1), ring_x(keyval, 2))

    place_block = jnp.stack([lax.rem(x + p, 4) for p in PLACES]) // 2
    own = place_block[:, None] <= place_block[None, :]
    bias = jnp.concatenate([own, jnp.broadcast_to(zh == 1, (4, 4))], axis=0)
    bias = jnp.repeat(jnp.where(bias, 0.0, -1e30).astype(f32), ROWS, axis=1)

    group = (2, 4 * ROWS)
    row_scratch = pltpu.VMEM((2, 4 * ROWS, MODEL_WIDTH), bf16)
    w_scratch = pltpu.VMEM((MODEL_WIDTH, 768), bf16)
    inner_one, query, keyval_all, log_total, attended, *out_parts = call(
        attention_kernel,
        2,
        at,
        [
            *flat(normed_places),
            *[(piece, ANY) for piece in keyval_places],
            (w, ANY),
            (q_in, None),
            (q_out, None),
            (o_in, None),
            (q_bias, None),
            (bias, None),
        ],
        [
            ((*group, RIDE), bf16, step_block((4 * ROWS, RIDE))),
            ((*group, 256), bf16, step_block((4 * ROWS, 256))),
            ((2, 8, ROWS, 256), bf16, step_block((8, ROWS, 256))),
            ((2, 2, 4 * ROWS), f32, step_block((2, 4 * ROWS))),
            ((*group, 256), bf16, step_block((4 * ROWS, 256))),
            *part_outs(MODEL_WIDTH + RIDE),
        ],
        [row_scratch, pltpu.VMEM((2, 8, ROWS, 256), bf16), w_scratch, dma(3)],
        "attention",
        9000000000,
    )
    out_sum = scatter_row(out_parts[:4], out_parts[4:])
    output_inner = out_sum[:, MODEL_WIDTH:].astype(bf16)
    middle = (
        input_rows
        + out_sum[:, :MODEL_WIDTH]
        + attention_output_bias.astype(f32)
        + dot(output_inner, o_out)
    )
    normed_two = layer_norm(middle, gain_two, shift_two).astype(bf16)
    place_scratch = pltpu.VMEM((4, 2 * ROWS, MODEL_WIDTH), bf16)
    feed_scratch = pltpu.VMEM((16, ROWS, 1024), bf16)
    inner_two, pre, act, *down_parts = call(
        feed_kernel,
        4,
        at,
        [
            *flat(gather_row(normed_two)),
            (feed, ANY),
            (u_in, None),
            (u_out, None),
            (d_in, None),
            (u_bias, None),
        ],
        [
            ((4, 2 * ROWS, RIDE), bf16, step_block((2 * ROWS, RIDE))),
            ((4, 2 * ROWS, 1024), f32, step_block((2 * ROWS, 1024))),
            ((4, 2 * ROWS, 1024), bf16, step_block((2 * ROWS, 1024))),
            *part_outs(MODEL_WIDTH + RIDE),
        ],
        [place_scratch, feed_scratch, feed_scratch, dma(6)],
        "feed",
        9500000000,
    )
    down_sum = scatter_row(down_parts[:4], down_parts[4:])
    down_inner = down_sum[:, MODEL_WIDTH:].astype(bf16)
    layer_output = (
        middle
        + down_sum[:, :MODEL_WIDTH]
        + down_projection_bias.astype(f32)
        + dot(down_inner, d_out)
    ).astype(bf16)

    up_b, down_a, *up_parts = call(
        feed_back_kernel,
        4,
        at,
        [
            (cot_all, ANY),
            (feed, ANY),
            (pre, step_block((2 * ROWS, 1024))),
            (act, step_block((2 * ROWS, 1024))),
            (inner_two, step_block((2 * ROWS, RIDE))),
            (d_out, None),
            (d_in, None),
            (u_out, None),
        ],
        [((32, 1024), f32, None), ((32, 1024), f32, None), *part_outs(MODEL_WIDTH + RIDE)],
        [place_scratch, feed_scratch, feed_scratch, dma(6)],
        "feed_back",
        9500000000,
    )
    up_sum = scatter_row(up_parts[:4], up_parts[4:])
    up_back = up_sum[:, MODEL_WIDTH:].astype(bf16)
    grad_normed_two = up_sum[:, :MODEL_WIDTH] + dot(up_back, u_in)
    _, norm_two_back = jax.vjp(lambda v: layer_norm(v, gain_two, shift_two), middle)
    grad_middle = cotangent.astype(f32) + norm_two_back(grad_normed_two)[0]
    grad_branch = grad_middle.astype(bf16)

    query_b, output_a, *query_parts = call(
        attention_back_kernel,
        2,
        at,
        [
            *flat(gather_row(grad_branch)),
            (w, ANY),
            (inner_one, step_block((4 * ROWS, RIDE))),
            (query, step_block((4 * ROWS, 256))),
            (keyval_all, step_block((8, ROWS, 256))),
            (log_total, step_block((2, 4 * ROWS))),
            (attended, step_block((4 * ROWS, 256))),
            (o_out, None),
            (o_in, None),
            (q_out, None),
            (bias, None),
        ],
        [((32, 256), f32, None), ((32, 256), f32, None), *part_outs(2688)],
        [
            row_scratch,
            w_scratch,
            pltpu.VMEM((8 * ROWS, HEAD_WIDTH), f32),
            pltpu.VMEM((8 * ROWS, HEAD_WIDTH), f32),
            dma(2),
        ],
        "attention_back",
        8000000000,
    )
    query_sum = scatter_row(query_parts[:4], query_parts[4:])
    grad_keyval = (
        query_sum[:, 2048:2304] + other_half(query_sum[:, 2304:2560].astype(bf16)).astype(f32)
    ).astype(bf16)
    query_back = query_sum[:, 2560:].astype(bf16)
    keyval_back = dot_t(grad_keyval, kv_out).astype(bf16)
    grad_normed = (
        query_sum[:, :MODEL_WIDTH]
        + dot(query_back, q_in)
        + dot_t(grad_keyval, w[:, 256:512])
        + dot_t(keyval_back, kv_in)
    )
    _, norm_one_back = jax.vjp(lambda v: layer_norm(v, gain_one, shift_one), input_rows)
    grad_tokens = (grad_middle + norm_one_back(grad_normed)[0]).astype(bf16)

    def ridden(back, rows):
        piece = tdot(back, rows)
        return piece[:16] + piece[16:32]

    def sliced(piece):
        return piece.reshape(16, 2, 4, -1).transpose(1, 2, 0, 3)

    def joined(*pieces):
        return jnp.concatenate([p.astype(bf16) for p in pieces], axis=-1)

    early = gather_sequences(own_slice(jnp.concatenate([up_b, down_a], axis=1), zh), zh, x)
    up_b, down_a = finish(early, all_ids, (1024, 1024))
    middle_set = joined(
        scatter_sequence(
            jnp.concatenate(
                [
                    sliced(ridden(up_back, normed_two)),
                    sliced(ridden(down_inner, cotangent)),
                    sliced(ridden(output_inner, grad_branch)),
                ],
                axis=-1,
            ),
            zh,
            x,
        ),
        own_slice(output_a, zh),
    )
    up_a, down_b, output_b, output_a = finish(
        gather_sequences(middle_set, zh, x), all_ids, (256, 256, 256, 256)
    )
    keyval_b = tdot(keyval_inner, grad_keyval).reshape(2, 4, 16, 32)
    late_set = joined(
        scatter_sequence(
            jnp.concatenate(
                [
                    sliced(ridden(query_back, normed)),
                    sliced(tdot(keyval_back, normed)),
                    jnp.pad(keyval_b, ((0, 0), (0, 0), (0, 0), (0, 96))),
                ],
                axis=-1,
            ),
            zh,
            x,
        ),
        own_slice(query_b, zh),
    )
    query_a, keyval_a, keyval_b, query_b = finish(
        gather_sequences(late_set, zh, x), all_ids, (256, 256, 128, 256)
    )
    keyval_b = keyval_b.reshape(8, 16, 8, 128)[..., :32].transpose(0, 2, 1, 3).reshape(8, 16, 256)

    def side_in(a):
        return jnp.swapaxes(a, 1, 2)

    return (
        layer_output,
        grad_tokens,
        side_in(query_a),
        query_b,
        side_in(keyval_a),
        keyval_b,
        side_in(output_a),
        output_b,
        side_in(up_a),
        up_b,
        side_in(down_a),
        down_b,
    )

def solution(mesh):
    fine = Mesh(mesh.devices.reshape(SIZES), AXES)
    in_specs = (
        P(AXES, None),
        P(AXES, None),
        P(),
        P(),
        P(DP, MP),
        P(MP),
        P(DP, None),
        P(),
        P(MP, DP),
        P(),
        P(),
        P(),
        P(DP, MP),
        P(MP),
        P(MP, DP),
        P(),
        P(DP, None),
        P(),
        P(None, None, MP),
        P(),
        P(),
        P(None, MP, None),
        P(),
        P(),
        P(None, None, MP),
        P(None, MP, None),
        P(),
    )
    out_specs = (P(AXES, None), P(AXES, None)) + (P(),) * 10
    return jax.shard_map(shards, mesh=fine, in_specs=in_specs, out_specs=out_specs, check_vma=False)
```

```python
import functools
import math

import jax
import jax.numpy as jnp
from jax import lax
from jax.experimental import pallas as pl
from jax.experimental.pallas import tpu as pltpu
from jax.sharding import Mesh
from jax.sharding import PartitionSpec as P

MODEL_WIDTH = 2048
H = 16
HEAD_WIDTH = 128
FEED_HIDDEN = 8192
ADAPTER_RANK = 16
ADAPTER_COUNT = 8
BLOCK = 256

AXES = ("y", "zl", "core", "zh", "x")
SIZES = (4, 2, 2, 2, 4)
DP = ("y", "zl", "core")
MP = ("zh", "x")
PLACES = (0, 3, 1, 2)
Z_RING = (0, 2, 1, 3)
ROWS = 128
RIDE = 128

f32 = jnp.float32
bf16 = jnp.bfloat16


def ring_x(a, step):
    return lax.ppermute(a, "x", [(i, (i + step) % 4) for i in range(4)])


def ring_y(a, step):
    return lax.ppermute(a, "y", [(i, (i + step) % 4) for i in range(4)])


def ring_z(a, step):
    return lax.ppermute(a, ("zl", "zh"), [(Z_RING[i], Z_RING[(i + step) % 4]) for i in range(4)])


def other_core(a):
    return lax.ppermute(a, "core", [(0, 1), (1, 0)])


def other_half(a):
    return lax.ppermute(a, "zh", [(0, 1), (1, 0)])


def turn(a):
    return lax.ppermute(a, ("core", "zh"), [(0, 0), (1, 2), (2, 1), (3, 3)])


def plane_pairs(step, swapped):
    def index(y, z, core):
        return ((y * 2 + z % 2) * 2 + core) * 2 + z // 2

    pairs = []
    for y in range(4):
        for z in range(4):
            for core in range(2):
                if (core == 0) != swapped:
                    to = index((y + step) % 4, z, core)
                else:
                    to = index(y, (z + step) % 4, core)
                pairs.append((index(y, z, core), to))
    return pairs


def gather_cross(a, swapped):
    return [a] + [
        lax.ppermute(a, ("y", "zl", "core", "zh"), plane_pairs(-step, swapped))
        for step in (1, 2, 3)
    ]


def gather_sides(a):
    return a, other_core(a), ring_x(a, 1), ring_x(a, -1)


def gather_rest(a, near, left, right):
    half = a.shape[0] // 2
    top, bottom = ring_x(left[:half], 1), ring_x(right[half:], -1)
    return (
        (a, near),
        (left, other_core(left)),
        (right, other_core(right)),
        (top, bottom, other_core(top), other_core(bottom)),
    )


def gather_row(a):
    return gather_rest(*gather_sides(a))


def add_cores(mine, theirs):
    return mine.astype(f32) + other_core(theirs).astype(f32)


def scatter_row(mine, theirs, far_mine, far_theirs):
    half = far_mine.shape[0] // 2
    far = add_cores(far_mine, far_theirs).astype(bf16)
    up, down = ring_x(far[:half], 1), ring_x(far[half:], -1)
    near = add_cores(mine, theirs)
    right = jnp.concatenate([near[2, :half] + up.astype(f32), near[2, half:]]).astype(bf16)
    left = jnp.concatenate([near[1, :half], near[1, half:] + down.astype(f32)]).astype(bf16)
    return near[0] + ring_x(right, 1).astype(f32) + ring_x(left, -1).astype(f32)


def scatter_start(mine, theirs, far_mine, far_theirs):
    far = add_cores(far_mine, far_theirs).astype(bf16)
    near = add_cores(mine, theirs)
    return near[0], near[1].astype(bf16), near[2].astype(bf16), far


def scatter_last(near, left, right, far):
    parts = (ring_x(left, -1), ring_x(right, 1), ring_x(far, 2))
    return near + sum(part.astype(f32) for part in parts)


def rolled(blocks, me, step=0):
    both = jnp.concatenate([blocks, blocks], axis=0)
    return lax.dynamic_slice_in_dim(both, lax.rem(me + step, 4), 4, 0)


def ring_by_core(a):
    pairs = [(i, (i + 1) % 4) for i in range(4)] + [(4 + i, 4 + (i + 3) % 4) for i in range(4)]
    return lax.ppermute(a, ("core", "x"), pairs)


def by_core(core, own, other):
    return jnp.where(
        core == 0, jnp.concatenate([own, other], -1), jnp.concatenate([other, own], -1)
    )


def row_slice(pair, core):
    own = jnp.where(core == 0, pair[:16], pair[16:]).astype(bf16)
    other = jnp.where(core == 0, pair[16:], pair[:16]).astype(bf16)
    return by_core(core, own, other_core(other))


def scatter_sequence(slices):
    low = slices
    return (
        low[0].astype(f32)
        + ring_x(low[1], 1).astype(f32)
        + ring_x(low[3], -1).astype(f32)
        + ring_x(low[2], 2).astype(f32)
    ).astype(bf16)


def layer_norm(values, gain, shift):
    mean_value = jnp.mean(values, axis=-1, keepdims=True)
    centred = values - mean_value
    variance = jnp.mean(centred * centred, axis=-1, keepdims=True)
    return centred * lax.rsqrt(variance + 1e-05) * gain + shift


def gelu_tanh(values):
    inner_product = math.sqrt(2.0 / math.pi) * (values + 0.044715 * values * values * values)
    return 0.5 * values * (1.0 + jnp.tanh(inner_product))


def pick(adapter_stack, position):
    return lax.dynamic_index_in_dim(adapter_stack, position, 0, keepdims=False)


def dot(left, right):
    return jnp.dot(left, right, preferred_element_type=f32)


def dot_t(left, right):
    return lax.dot_general(left, right, (((1,), (1,)), ((), ())), preferred_element_type=f32)


def tdot(left, right):
    return lax.dot_general(left, right, (((0,), (0,)), ((), ())), preferred_element_type=f32)


def lane_owner(rows, row_core):
    lane = lax.broadcasted_iota(jnp.int32, (rows, RIDE), 1)
    owner = lax.rem(lane // ADAPTER_RANK, 2)
    return jnp.logical_and(owner == row_core, lane < 4 * ADAPTER_RANK)


def place_mask(core):
    row = lax.broadcasted_iota(jnp.int32, (2 * ROWS, RIDE), 0)
    return lane_owner(2 * ROWS, jnp.where(row < ROWS, core, 1 - core))


def copy(source, target, sem):
    pltpu.make_async_copy(source, target, sem).start()


def wait(target, sem):
    pltpu.make_async_copy(target, target, sem).wait()


def copy_place(pieces, target_mine, target_theirs, sem):
    half = ROWS // 2
    if len(pieces) == 2:
        copy(pieces[0], target_mine, sem)
        copy(pieces[1], target_theirs, sem)
    else:
        copy(pieces[0], target_mine.at[pl.ds(0, half)], sem)
        copy(pieces[1], target_mine.at[pl.ds(half, half)], sem)
        copy(pieces[2], target_theirs.at[pl.ds(0, half)], sem)
        copy(pieces[3], target_theirs.at[pl.ds(half, half)], sem)


def split_pieces(refs):
    return (refs[0:2], refs[2:4], refs[4:6], refs[6:10])


def copy_row(gathered, at, target_of, sem_of):
    core, x = at[0], at[1]
    for p in range(4):
        there = lax.rem(x + PLACES[p], 4)
        copy(gathered.at[core, there], target_of(p, 0), sem_of(p))
        copy(gathered.at[1 - core, there], target_of(p, 1), sem_of(p))


def assemble_kernel(at, *refs):
    pieces, (out, sem) = refs[:4], refs[4:]
    core, y, z = at[0], at[3], at[4]
    for far, piece in enumerate(pieces):
        for near in range(4):
            to_y = lax.rem(y + jnp.where(core == 0, near, far), 4)
            to_z = lax.rem(z + jnp.where(core == 0, far, near), 4)
            shard = (to_y * 2 + lax.rem(to_z, 2)) * 2 + to_z // 2
            copy(piece.at[near], out.at[pl.ds(pl.multiple_of(shard * ROWS, ROWS), ROWS)], sem)
    wait(out, sem)


def pack_kernel(at, query, keyval, output, up, down, attention_out, feed_out):
    attention_out[:, :256] = query[...]
    attention_out[:, 256:512] = keyval[...]
    attention_out[:, 512:] = output[...].astype(f32).T.astype(bf16)
    feed_out[:, :1024] = up[...]
    feed_out[:, 1024:] = down[...].astype(f32).T.astype(bf16)


def sum_kernel(at, *refs):
    pieces, (out, total) = refs[:-2], refs[-2:]
    total[...] = jnp.zeros_like(total)
    count = out.shape[0]
    row = 1
    for piece in pieces:
        for k in range(piece.shape[0]):
            place = at[row] - at[0]
            place = jnp.where(jnp.logical_and(place >= 0, place < count), place, count)
            total[place] += piece[k].astype(f32)
            row += 1
    out[...] = total[:count].astype(bf16)


def slices_kernel(count, at, *refs):
    ins, out = refs[: 2 * count], refs[2 * count]
    x = at[1]
    for n in range(count):
        back, rows = ins[2 * n], ins[2 * n + 1]
        turned = back[...].astype(f32).T
        turned = (turned[:16] + turned[16:32]).astype(bf16)
        product = dot(turned, rows[...]).astype(bf16)
        for to in range(4):
            place = lax.rem(to + 4 - x, 4)
            for c in range(2):
                first = (c * 4 + to) * 256
                lanes = slice(n * 512 + c * 256, n * 512 + (c + 1) * 256)
                out[place, :, lanes] = product[:, first : first + 256]


def spread(scratch, outs, widths):
    x, c = pl.program_id(0), pl.program_id(1)
    first = 0
    for out, width in zip(outs, widths):
        if width < 128:
            out[...] = scratch[x, :, :, first : first + 128].astype(f32)
            first += 128
        else:
            here = pl.ds(pl.multiple_of(first + c * width, 128), width)
            out[...] = scratch[x, :, :, here].astype(f32)
            first += 2 * width


def feed_spread_kernel(widths, at, *refs):
    gathered, (scratch, sem) = refs[0], refs[-2:]

    @pl.when((pl.program_id(0) == 0) & (pl.program_id(1) == 0))
    def _():
        for c in range(2):
            for x in range(4):
                copy(gathered.at[c, x], scratch.at[x, pl.ds(4 * c, 4)], sem)
        wait(scratch, sem)

    spread(scratch, refs[1:-2], widths)


def late_spread_kernel(widths, at, *refs):
    own, other, near, near_other, far, far_other = refs[:6]
    scratch, sem = refs[-2:]
    core, x = at[0], at[1]

    @pl.when((pl.program_id(0) == 0) & (pl.program_id(1) == 0))
    def _():
        mine, theirs = pl.ds(4 * core, 4), pl.ds(4 * (1 - core), 4)
        side = lax.rem(x + jnp.where(core == 0, 3, 1), 4)
        other_side = lax.rem(x + jnp.where(core == 0, 1, 3), 4)
        across = lax.rem(x + 2, 4)
        copy(own, scratch.at[x, mine], sem)
        copy(other, scratch.at[x, theirs], sem)
        for part, where in ((0, mine), (1, theirs)):
            copy(near.at[pl.ds(4 * part, 4)], scratch.at[side, where], sem)
        for part, where in ((0, theirs), (1, mine)):
            copy(near_other.at[pl.ds(4 * part, 4)], scratch.at[other_side, where], sem)
        copy(far, scratch.at[across, mine], sem)
        copy(far_other, scratch.at[across, theirs], sem)
        wait(scratch, sem)

    spread(scratch, refs[6:-2], widths)


def attention_kernel(at, *refs):
    rows_in = split_pieces(refs[:10])
    kv_in = refs[10:14]
    w, q_in, q_out, kv_out, o_in, q_bias, kv_bias, bias = refs[14:22]
    inner_out, query_out, kv_all, lse_out, att_out = refs[22:27]
    parts, far_parts = refs[27:29], refs[29:31]
    rows, kvs, ws, sems = refs[31:]
    s = pl.program_id(0)
    core = at[0]

    @pl.when(s == 0)
    def _():
        copy(w, ws, sems.at[2])
        for p in range(4):
            here = pl.ds(p * ROWS, ROWS)
            copy_place(rows_in[p], rows.at[0, here], rows.at[1, here], sems.at[0])
            for q in range(2):
                copy(kv_in[p].at[pl.ds(q * ROWS, ROWS)], kvs.at[q, p], sems.at[1])
        wait(rows, sems.at[0])
        wait(ws, sems.at[2])
        wait(kvs, sems.at[1])

    owner = lane_owner(4 * ROWS, jnp.where(s == 0, core, 1 - core))
    x = rows[s]
    inner = jnp.where(owner, dot_t(x, q_in[...]), 0.0).astype(bf16)
    inner_out[0] = inner
    query = (dot(x, ws[:, :256]) + q_bias[...] + dot(inner, q_out[...])).astype(bf16)
    query_out[0] = query
    kv_own = (dot(x, ws[:, 256:512]) + kv_bias[...] + dot(inner, kv_out[...])).astype(bf16)
    kv = jnp.concatenate([kv_own.reshape(4, ROWS, 256), kvs[s]], axis=0)
    kv_all[0] = kv
    keys = kv[:, :, :HEAD_WIDTH].reshape(8 * ROWS, HEAD_WIDTH)
    values_t = kv[:, :, HEAD_WIDTH:].reshape(8 * ROWS, HEAD_WIDTH).astype(f32).T.astype(bf16)
    columns = []
    for h in range(2):
        chunks = []
        for c in range(2):
            lanes = slice(c * 256, c * 256 + 256)
            q = query[lanes, h * HEAD_WIDTH : (h + 1) * HEAD_WIDTH]
            scores = dot_t(keys, q) * (HEAD_WIDTH**-0.5)
            scores = scores.reshape(8, ROWS, 256) + bias[:, lanes][:, None, :]
            scores = scores.reshape(8 * ROWS, 256)
            top = jnp.max(scores, axis=0, keepdims=True)
            expo = jnp.exp(scores - top)
            total = jnp.sum(expo, axis=0, keepdims=True)
            probs = (expo * (1.0 / total)).astype(bf16)
            lse_out[0, h : h + 1, lanes] = top + jnp.log(total)
            chunks.append(dot(values_t, probs).T)
        columns.append(jnp.concatenate(chunks, axis=0))
    attended = jnp.concatenate(columns, axis=1).astype(bf16)
    att_out[0] = attended
    low = jnp.where(owner, dot_t(attended, o_in[...]), 0.0).astype(bf16)
    for which in range(2):

        @pl.when(s == which)
        def _(which=which):
            for p in range(4):
                here = slice(p * ROWS, (p + 1) * ROWS)
                part = parts[which].at[p] if p < 3 else far_parts[which]
                part[:, :MODEL_WIDTH] = dot_t(attended[here], ws[:, 512:]).astype(bf16)
                part[:, MODEL_WIDTH:] = low[here]


def store_parts(p, parts, far_parts, out, low):
    for which in range(2):
        here = slice(which * ROWS, (which + 1) * ROWS)

        @pl.when(p < 3)
        def _(which=which, here=here):
            parts[which][0, :, :MODEL_WIDTH] = out[here]
            parts[which][0, :, MODEL_WIDTH:] = low[here]

        @pl.when(p == 3)
        def _(which=which, here=here):
            far_parts[which][:, :MODEL_WIDTH] = out[here]
            far_parts[which][:, MODEL_WIDTH:] = low[here]


def feed_kernel(at, *refs):
    rows_in = split_pieces(refs[:10])
    feed, u_in, u_out, d_in, u_bias = refs[10:15]
    inner_out, pre_out, act_out = refs[15:18]
    parts, far_parts = refs[18:20], refs[20:22]
    rows, up, down, sems = refs[22:]
    p = pl.program_id(0)
    core = at[0]

    @pl.when(p == 0)
    def _():
        copy(feed.at[:, core, :, pl.ds(0, 1024)], up, sems.at[4])
        for k in range(4):
            copy_place(
                rows_in[k], rows.at[k, pl.ds(0, ROWS)], rows.at[k, pl.ds(ROWS, ROWS)], sems.at[k]
            )
        copy(feed.at[:, core, :, pl.ds(1024, 1024)], down, sems.at[5])
        wait(up, sems.at[4])

    wait(rows.at[p], sems.at[p])
    mask = place_mask(core)
    x = rows[p]
    inner = jnp.where(mask, dot_t(x, u_in[...]), 0.0).astype(bf16)
    inner_out[0] = inner
    pre = dot(x, up[...].reshape(MODEL_WIDTH, 1024)) + u_bias[...] + dot(inner, u_out[...])
    pre_out[0] = pre
    act = gelu_tanh(pre).astype(bf16)
    act_out[0] = act

    @pl.when(p == 0)
    def _():
        wait(down, sems.at[5])

    low = jnp.where(mask, dot_t(act, d_in[...]), 0.0).astype(bf16)
    out = dot_t(act, down[...].reshape(MODEL_WIDTH, 1024)).astype(bf16)
    store_parts(p, parts, far_parts, out, low)


def feed_back_kernel(at, *refs):
    cot, feed, pre_in, act_in, inner_in, d_out, d_in, u_out = refs[:8]
    up_b, down_a = refs[8:10]
    parts, far_parts = refs[10:12], refs[12:14]
    rows, up, down, sems = refs[14:]
    p = pl.program_id(0)
    core = at[0]

    @pl.when(p == 0)
    def _():
        copy(feed.at[:, core, :, pl.ds(1024, 1024)], down, sems.at[5])
        copy_row(
            cot, at, lambda k, which: rows.at[k, pl.ds(which * ROWS, ROWS)], lambda k: sems.at[k]
        )
        copy(feed.at[:, core, :, pl.ds(0, 1024)], up, sems.at[4])
        up_b[...] = jnp.zeros_like(up_b)
        down_a[...] = jnp.zeros_like(down_a)
        wait(down, sems.at[5])

    wait(rows.at[p], sems.at[p])
    mask = place_mask(core)
    grad = rows[p]
    back = jnp.where(mask, dot_t(grad, d_out[...]), 0.0)
    back_t = back.T[:32].astype(bf16)
    act = act_in[0]
    down_a[...] += dot(back_t, act)
    grad_act = dot(grad, down[...].reshape(MODEL_WIDTH, 1024)) + dot(back.astype(bf16), d_in[...])
    pre = pre_in[0]
    k0 = math.sqrt(2.0 / math.pi)
    square = pre * pre
    bend = jnp.tanh(k0 * (pre + 0.044715 * square * pre))
    slope = 0.5 * (1.0 + bend) + 0.5 * pre * (1.0 - bend * bend) * (
        k0 * (1.0 + 3.0 * 0.044715 * square)
    )
    grad_pre = (grad_act * slope).astype(bf16)
    inner_t = inner_in[0].astype(f32).T[:32].astype(bf16)
    up_b[...] += dot(inner_t, grad_pre)
    low = jnp.where(mask, dot_t(grad_pre, u_out[...]), 0.0).astype(bf16)

    @pl.when(p == 0)
    def _():
        wait(up, sems.at[4])

    out = dot_t(grad_pre, up[...].reshape(MODEL_WIDTH, 1024)).astype(bf16)
    store_parts(p, parts, far_parts, out, low)


def attention_back_kernel(at, *refs):
    branch, w, inner_in, query_in, kv_in, lse_in, att_in, o_out, o_in, q_out, bias = refs[:11]
    query_b, output_a = refs[11:13]
    parts, far_parts = refs[13:15], refs[15:17]
    rows, ws, grad_k, grad_v, sems = refs[17:]
    s = pl.program_id(0)
    core = at[0]

    @pl.when(s == 0)
    def _():
        copy(w, ws, sems.at[1])
        copy_row(
            branch, at, lambda p, which: rows.at[which, pl.ds(p * ROWS, ROWS)], lambda p: sems.at[0]
        )
        query_b[...] = jnp.zeros_like(query_b)
        output_a[...] = jnp.zeros_like(output_a)
        wait(rows, sems.at[0])
        wait(ws, sems.at[1])

    owner = lane_owner(4 * ROWS, jnp.where(s == 0, core, 1 - core))
    scale = HEAD_WIDTH**-0.5
    x = rows[s]
    back = jnp.where(owner, dot_t(x, o_out[...]), 0.0)
    output_a[...] += dot(back.T[:32].astype(bf16), att_in[0])
    grad_att = (dot(x, ws[:, 512:]) + dot(back.astype(bf16), o_in[...])).astype(bf16)
    query = query_in[0]
    kv = kv_in[0]
    keys = kv[:, :, :HEAD_WIDTH].reshape(8 * ROWS, HEAD_WIDTH)
    values = kv[:, :, HEAD_WIDTH:].reshape(8 * ROWS, HEAD_WIDTH)
    keys_t = keys.astype(f32).T.astype(bf16)
    columns = []
    for h in range(2):
        chunks = []
        for c in range(2):
            lanes = slice(c * 256, c * 256 + 256)
            head = slice(h * HEAD_WIDTH, (h + 1) * HEAD_WIDTH)
            q, g = query[lanes, head], grad_att[lanes, head]
            scores = dot_t(keys, q) * scale
            scores = scores.reshape(8, ROWS, 256) + bias[:, lanes][:, None, :]
            probs = jnp.exp(scores.reshape(8 * ROWS, 256) - lse_in[0, h : h + 1, lanes])
            grad_probs = dot_t(values, g)
            delta = jnp.sum(probs * grad_probs, axis=0, keepdims=True)
            grad_scores = (probs * (grad_probs - delta)).astype(bf16)
            chunks.append((dot(keys_t, grad_scores) * scale).T)
            more_k = dot(grad_scores, q) * scale
            more_v = dot(probs.astype(bf16), g)
            if h == 0 and c == 0:
                grad_k[...] = more_k
                grad_v[...] = more_v
            else:
                grad_k[...] += more_k
                grad_v[...] += more_v
        columns.append(jnp.concatenate(chunks, axis=0))
    grad_query = jnp.concatenate(columns, axis=1).astype(bf16)
    query_b[...] += dot(inner_in[0].astype(f32).T[:32].astype(bf16), grad_query)
    low = jnp.where(owner, dot_t(grad_query, q_out[...]), 0.0).astype(bf16)
    for which in range(2):

        @pl.when(s == which)
        def _(which=which):
            for p in range(4):
                here = slice(p * ROWS, (p + 1) * ROWS)
                part = parts[which].at[p] if p < 3 else far_parts[which]
                part[:, :2048] = dot_t(grad_query[here], ws[:, :256]).astype(bf16)
                part[:, 2048:2176] = grad_k[here].astype(bf16)
                part[:, 2176:2304] = grad_v[here].astype(bf16)
                after = slice((p + 4) * ROWS, (p + 5) * ROWS)
                part[:, 2304:2432] = grad_k[after].astype(bf16)
                part[:, 2432:2560] = grad_v[after].astype(bf16)
                part[:, 2560:] = low[here]


VMEM_LIMIT = 56 * 1024 * 1024
ANY = pl.BlockSpec(memory_space=pl.ANY)


def whole_block(shape):
    return pl.BlockSpec(shape, lambda i, at: (0,) * len(shape))


def step_block(shape):
    return pl.BlockSpec((1, *shape), lambda i, at: (i,) + (0,) * len(shape))


def call(kernel, steps, at, ins, outs, scratch, name, flops=0):
    arrays = [a for a, _ in ins]
    in_specs = [whole_block(a.shape) if b is None else b for a, b in ins]
    out_specs = [whole_block(s) if b is None else b for s, _, b in outs]
    return pl.pallas_call(
        kernel,
        out_shape=[jax.ShapeDtypeStruct(s, d) for s, d, _ in outs],
        grid_spec=pltpu.PrefetchScalarGridSpec(
            num_scalar_prefetch=1,
            grid=(steps,),
            in_specs=in_specs,
            out_specs=out_specs,
            scratch_shapes=scratch,
        ),
        compiler_params=pltpu.CompilerParams(vmem_limit_bytes=VMEM_LIMIT),
        cost_estimate=pl.CostEstimate(
            flops=flops,
            bytes_accessed=sum(a.size * a.dtype.itemsize for a in arrays)
            + sum(math.prod(s) * 4 for s, _, _ in outs),
            transcendentals=0,
        ),
        name=name,
    )(at, *arrays)


def flat(places):
    return [(piece, ANY) for place in places for piece in place]


def part_outs(width, steps=False):
    block = pl.BlockSpec((1, ROWS, width), lambda i, at: (jnp.minimum(i, 2), 0, 0))
    near = ((3, ROWS, width), bf16, block if steps else None)
    return [near, near, ((ROWS, width), bf16, None), ((ROWS, width), bf16, None)]


def dma(n):
    return pltpu.SemaphoreType.DMA((n,))


def sum_by_adapter(pieces, first, ids, count):
    width = pieces[0].shape[-1]
    block = max(w for w in range(128, 2305, 128) if width % w == 0)
    return pl.pallas_call(
        sum_kernel,
        out_shape=jax.ShapeDtypeStruct((count, ADAPTER_RANK, width), bf16),
        grid_spec=pltpu.PrefetchScalarGridSpec(
            num_scalar_prefetch=1,
            grid=(width // block,),
            in_specs=[
                pl.BlockSpec((p.shape[0], ADAPTER_RANK, block), lambda i, at: (0, 0, i))
                for p in pieces
            ],
            out_specs=pl.BlockSpec((count, ADAPTER_RANK, block), lambda i, at: (0, 0, i)),
            scratch_shapes=[pltpu.VMEM((count + 1, ADAPTER_RANK, block), f32)],
        ),
        compiler_params=pltpu.CompilerParams(vmem_limit_bytes=VMEM_LIMIT),
        name="sum_by_adapter",
    )(jnp.concatenate([jnp.reshape(first, (1,)), ids]).astype(jnp.int32), *pieces)


def spread_out(kernel, at, pieces, widths, name):
    total = pieces[0].shape[-1]
    wide = [(w, lambda i, j, at: (0, 0, j * 4 + i)) for w in widths]
    blocks = [b if b[0] >= 128 else (128, lambda i, j, at: (0, 0, i)) for b in wide]
    return pl.pallas_call(
        functools.partial(kernel, widths),
        out_shape=[
            jax.ShapeDtypeStruct((ADAPTER_COUNT, ADAPTER_RANK, 8 * w if w >= 128 else 512), f32)
            for w in widths
        ],
        grid_spec=pltpu.PrefetchScalarGridSpec(
            num_scalar_prefetch=1,
            grid=(4, 2),
            in_specs=[ANY] * len(pieces),
            out_specs=[pl.BlockSpec((ADAPTER_COUNT, ADAPTER_RANK, w), m) for w, m in blocks],
            scratch_shapes=[
                pltpu.VMEM((4, ADAPTER_COUNT, ADAPTER_RANK, total), bf16),
                pltpu.SemaphoreType.DMA,
            ],
        ),
        compiler_params=pltpu.CompilerParams(vmem_limit_bytes=VMEM_LIMIT),
        name=name,
    )(at, *pieces)


def slices_of(at, pairs, name):
    shape = (4, ADAPTER_RANK, 512 * len(pairs))
    ins = [(a, None) for pair in pairs for a in pair]
    kernel = functools.partial(slices_kernel, len(pairs))
    return call(kernel, 1, at, ins, [(shape, bf16, None)], [], name)[0]


def shards(
    tokens,
    cotangent,
    attention_norm_scale,
    attention_norm_bias,
    query_projection,
    query_projection_bias,
    keyvalue_projection,
    value_projection_bias,
    attention_output_weight,
    attention_output_bias,
    feedforward_norm_scale,
    feedforward_norm_bias,
    up_projection_weight,
    up_projection_bias,
    down_projection_weight,
    down_projection_bias,
    sequence_adapter,
    query_adapter_input,
    query_adapter_output,
    keyvalue_adapter_input,
    keyvalue_adapter_output,
    output_adapter_input,
    output_adapter_output,
    up_adapter_input,
    up_adapter_output,
    down_adapter_input,
    down_adapter_output,
):
    y, core, zl, zh, x = (lax.axis_index(n) for n in ("y", "core", "zl", "zh", "x"))
    z = zh * 2 + zl
    at = jnp.stack([core, x, zh, y, z]).astype(jnp.int32)
    gain_one, shift_one = attention_norm_scale.astype(f32), attention_norm_bias.astype(f32)
    gain_two, shift_two = feedforward_norm_scale.astype(f32), feedforward_norm_bias.astype(f32)

    cot_all = lax.all_gather(cotangent, ("core", "x"), axis=0, tiled=True)
    cot_all = cot_all.reshape(2, 4, ROWS, MODEL_WIDTH)
    attention_shard, feed_shard = call(
        pack_kernel,
        1,
        at,
        [
            (query_projection, None),
            (keyvalue_projection, None),
            (attention_output_weight, None),
            (up_projection_weight, None),
            (down_projection_weight, None),
        ],
        [((ROWS, 768), bf16, None), ((ROWS, 2048), bf16, None)],
        [],
        "pack",
    )
    attention_shard = turn(attention_shard)
    input_rows = tokens.astype(f32)
    normed = layer_norm(input_rows, gain_one, shift_one).astype(bf16)
    column = jnp.stack(gather_cross(attention_shard, False))
    column, normed = lax.optimization_barrier((column, normed))
    plane = gather_cross(column, True)
    plane, normed_sides = lax.optimization_barrier((plane, gather_sides(normed)))
    normed_places = gather_rest(*normed_sides)
    (w,) = call(
        assemble_kernel,
        1,
        at,
        [(piece, ANY) for piece in plane],
        [((MODEL_WIDTH, 768), bf16, None)],
        [pltpu.SemaphoreType.DMA],
        "assemble",
    )
    feed_shard, w, cot_all = lax.optimization_barrier((feed_shard, w, cot_all))
    feed = lax.all_gather(feed_shard, DP + ("zh",), axis=0, tiled=True)
    feed = feed.reshape(16, 2, ROWS, 2048)

    mine = sequence_adapter[0, 0]
    theirs = other_core(sequence_adapter)[0, 0]
    low = jnp.where(core == 0, mine, theirs)
    high = jnp.where(core == 0, theirs, mine)

    def ordered(stack):
        return jnp.concatenate([pick(stack, low), pick(stack, high)], axis=0)

    def ordered_t(stack):
        return ordered(jnp.swapaxes(stack, 1, 2))

    def padded(*pairs):
        rest = jnp.zeros((RIDE - 32 * len(pairs), pairs[0].shape[1]), bf16)
        return jnp.concatenate([*pairs, rest], axis=0)

    small = jnp.concatenate(
        [
            ordered(query_adapter_output),
            ordered_t(output_adapter_input),
            ordered(up_adapter_output),
            ordered_t(down_adapter_input),
        ],
        axis=1,
    )
    biases = jnp.concatenate(
        [
            query_projection_bias,
            jnp.zeros((256,), bf16),
            up_projection_bias,
            jnp.zeros((1024,), bf16),
        ]
    )
    small = turn(jnp.concatenate([small, biases[None], jnp.zeros((15, 2560), bf16)], axis=0))
    q_bias, u_bias = small[32:33, :256].astype(f32), small[32:33, 512:1536].astype(f32)
    small = padded(small[:32])
    q_out, o_in, u_out, d_in = (
        small[:, :256],
        small[:, 256:512],
        small[:, 512:1536],
        small[:, 1536:],
    )
    q_in = padded(ordered_t(query_adapter_input), ordered_t(keyvalue_adapter_input))
    u_in = padded(ordered_t(up_adapter_input))
    kv_out_pair = ordered(keyvalue_adapter_output)
    kv_out_both = padded(jnp.zeros_like(kv_out_pair), kv_out_pair)
    o_out, d_out = padded(ordered(output_adapter_output)), padded(ordered(down_adapter_output))

    kv_in, kv_out = pick(keyvalue_adapter_input, mine), pick(keyvalue_adapter_output, mine)
    keyval_inner = dot(normed, kv_in).astype(bf16)
    keyval_bias = jnp.concatenate(
        [jnp.zeros((HEAD_WIDTH,), f32), value_projection_bias.astype(f32)]
    )
    keyval = (dot(normed, w[:, 256:512]) + keyval_bias + dot(keyval_inner, kv_out)).astype(bf16)
    keyval = other_half(keyval)
    keyval = jnp.concatenate([keyval, other_core(keyval)], axis=0)
    keyval_places = (keyval, ring_x(keyval, 1), ring_x(keyval, -1), ring_x(keyval, 2))

    place_block = jnp.stack([lax.rem(x + p, 4) for p in PLACES]) // 2
    own = place_block[:, None] <= place_block[None, :]
    bias = jnp.concatenate([own, jnp.broadcast_to(zh == 1, (4, 4))], axis=0)
    bias = jnp.repeat(jnp.where(bias, 0.0, -1e30).astype(f32), ROWS, axis=1)

    group = (2, 4 * ROWS)
    row_scratch = pltpu.VMEM((2, 4 * ROWS, MODEL_WIDTH), bf16)
    w_scratch = pltpu.VMEM((MODEL_WIDTH, 768), bf16)
    inner_one, query, keyval_all, log_total, attended, *out_parts = call(
        attention_kernel,
        2,
        at,
        [
            *flat(normed_places),
            *[(piece, ANY) for piece in keyval_places],
            (w, ANY),
            (q_in, None),
            (q_out, None),
            (kv_out_both, None),
            (o_in, None),
            (q_bias, None),
            (keyval_bias[None], None),
            (bias, None),
        ],
        [
            ((*group, RIDE), bf16, step_block((4 * ROWS, RIDE))),
            ((*group, 256), bf16, step_block((4 * ROWS, 256))),
            ((2, 8, ROWS, 256), bf16, step_block((8, ROWS, 256))),
            ((2, 2, 4 * ROWS), f32, step_block((2, 4 * ROWS))),
            ((*group, 256), bf16, step_block((4 * ROWS, 256))),
            *part_outs(MODEL_WIDTH + RIDE),
        ],
        [row_scratch, pltpu.VMEM((2, 4, ROWS, 256), bf16), w_scratch, dma(3)],
        "attention",
        9000000000,
    )
    out_sum = scatter_row(*out_parts)
    output_inner = out_sum[:, MODEL_WIDTH:].astype(bf16)
    middle = (
        input_rows
        + out_sum[:, :MODEL_WIDTH]
        + attention_output_bias.astype(f32)
        + dot(output_inner, o_out)
    )
    normed_two = layer_norm(middle, gain_two, shift_two).astype(bf16)
    place_scratch = pltpu.VMEM((4, 2 * ROWS, MODEL_WIDTH), bf16)
    feed_scratch = pltpu.VMEM((16, ROWS, 1024), bf16)
    inner_two, pre, act, *down_parts = call(
        feed_kernel,
        4,
        at,
        [
            *flat(gather_row(normed_two)),
            (feed, ANY),
            (u_in, None),
            (u_out, None),
            (d_in, None),
            (u_bias, None),
        ],
        [
            ((4, 2 * ROWS, RIDE), bf16, step_block((2 * ROWS, RIDE))),
            ((4, 2 * ROWS, 1024), f32, step_block((2 * ROWS, 1024))),
            ((4, 2 * ROWS, 1024), bf16, step_block((2 * ROWS, 1024))),
            *part_outs(MODEL_WIDTH + RIDE, True),
        ],
        [place_scratch, feed_scratch, feed_scratch, dma(6)],
        "feed",
        9500000000,
    )
    down_low = scatter_start(*down_parts)
    down_low, act = lax.optimization_barrier((down_low, act))
    down_moved = (ring_x(down_low[1], -1), ring_x(down_low[2], 1), ring_x(down_low[3], 2))

    up_b, down_a, *up_parts = call(
        feed_back_kernel,
        4,
        at,
        [
            (cot_all, ANY),
            (feed, ANY),
            (pre, step_block((2 * ROWS, 1024))),
            (act, step_block((2 * ROWS, 1024))),
            (inner_two, step_block((2 * ROWS, RIDE))),
            (d_out, None),
            (d_in, None),
            (u_out, None),
        ],
        [((32, 1024), f32, None), ((32, 1024), f32, None), *part_outs(MODEL_WIDTH + RIDE, True)],
        [place_scratch, feed_scratch, feed_scratch, dma(6)],
        "feed_back",
        9500000000,
    )
    up_parts, down_moved = lax.optimization_barrier((up_parts, down_moved))
    down_sum = down_low[0] + sum(part.astype(f32) for part in down_moved)
    up_sum = scatter_row(*up_parts)
    up_back = up_sum[:, MODEL_WIDTH:].astype(bf16)
    grad_normed_two = up_sum[:, :MODEL_WIDTH] + dot(up_back, u_in)
    _, norm_two_back = jax.vjp(lambda v: layer_norm(v, gain_two, shift_two), middle)
    grad_middle = cotangent.astype(f32) + norm_two_back(grad_normed_two)[0]
    grad_branch = grad_middle.astype(bf16)

    down_inner = down_sum[:, MODEL_WIDTH:].astype(bf16)
    layer_output = (
        middle
        + down_sum[:, :MODEL_WIDTH]
        + down_projection_bias.astype(f32)
        + dot(down_inner, d_out)
    ).astype(bf16)

    branch_all = lax.all_gather(grad_branch, ("core", "x"), axis=0, tiled=True)
    branch_all = branch_all.reshape(2, 4, ROWS, MODEL_WIDTH)
    feed_set = jnp.concatenate(
        [
            row_slice(up_b, core),
            row_slice(down_a, core),
            scatter_sequence(
                slices_of(
                    at,
                    [(up_back, normed_two), (output_inner, grad_branch), (down_inner, cotangent)],
                    "slices",
                )
            ),
            jnp.full((16, RIDE), mine, jnp.int32).astype(bf16),
        ],
        axis=-1,
    )
    feed_all = lax.all_gather(feed_set, DP + ("zh",), axis=0)
    query_b, output_a, *query_parts = call(
        attention_back_kernel,
        2,
        at,
        [
            (branch_all, ANY),
            (w, ANY),
            (inner_one, step_block((4 * ROWS, RIDE))),
            (query, step_block((4 * ROWS, 256))),
            (keyval_all, step_block((8, ROWS, 256))),
            (log_total, step_block((2, 4 * ROWS))),
            (attended, step_block((4 * ROWS, 256))),
            (o_out, None),
            (o_in, None),
            (q_out, None),
            (bias, None),
        ],
        [((32, 256), f32, None), ((32, 256), f32, None), *part_outs(2688)],
        [
            row_scratch,
            w_scratch,
            pltpu.VMEM((8 * ROWS, HEAD_WIDTH), f32),
            pltpu.VMEM((8 * ROWS, HEAD_WIDTH), f32),
            dma(2),
        ],
        "attention_back",
        8000000000,
    )
    query_sum = scatter_row(*query_parts)
    grad_keyval = (
        query_sum[:, 2048:2304] + other_half(query_sum[:, 2304:2560].astype(bf16)).astype(f32)
    ).astype(bf16)
    query_back = query_sum[:, 2560:].astype(bf16)
    keyval_back = dot_t(grad_keyval, kv_out).astype(bf16)
    keyval_ride = jnp.pad(keyval_back, ((0, 0), (0, RIDE - 16)))
    grad_normed = (
        query_sum[:, :MODEL_WIDTH]
        + dot(query_back, q_in)
        + dot_t(grad_keyval, w[:, 256:512])
        + dot_t(keyval_back, kv_in)
    )
    _, norm_one_back = jax.vjp(lambda v: layer_norm(v, gain_one, shift_one), input_rows)
    grad_tokens = (grad_middle + norm_one_back(grad_normed)[0]).astype(bf16)

    late_set = jnp.concatenate(
        [
            scatter_sequence(
                jnp.concatenate(
                    [
                        slices_of(
                            at,
                            [(query_back, normed), (keyval_ride, normed)],
                            "late_slices",
                        ),
                        jnp.pad(
                            rolled(
                                tdot(keyval_inner, grad_keyval)
                                .astype(bf16)
                                .reshape(16, 4, 64)
                                .transpose(1, 0, 2),
                                x,
                            ),
                            ((0, 0), (0, 0), (0, 64)),
                        ),
                    ],
                    axis=-1,
                )
            ),
            row_slice(query_b, core),
            row_slice(output_a, core),
        ],
        axis=-1,
    )
    column = jnp.stack(
        [late_set, ring_y(late_set, -1), ring_y(late_set, 2), ring_y(late_set, 1)]
    )
    feed_all, column = lax.optimization_barrier((feed_all, column))
    all_ids = feed_all[:, 0, 5632].astype(jnp.int32)
    feed_sum = sum_by_adapter([feed_all], 4 * core, all_ids, 4)
    feed_sum = lax.all_gather(feed_sum, ("core", "x"), axis=0).reshape(2, 4, 4, 16, 5760)
    late_pieces = [column, ring_z(column, -1), ring_z(column, 2), ring_z(column, 1)]
    plane_ids = all_ids.reshape(4, 2, 2, 2)
    plane_ids = jnp.where(core == 0, plane_ids[:, :, 0], plane_ids[:, :, 1])
    plane_ids = rolled(jnp.swapaxes(plane_ids, 1, 2).reshape(4, 4), y)
    plane_ids = rolled(plane_ids.T, z)
    late_sum = sum_by_adapter(late_pieces, 0, plane_ids.reshape(16), ADAPTER_COUNT)
    kept = jnp.where(core == 0, late_sum[:4], late_sum[4:])
    sent = jnp.where(core == 0, late_sum[4:], late_sum[:4])
    own_half = (kept.astype(f32) + other_core(sent).astype(f32)).astype(bf16)
    other_part = other_core(own_half)
    near = ring_by_core(jnp.concatenate([own_half, other_part], axis=0))
    far = ring_x(own_half, 2)
    query_a, keyval_a, keyval_b, query_b, output_a = spread_out(
        late_spread_kernel,
        at,
        [own_half, other_part, near, other_core(near), far, other_core(far)],
        (256, 256, 64, 256, 256),
        "late_spread",
    )
    keyval_b = keyval_b.reshape(8, 16, 4, 128)[..., :64].reshape(8, 16, 256)
    up_b, down_a, up_a, output_b, down_b = spread_out(
        feed_spread_kernel, at, [feed_sum], (1024, 1024, 256, 256, 256), "feed_spread"
    )

    def side_in(a):
        return jnp.swapaxes(a, 1, 2)

    return (
        layer_output,
        grad_tokens,
        side_in(query_a),
        query_b,
        side_in(keyval_a),
        keyval_b,
        side_in(output_a),
        output_b,
        side_in(up_a),
        up_b,
        side_in(down_a),
        down_b,
    )

def solution(mesh):
    fine = Mesh(mesh.devices.reshape(SIZES), AXES)
    in_specs = (
        P(AXES, None),
        P(AXES, None),
        P(),
        P(),
        P(DP, MP),
        P(MP),
        P(DP, None),
        P(),
        P(MP, DP),
        P(),
        P(),
        P(),
        P(DP, MP),
        P(MP),
        P(MP, DP),
        P(),
        P(DP, None),
        P(),
        P(None, None, MP),
        P(),
        P(),
        P(None, MP, None),
        P(),
        P(),
        P(None, None, MP),
        P(None, MP, None),
        P(),
    )
    out_specs = (P(AXES, None), P(AXES, None)) + (P(),) * 10
    return jax.shard_map(shards, mesh=fine, in_specs=in_specs, out_specs=out_specs, check_vma=False)
```

```python
import functools
import math

import jax
import jax.numpy as jnp
from jax import lax
from jax.experimental import pallas as pl
from jax.experimental.pallas import tpu as pltpu
from jax.sharding import Mesh
from jax.sharding import PartitionSpec as P

MODEL_WIDTH = 2048
H = 16
HEAD_WIDTH = 128
FEED_HIDDEN = 8192
ADAPTER_RANK = 16
ADAPTER_COUNT = 8
BLOCK = 256

AXES = ("y", "zl", "core", "zh", "x")
SIZES = (4, 2, 2, 2, 4)
DP = ("y", "zl", "core")
MP = ("zh", "x")
PLACES = (0, 3, 1, 2)
Z_RING = (0, 2, 1, 3)
ROWS = 128
RIDE = 128

f32 = jnp.float32
bf16 = jnp.bfloat16


together = lax.optimization_barrier


def ring_x(a, step):
    return lax.ppermute(a, "x", [(i, (i + step) % 4) for i in range(4)])


def ring_y(a, step):
    return lax.ppermute(a, "y", [(i, (i + step) % 4) for i in range(4)])


def ring_z(a, step):
    return lax.ppermute(a, ("zl", "zh"), [(Z_RING[i], Z_RING[(i + step) % 4]) for i in range(4)])


def other_core(a):
    return lax.ppermute(a, "core", [(0, 1), (1, 0)])


def other_half(a):
    return lax.ppermute(a, "zh", [(0, 1), (1, 0)])


def turn(a):
    return lax.ppermute(a, ("core", "zh"), [(0, 0), (1, 2), (2, 1), (3, 3)])


def plane_pairs(step, swapped):
    def index(y, z, core):
        return ((y * 2 + z % 2) * 2 + core) * 2 + z // 2

    pairs = []
    for y in range(4):
        for z in range(4):
            for core in range(2):
                if (core == 0) != swapped:
                    to = index((y + step) % 4, z, core)
                else:
                    to = index(y, (z + step) % 4, core)
                pairs.append((index(y, z, core), to))
    return pairs


def gather_cross(a, swapped):
    return [a] + [
        lax.ppermute(a, ("y", "zl", "core", "zh"), plane_pairs(-step, swapped))
        for step in (1, 2, 3)
    ]


def gather_sides(a):
    return a, other_core(a), ring_x(a, 1), ring_x(a, -1)


def gather_rest(a, near, left, right):
    half = a.shape[0] // 2
    top, bottom = ring_x(left[:half], 1), ring_x(right[half:], -1)
    return (
        (a, near),
        (left, other_core(left)),
        (right, other_core(right)),
        (top, bottom, other_core(top), other_core(bottom)),
    )


def gather_row(a):
    return gather_rest(*gather_sides(a))


def add_cores(mine, theirs):
    return mine.astype(f32) + other_core(theirs).astype(f32)


def scatter_far(far_mine, far_theirs):
    return add_cores(far_mine, far_theirs).astype(bf16)


def scatter_sides(far):
    half = far.shape[0] // 2
    return ring_x(far[:half], 1), ring_x(far[half:], -1)


def scatter_joined(near, up, down):
    half = up.shape[0]
    right = jnp.concatenate([near[2, :half] + up.astype(f32), near[2, half:]]).astype(bf16)
    left = jnp.concatenate([near[1, :half], near[1, half:] + down.astype(f32)]).astype(bf16)
    return right, left


def scatter_last(near, up, down):
    right, left = scatter_joined(near, up, down)
    return near[0] + ring_x(right, 1).astype(f32) + ring_x(left, -1).astype(f32)


def scatter_row(mine, theirs, far_mine, far_theirs):
    up, down = scatter_sides(scatter_far(far_mine, far_theirs))
    return scatter_last(add_cores(mine, theirs), up, down)


def scatter_start(mine, theirs, far_mine, far_theirs):
    far = add_cores(far_mine, far_theirs).astype(bf16)
    near = add_cores(mine, theirs)
    return near[0], near[1].astype(bf16), near[2].astype(bf16), far


def gather_y(a):
    return [a, ring_y(a, -1), ring_y(a, 2), ring_y(a, 1)]


def gather_z(a):
    return [a, ring_z(a, -1), ring_z(a, 2), ring_z(a, 1)]


def halves_of(sums, core):
    return jnp.where(core == 0, sums[:4], sums[4:]), jnp.where(core == 0, sums[4:], sums[:4])


def ring_by_core(a):
    pairs = [(i, (i + 1) % 4) for i in range(4)] + [(4 + i, 4 + (i + 3) % 4) for i in range(4)]
    return lax.ppermute(a, ("core", "x"), pairs)


def by_core(core, own, other):
    return jnp.where(
        core == 0, jnp.concatenate([own, other], -1), jnp.concatenate([other, own], -1)
    )


def row_slice(pair, core, widths):
    own = jnp.where(core == 0, pair[:16], pair[16:]).astype(bf16)
    other = other_core(jnp.where(core == 0, pair[16:], pair[:16]).astype(bf16))
    ends = [sum(widths[:k]) for k in range(1, len(widths))]
    pieces = zip(jnp.split(own, ends, axis=1), jnp.split(other, ends, axis=1))
    return jnp.concatenate([by_core(core, a, b) for a, b in pieces], axis=1)


def scatter_sequence(slices):
    return slices[0], ring_x(slices[1], 1), ring_x(slices[3], -1), ring_x(slices[2], 2)


def total(parts):
    return sum(part.astype(f32) for part in parts).astype(bf16)


def layer_norm(values, gain, shift):
    mean_value = jnp.mean(values, axis=-1, keepdims=True)
    centred = values - mean_value
    variance = jnp.mean(centred * centred, axis=-1, keepdims=True)
    return centred * lax.rsqrt(variance + 1e-05) * gain + shift


def gelu_tanh(values):
    inner_product = math.sqrt(2.0 / math.pi) * (values + 0.044715 * values * values * values)
    return 0.5 * values * (1.0 + jnp.tanh(inner_product))


def pick(adapter_stack, position):
    return lax.dynamic_index_in_dim(adapter_stack, position, 0, keepdims=False)


def dot(left, right):
    return jnp.dot(left, right, preferred_element_type=f32)


def dot_t(left, right):
    return lax.dot_general(left, right, (((1,), (1,)), ((), ())), preferred_element_type=f32)


def tdot(left, right):
    return lax.dot_general(left, right, (((0,), (0,)), ((), ())), preferred_element_type=f32)


def lane_owner(rows, row_core):
    lane = lax.broadcasted_iota(jnp.int32, (rows, RIDE), 1)
    owner = lax.rem(lane // ADAPTER_RANK, 2)
    return jnp.logical_and(owner == row_core, lane < 4 * ADAPTER_RANK)


def place_mask(core):
    row = lax.broadcasted_iota(jnp.int32, (2 * ROWS, RIDE), 0)
    return lane_owner(2 * ROWS, jnp.where(row < ROWS, core, 1 - core))


def copy(source, target, sem):
    pltpu.make_async_copy(source, target, sem).start()


def wait(target, sem):
    pltpu.make_async_copy(target, target, sem).wait()


def copy_place(pieces, target_mine, target_theirs, sem):
    half = ROWS // 2
    if len(pieces) == 2:
        copy(pieces[0], target_mine, sem)
        copy(pieces[1], target_theirs, sem)
    else:
        copy(pieces[0], target_mine.at[pl.ds(0, half)], sem)
        copy(pieces[1], target_mine.at[pl.ds(half, half)], sem)
        copy(pieces[2], target_theirs.at[pl.ds(0, half)], sem)
        copy(pieces[3], target_theirs.at[pl.ds(half, half)], sem)


def split_pieces(refs):
    return (refs[0:2], refs[2:4], refs[4:6], refs[6:10])


def copy_row(gathered, at, target_of, sem_of):
    core, x = at[0], at[1]
    for p in range(4):
        there = lax.rem(x + PLACES[p], 4)
        copy(gathered.at[core, there], target_of(p, 0), sem_of(p))
        copy(gathered.at[1 - core, there], target_of(p, 1), sem_of(p))


def assemble_kernel(at, *refs):
    pieces, (out, sem) = refs[:4], refs[4:]
    core, y, z = at[0], at[3], at[4]
    for far, piece in enumerate(pieces):
        for near in range(4):
            to_y = lax.rem(y + jnp.where(core == 0, near, far), 4)
            to_z = lax.rem(z + jnp.where(core == 0, far, near), 4)
            shard = (to_y * 2 + lax.rem(to_z, 2)) * 2 + to_z // 2
            copy(piece.at[near], out.at[pl.ds(pl.multiple_of(shard * ROWS, ROWS), ROWS)], sem)
    wait(out, sem)


def pack_kernel(at, query, keyval, output, up, down, attention_out, feed_out):
    attention_out[:, :256] = query[...]
    attention_out[:, 256:512] = keyval[...]
    attention_out[:, 512:] = output[...].astype(f32).T.astype(bf16)
    feed_out[:, :1024] = up[...]
    feed_out[:, 1024:] = down[...].astype(f32).T.astype(bf16)


def sum_kernel(ids, *refs):
    pieces, (out, total) = refs[:-2], refs[-2:]
    total[...] = jnp.zeros_like(total)
    row = 0
    for piece in pieces:
        for k in range(piece.shape[0]):
            total[ids[row]] += piece[k].astype(f32)
            row += 1
    out[...] = total[...].astype(bf16)


def slices_kernel(count, at, *refs):
    ins, out = refs[: 2 * count], refs[2 * count]
    x = at[1]
    for n in range(count):
        back, rows = ins[2 * n], ins[2 * n + 1]
        turned = back[...].astype(f32).T
        turned = (turned[:16] + turned[16:32]).astype(bf16)
        product = dot(turned, rows[...]).astype(bf16)
        for to in range(4):
            place = lax.rem(to + 4 - x, 4)
            for c in range(2):
                first = (c * 4 + to) * 256
                lanes = slice(n * 512 + c * 256, n * 512 + (c + 1) * 256)
                out[place, :, lanes] = product[:, first : first + 256]


def spread(scratch, outs, widths):
    x, c = pl.program_id(0), pl.program_id(1)
    first = 0
    for out, width in zip(outs, widths):
        if width < 128:
            out[...] = scratch[x, :, :, first : first + 128].astype(f32)
            first += 128
        else:
            here = pl.ds(pl.multiple_of(first + c * width, 128), width)
            out[...] = scratch[x, :, :, here].astype(f32)
            first += 2 * width


def feed_spread_kernel(widths, at, *refs):
    gathered, (scratch, sem) = refs[0], refs[-2:]

    @pl.when((pl.program_id(0) == 0) & (pl.program_id(1) == 0))
    def _():
        for c in range(2):
            for x in range(4):
                copy(gathered.at[c, x], scratch.at[x, pl.ds(4 * c, 4)], sem)
        wait(scratch, sem)

    spread(scratch, refs[1:-2], widths)


def late_spread_kernel(widths, at, *refs):
    own, other, near, near_other, far, far_other = refs[:6]
    scratch, sem = refs[-2:]
    core, x = at[0], at[1]

    @pl.when((pl.program_id(0) == 0) & (pl.program_id(1) == 0))
    def _():
        mine, theirs = pl.ds(4 * core, 4), pl.ds(4 * (1 - core), 4)
        side = lax.rem(x + jnp.where(core == 0, 3, 1), 4)
        other_side = lax.rem(x + jnp.where(core == 0, 1, 3), 4)
        across = lax.rem(x + 2, 4)
        copy(own, scratch.at[x, mine], sem)
        copy(other, scratch.at[x, theirs], sem)
        for part, where in ((0, mine), (1, theirs)):
            copy(near.at[pl.ds(4 * part, 4)], scratch.at[side, where], sem)
        for part, where in ((0, theirs), (1, mine)):
            copy(near_other.at[pl.ds(4 * part, 4)], scratch.at[other_side, where], sem)
        copy(far, scratch.at[across, mine], sem)
        copy(far_other, scratch.at[across, theirs], sem)
        wait(scratch, sem)

    spread(scratch, refs[6:-2], widths)


def copy_rows(rows_in, rows, sems):
    half = ROWS // 2
    for s in range(2):
        for p in range(4):
            pieces = rows_in[p]
            if len(pieces) == 2:
                copy(pieces[s], rows.at[s, pl.ds(p * ROWS, ROWS)], sems.at[s])
            else:
                for n in range(2):
                    here = pl.ds(p * ROWS + n * half, half)
                    copy(pieces[2 * s + n], rows.at[s, here], sems.at[s])


def attention_kernel(at, *refs):
    rows_in = split_pieces(refs[:10])
    kv_in = refs[10:14]
    w, q_in, q_out, kv_out, o_in, q_bias, kv_bias, bias = refs[14:22]
    inner_out, inner_far, query_out, kv_all, lse_out, att_out = refs[22:28]
    parts, far_parts = refs[28:30], refs[30:32]
    rows, kvs, ws, sems = refs[32:]
    s = pl.program_id(0)
    core = at[0]

    @pl.when(s == 0)
    def _():
        copy(w, ws, sems.at[2])
        copy_rows(rows_in, rows, sems)
        for p in range(4):
            for q in range(2):
                copy(kv_in[p].at[pl.ds(q * ROWS, ROWS)], kvs.at[q, p], sems.at[3])
        wait(ws, sems.at[2])
        wait(kvs, sems.at[3])

    wait(rows.at[s], sems.at[s])

    owner = lane_owner(4 * ROWS, jnp.where(s == 0, core, 1 - core))
    x = rows[s]
    inner = jnp.where(owner, dot_t(x, q_in[...]), 0.0).astype(bf16)
    inner_out[0] = inner
    query = (dot(x, ws[:, :256]) + q_bias[...] + dot(inner, q_out[...])).astype(bf16)
    query_out[0] = query
    kv_own = (dot(x, ws[:, 256:512]) + kv_bias[...] + dot(inner, kv_out[...])).astype(bf16)
    inner_far[0] = kvs[s, :, :, 256:].reshape(4 * ROWS, RIDE)
    kv = jnp.concatenate([kv_own.reshape(4, ROWS, 256), kvs[s, :, :, :256]], axis=0)
    kv_all[0] = kv
    keys = kv[:, :, :HEAD_WIDTH].reshape(8 * ROWS, HEAD_WIDTH)
    values_t = kv[:, :, HEAD_WIDTH:].reshape(8 * ROWS, HEAD_WIDTH).astype(f32).T.astype(bf16)
    columns = []
    for h in range(2):
        chunks = []
        for c in range(2):
            lanes = slice(c * 256, c * 256 + 256)
            q = query[lanes, h * HEAD_WIDTH : (h + 1) * HEAD_WIDTH]
            scores = dot_t(keys, q) * (HEAD_WIDTH**-0.5)
            scores = scores.reshape(8, ROWS, 256) + bias[:, lanes][:, None, :]
            scores = scores.reshape(8 * ROWS, 256)
            top = jnp.max(scores, axis=0, keepdims=True)
            expo = jnp.exp(scores - top)
            total = jnp.sum(expo, axis=0, keepdims=True)
            probs = (expo * (1.0 / total)).astype(bf16)
            lse_out[0, h : h + 1, lanes] = top + jnp.log(total)
            chunks.append(dot(values_t, probs).T)
        columns.append(jnp.concatenate(chunks, axis=0))
    attended = jnp.concatenate(columns, axis=1).astype(bf16)
    att_out[0] = attended
    low = jnp.where(owner, dot_t(attended, o_in[...]), 0.0).astype(bf16)
    for which in range(2):

        @pl.when(s == which)
        def _(which=which):
            for p in range(4):
                here = slice(p * ROWS, (p + 1) * ROWS)
                part = parts[which].at[p] if p < 3 else far_parts[which]
                part[:, :MODEL_WIDTH] = dot_t(attended[here], ws[:, 512:]).astype(bf16)
                part[:, MODEL_WIDTH:] = low[here]


def store_parts(p, parts, far_parts, out, low):
    for which in range(2):
        here = slice(which * ROWS, (which + 1) * ROWS)

        @pl.when(p < 3)
        def _(which=which, here=here):
            parts[which][0, :, :MODEL_WIDTH] = out[here]
            parts[which][0, :, MODEL_WIDTH:] = low[here]

        @pl.when(p == 3)
        def _(which=which, here=here):
            far_parts[which][:, :MODEL_WIDTH] = out[here]
            far_parts[which][:, MODEL_WIDTH:] = low[here]


def feed_kernel(at, *refs):
    rows_in = split_pieces(refs[:10])
    feed, u_in, u_out, d_in, u_bias = refs[10:15]
    inner_out, pre_out, act_out = refs[15:18]
    parts, far_parts = refs[18:20], refs[20:22]
    rows, up, down, sems = refs[22:]
    p = pl.program_id(0)
    core = at[0]

    @pl.when(p == 0)
    def _():
        copy(feed.at[:, core, :, pl.ds(0, 1024)], up, sems.at[4])
        for k in range(4):
            copy_place(
                rows_in[k], rows.at[k, pl.ds(0, ROWS)], rows.at[k, pl.ds(ROWS, ROWS)], sems.at[k]
            )
        copy(feed.at[:, core, :, pl.ds(1024, 1024)], down, sems.at[5])
        wait(up, sems.at[4])

    wait(rows.at[p], sems.at[p])
    mask = place_mask(core)
    x = rows[p]
    inner = jnp.where(mask, dot_t(x, u_in[...]), 0.0).astype(bf16)
    inner_out[0] = inner
    pre = dot(x, up[...].reshape(MODEL_WIDTH, 1024)) + u_bias[...] + dot(inner, u_out[...])
    pre_out[0] = pre
    act = gelu_tanh(pre).astype(bf16)
    act_out[0] = act

    @pl.when(p == 0)
    def _():
        wait(down, sems.at[5])

    low = jnp.where(mask, dot_t(act, d_in[...]), 0.0).astype(bf16)
    out = dot_t(act, down[...].reshape(MODEL_WIDTH, 1024)).astype(bf16)
    store_parts(p, parts, far_parts, out, low)


def feed_back_kernel(at, *refs):
    cot, feed, pre_in, act_in, inner_in, d_in, u_out = refs[:7]
    up_b, down_a = refs[7:9]
    parts, far_parts = refs[9:11], refs[11:13]
    rows, up, down, sems = refs[13:]
    p = pl.program_id(0)
    core = at[0]

    @pl.when(p == 0)
    def _():
        copy(feed.at[:, core, :, pl.ds(1024, 1024)], down, sems.at[5])
        copy_row(
            cot, at, lambda k, which: rows.at[k, pl.ds(which * ROWS, ROWS)], lambda k: sems.at[k]
        )
        copy(feed.at[:, core, :, pl.ds(0, 1024)], up, sems.at[4])
        up_b[...] = jnp.zeros_like(up_b)
        down_a[...] = jnp.zeros_like(down_a)
        wait(down, sems.at[5])

    wait(rows.at[p], sems.at[p])
    mask = place_mask(core)
    grad, back = rows[p, :, :MODEL_WIDTH], rows[p, :, MODEL_WIDTH:]
    back_t = back.astype(f32).T[:32].astype(bf16)
    act = act_in[0]
    down_a[...] += dot(back_t, act)
    grad_act = dot(grad, down[...].reshape(MODEL_WIDTH, 1024)) + dot(back, d_in[...])
    pre = pre_in[0]
    k0 = math.sqrt(2.0 / math.pi)
    square = pre * pre
    bend = jnp.tanh(k0 * (pre + 0.044715 * square * pre))
    slope = 0.5 * (1.0 + bend) + 0.5 * pre * (1.0 - bend * bend) * (
        k0 * (1.0 + 3.0 * 0.044715 * square)
    )
    grad_pre = (grad_act * slope).astype(bf16)
    inner_t = inner_in[0].astype(f32).T[:32].astype(bf16)
    up_b[...] += dot(inner_t, grad_pre)
    low = jnp.where(mask, dot_t(grad_pre, u_out[...]), 0.0).astype(bf16)

    @pl.when(p == 0)
    def _():
        wait(up, sems.at[4])

    out = dot_t(grad_pre, up[...].reshape(MODEL_WIDTH, 1024)).astype(bf16)
    store_parts(p, parts, far_parts, out, low)


def late_kernel(at, *refs):
    rows_in = split_pieces(refs[:10])
    backs, backs_far, keyval_b = refs[10:13]
    outs, (rows, sems) = refs[13:15], refs[15:]
    core, x = at[0], at[1]
    copy_rows(rows_in, rows, sems)
    product = jnp.zeros((64, MODEL_WIDTH), f32)
    for s in range(2):
        wait(rows.at[s], sems.at[s])
        back = backs[s].astype(f32).T
        back = jnp.concatenate([back[:32], back[32:64] + backs_far[s].astype(f32)], axis=0)
        product += dot(back.astype(bf16), rows[s])
    first, second = keyval_b[:16], keyval_b[16:]
    lane = lax.broadcasted_iota(jnp.int32, (ADAPTER_RANK, RIDE), 1) // 64
    for which in range(2):
        out = outs[which]
        is_first = (core == 0) if which == 0 else (core != 0)
        for n in range(2):
            both = product[32 * n : 32 * n + 32]
            picked = jnp.where(is_first, both[:16], both[16:]).astype(bf16)
            for to in range(4):
                place = lax.rem(to + 4 - x, 4)
                for c in range(2):
                    begin = (c * 4 + to) * 256
                    lanes = slice(n * 512 + c * 256, n * 512 + (c + 1) * 256)
                    out[place, :, lanes] = picked[:, begin : begin + 256]
        picked = jnp.where(is_first, first, second).astype(bf16)
        for to in range(4):
            place = lax.rem(to + 4 - x, 4)
            part = picked[:, (to // 2) * 128 : (to // 2) * 128 + 128]
            out[place, :, 1024:1152] = jnp.where(lane == to % 2, part, jnp.zeros_like(part))


def attention_back_kernel(at, *refs):
    rows_in = split_pieces(refs[:10])
    w, inner_in, inner_far, query_in, kv_in, lse_in, att_in = refs[10:17]
    o_out, o_in, q_out, kv_out, bias = refs[17:22]
    query_b, output_a, keyval_b, backs, backs_far = refs[22:27]
    parts, far_parts = refs[27:29], refs[29:31]
    rows, ws, grad_k, grad_v, sems = refs[31:]
    s = pl.program_id(0)
    core = at[0]

    @pl.when(s == 0)
    def _():
        copy(w, ws, sems.at[2])
        copy_rows(rows_in, rows, sems)
        query_b[...] = jnp.zeros_like(query_b)
        output_a[...] = jnp.zeros_like(output_a)
        keyval_b[...] = jnp.zeros_like(keyval_b)
        wait(ws, sems.at[2])

    wait(rows.at[s], sems.at[s])

    owner = lane_owner(4 * ROWS, jnp.where(s == 0, core, 1 - core))
    scale = HEAD_WIDTH**-0.5
    x = rows[s]
    back = jnp.where(owner, dot_t(x, o_out[...]), 0.0)
    output_a[...] += dot(back.T[:32].astype(bf16), att_in[0])
    grad_att = (dot(x, ws[:, 512:]) + dot(back.astype(bf16), o_in[...])).astype(bf16)
    query = query_in[0]
    kv = kv_in[0]
    keys = kv[:, :, :HEAD_WIDTH].reshape(8 * ROWS, HEAD_WIDTH)
    values = kv[:, :, HEAD_WIDTH:].reshape(8 * ROWS, HEAD_WIDTH)
    keys_t = keys.astype(f32).T.astype(bf16)
    columns = []
    for h in range(2):
        chunks = []
        for c in range(2):
            lanes = slice(c * 256, c * 256 + 256)
            head = slice(h * HEAD_WIDTH, (h + 1) * HEAD_WIDTH)
            q, g = query[lanes, head], grad_att[lanes, head]
            scores = dot_t(keys, q) * scale
            scores = scores.reshape(8, ROWS, 256) + bias[:, lanes][:, None, :]
            probs = jnp.exp(scores.reshape(8 * ROWS, 256) - lse_in[0, h : h + 1, lanes])
            grad_probs = dot_t(values, g)
            delta = jnp.sum(probs * grad_probs, axis=0, keepdims=True)
            grad_scores = (probs * (grad_probs - delta)).astype(bf16)
            chunks.append((dot(keys_t, grad_scores) * scale).T)
            more_k = dot(grad_scores, q) * scale
            more_v = dot(probs.astype(bf16), g)
            if h == 0 and c == 0:
                grad_k[...] = more_k
                grad_v[...] = more_v
            else:
                grad_k[...] += more_k
                grad_v[...] += more_v
        columns.append(jnp.concatenate(chunks, axis=0))
    grad_query = jnp.concatenate(columns, axis=1).astype(bf16)
    inner_t = inner_in[0].astype(f32).T
    query_b[...] += dot(inner_t[:32].astype(bf16), grad_query)
    low = jnp.where(owner, dot_t(grad_query, q_out[...]), 0.0).astype(bf16)
    grad_kv = jnp.concatenate([grad_k[...], grad_v[...]], axis=1).astype(bf16)
    own_kv, far_kv = grad_kv[: 4 * ROWS], grad_kv[4 * ROWS :]
    keyval_b[...] += dot(inner_t[32:64].astype(bf16), own_kv)
    keyval_b[...] += dot(inner_far[0].astype(f32).T[32:64].astype(bf16), far_kv)
    backs[0] = low + jnp.where(owner, dot_t(own_kv, kv_out[...]), 0.0).astype(bf16)
    backs_far[0] = jnp.where(owner, dot_t(far_kv, kv_out[...]), 0.0).T[32:64].astype(bf16)
    for which in range(2):

        @pl.when(s == which)
        def _(which=which):
            for p in range(4):
                here = slice(p * ROWS, (p + 1) * ROWS)
                part = parts[which].at[p] if p < 3 else far_parts[which]
                part[:, :2048] = dot_t(grad_query[here], ws[:, :256]).astype(bf16)
                part[:, 2048:2304] = own_kv[here]
                part[:, 2304:2560] = far_kv[here]
                part[:, 2560:] = low[here]


VMEM_LIMIT = 56 * 1024 * 1024
ANY = pl.BlockSpec(memory_space=pl.ANY)


def whole_block(shape):
    return pl.BlockSpec(shape, lambda i, at: (0,) * len(shape))


def step_block(shape):
    return pl.BlockSpec((1, *shape), lambda i, at: (i,) + (0,) * len(shape))


def call(kernel, steps, at, ins, outs, scratch, name, flops=0):
    arrays = [a for a, _ in ins]
    in_specs = [whole_block(a.shape) if b is None else b for a, b in ins]
    out_specs = [whole_block(s) if b is None else b for s, _, b in outs]
    return pl.pallas_call(
        kernel,
        out_shape=[jax.ShapeDtypeStruct(s, d) for s, d, _ in outs],
        grid_spec=pltpu.PrefetchScalarGridSpec(
            num_scalar_prefetch=1,
            grid=(steps,),
            in_specs=in_specs,
            out_specs=out_specs,
            scratch_shapes=scratch,
        ),
        compiler_params=pltpu.CompilerParams(vmem_limit_bytes=VMEM_LIMIT),
        cost_estimate=pl.CostEstimate(
            flops=flops,
            bytes_accessed=sum(a.size * a.dtype.itemsize for a in arrays)
            + sum(math.prod(s) * 4 for s, _, _ in outs),
            transcendentals=0,
        ),
        name=name,
    )(at, *arrays)


def flat(places):
    return [(piece, ANY) for place in places for piece in place]


def part_outs(width, steps=False):
    block = pl.BlockSpec((1, ROWS, width), lambda i, at: (jnp.minimum(i, 2), 0, 0))
    near = ((3, ROWS, width), bf16, block if steps else None)
    return [near, near, ((ROWS, width), bf16, None), ((ROWS, width), bf16, None)]


def dma(n):
    return pltpu.SemaphoreType.DMA((n,))


def sum_by_adapter(pieces, ids):
    width, count = pieces[0].shape[-1], ADAPTER_COUNT
    block = max(w for w in range(128, 3713, 128) if width % w == 0)
    return pl.pallas_call(
        sum_kernel,
        out_shape=jax.ShapeDtypeStruct((count, ADAPTER_RANK, width), bf16),
        grid_spec=pltpu.PrefetchScalarGridSpec(
            num_scalar_prefetch=1,
            grid=(width // block,),
            in_specs=[
                pl.BlockSpec((p.shape[0], ADAPTER_RANK, block), lambda i, at: (0, 0, i))
                for p in pieces
            ],
            out_specs=pl.BlockSpec((count, ADAPTER_RANK, block), lambda i, at: (0, 0, i)),
            scratch_shapes=[pltpu.VMEM((count, ADAPTER_RANK, block), f32)],
        ),
        compiler_params=pltpu.CompilerParams(vmem_limit_bytes=VMEM_LIMIT),
        name="sum_by_adapter",
    )(ids, *pieces)


def spread_out(kernel, at, pieces, widths, name):
    total = pieces[0].shape[-1]
    wide = [(w, lambda i, j, at: (0, 0, j * 4 + i)) for w in widths]
    blocks = [b if b[0] >= 128 else (128, lambda i, j, at: (0, 0, i)) for b in wide]
    return pl.pallas_call(
        functools.partial(kernel, widths),
        out_shape=[
            jax.ShapeDtypeStruct((ADAPTER_COUNT, ADAPTER_RANK, 8 * w if w >= 128 else 512), f32)
            for w in widths
        ],
        grid_spec=pltpu.PrefetchScalarGridSpec(
            num_scalar_prefetch=1,
            grid=(4, 2),
            in_specs=[ANY] * len(pieces),
            out_specs=[pl.BlockSpec((ADAPTER_COUNT, ADAPTER_RANK, w), m) for w, m in blocks],
            scratch_shapes=[
                pltpu.VMEM((4, ADAPTER_COUNT, ADAPTER_RANK, total), bf16),
                pltpu.SemaphoreType.DMA,
            ],
        ),
        compiler_params=pltpu.CompilerParams(vmem_limit_bytes=VMEM_LIMIT),
        name=name,
    )(at, *pieces)


def slices_of(at, pairs, name):
    shape = (4, ADAPTER_RANK, 512 * len(pairs))
    ins = [(a, None) for pair in pairs for a in pair]
    kernel = functools.partial(slices_kernel, len(pairs))
    return call(kernel, 1, at, ins, [(shape, bf16, None)], [], name)[0]


def shards(
    tokens,
    cotangent,
    attention_norm_scale,
    attention_norm_bias,
    query_projection,
    query_projection_bias,
    keyvalue_projection,
    value_projection_bias,
    attention_output_weight,
    attention_output_bias,
    feedforward_norm_scale,
    feedforward_norm_bias,
    up_projection_weight,
    up_projection_bias,
    down_projection_weight,
    down_projection_bias,
    sequence_adapter,
    query_adapter_input,
    query_adapter_output,
    keyvalue_adapter_input,
    keyvalue_adapter_output,
    output_adapter_input,
    output_adapter_output,
    up_adapter_input,
    up_adapter_output,
    down_adapter_input,
    down_adapter_output,
):
    y, core, zl, zh, x = (lax.axis_index(n) for n in ("y", "core", "zl", "zh", "x"))
    z = zh * 2 + zl
    at = jnp.stack([core, x, zh, y, z]).astype(jnp.int32)
    gain_one, shift_one = attention_norm_scale.astype(f32), attention_norm_bias.astype(f32)
    gain_two, shift_two = feedforward_norm_scale.astype(f32), feedforward_norm_bias.astype(f32)

    def ride(inner, first):
        wide = jnp.pad(inner, ((0, 0), (first, RIDE - 16 - first)))
        return jnp.where(core == 0, wide, jnp.roll(wide, 16, axis=1))

    mine = sequence_adapter[0, 0]
    down_back = dot_t(cotangent, pick(down_adapter_output, mine)).astype(bf16)
    cot_all = jnp.concatenate([cotangent, ride(down_back, 0)], axis=1)
    cot_all = lax.all_gather(cot_all, ("core", "x"), axis=0, tiled=True)
    cot_all = cot_all.reshape(2, 4, ROWS, MODEL_WIDTH + RIDE)
    attention_shard, feed_shard = call(
        pack_kernel,
        1,
        at,
        [
            (query_projection, None),
            (keyvalue_projection, None),
            (attention_output_weight, None),
            (up_projection_weight, None),
            (down_projection_weight, None),
        ],
        [((ROWS, 768), bf16, None), ((ROWS, 2048), bf16, None)],
        [],
        "pack",
    )
    attention_shard = turn(attention_shard)
    column = gather_cross(attention_shard, False)
    input_rows = tokens.astype(f32)
    normed = layer_norm(input_rows, gain_one, shift_one).astype(bf16)

    theirs = other_core(sequence_adapter)[0, 0]
    low = jnp.where(core == 0, mine, theirs)
    high = jnp.where(core == 0, theirs, mine)

    stacks = (
        query_adapter_input,
        query_adapter_output,
        keyvalue_adapter_input,
        keyvalue_adapter_output,
        output_adapter_input,
        output_adapter_output,
        up_adapter_input,
        up_adapter_output,
        down_adapter_input,
        down_adapter_output,
    )
    column, normed, stacks, low, high = together((column, normed, stacks, low, high))
    plane = gather_cross(jnp.stack(column), True)
    normed_sides = gather_sides(normed)
    (
        query_adapter_input,
        query_adapter_output,
        keyvalue_adapter_input,
        keyvalue_adapter_output,
        output_adapter_input,
        output_adapter_output,
        up_adapter_input,
        up_adapter_output,
        down_adapter_input,
        down_adapter_output,
    ) = stacks

    def ordered(stack):
        return jnp.concatenate([pick(stack, low), pick(stack, high)], axis=0)

    def ordered_t(stack):
        return ordered(jnp.swapaxes(stack, 1, 2))

    def padded(*pairs):
        rest = jnp.zeros((RIDE - 32 * len(pairs), pairs[0].shape[1]), bf16)
        return jnp.concatenate([*pairs, rest], axis=0)

    small = jnp.concatenate(
        [
            ordered(query_adapter_output),
            ordered_t(output_adapter_input),
            ordered(up_adapter_output),
            ordered_t(down_adapter_input),
        ],
        axis=1,
    )
    biases = jnp.concatenate(
        [
            query_projection_bias,
            jnp.zeros((256,), bf16),
            up_projection_bias,
            jnp.zeros((1024,), bf16),
        ]
    )
    small = turn(jnp.concatenate([small, biases[None], jnp.zeros((15, 2560), bf16)], axis=0))
    q_in = padded(ordered_t(query_adapter_input), ordered_t(keyvalue_adapter_input))
    u_in = padded(ordered_t(up_adapter_input))
    kv_out_pair = ordered(keyvalue_adapter_output)
    kv_out_both = padded(jnp.zeros_like(kv_out_pair), kv_out_pair)
    o_out, d_out = padded(ordered(output_adapter_output)), padded(ordered(down_adapter_output))

    kv_in, kv_out = pick(keyvalue_adapter_input, mine), pick(keyvalue_adapter_output, mine)
    keyval_bias = jnp.concatenate(
        [jnp.zeros((HEAD_WIDTH,), f32), value_projection_bias.astype(f32)]
    )
    place_block = jnp.stack([lax.rem(x + p, 4) for p in PLACES]) // 2
    own = place_block[:, None] <= place_block[None, :]
    bias = jnp.concatenate([own, jnp.broadcast_to(zh == 1, (4, 4))], axis=0)
    bias = jnp.repeat(jnp.where(bias, 0.0, -1e30).astype(f32), ROWS, axis=1)

    keyval_inner = dot(normed, kv_in).astype(bf16)
    keyval_ride = ride(keyval_inner, 32)
    q_bias, u_bias = small[32:33, :256].astype(f32), small[32:33, 512:1536].astype(f32)
    small = padded(small[:32])
    q_out, o_in, u_out, d_in = (
        small[:, :256],
        small[:, 256:512],
        small[:, 512:1536],
        small[:, 1536:],
    )
    prepared = (keyval_inner, keyval_ride, kv_in, kv_out, q_in, u_in, o_out, d_out)
    prepared += (kv_out_both, q_out, o_in, u_out, d_in, bias)
    plane, normed_sides, prepared = together((plane, normed_sides, prepared))
    keyval_inner, keyval_ride, kv_in, kv_out, q_in, u_in, o_out, d_out = prepared[:8]
    kv_out_both, q_out, o_in, u_out, d_in, bias = prepared[8:]
    normed_places = gather_rest(*normed_sides)
    (w,) = call(
        assemble_kernel,
        1,
        at,
        [(piece, ANY) for piece in plane],
        [((MODEL_WIDTH, 768), bf16, None)],
        [pltpu.SemaphoreType.DMA],
        "assemble",
    )
    feed_shard, w, cot_all = together((feed_shard, w, cot_all))
    feed = lax.all_gather(feed_shard, DP + ("zh",), axis=0, tiled=True)
    feed = feed.reshape(16, 2, ROWS, 2048)

    keyval = (dot(normed, w[:, 256:512]) + keyval_bias + dot(keyval_inner, kv_out)).astype(bf16)
    keyval = other_half(jnp.concatenate([keyval, keyval_ride], axis=1))
    keyval = jnp.concatenate([keyval, other_core(keyval)], axis=0)
    keyval_places = (keyval, ring_x(keyval, 1), ring_x(keyval, -1), ring_x(keyval, 2))

    group = (2, 4 * ROWS)
    row_scratch = pltpu.VMEM((2, 4 * ROWS, MODEL_WIDTH), bf16)
    w_scratch = pltpu.VMEM((MODEL_WIDTH, 768), bf16)
    inner_one, inner_far, query, keyval_all, log_total, attended, *out_parts = call(
        attention_kernel,
        2,
        at,
        [
            *flat(normed_places),
            *[(piece, ANY) for piece in keyval_places],
            (w, ANY),
            (q_in, None),
            (q_out, None),
            (kv_out_both, None),
            (o_in, None),
            (q_bias, None),
            (keyval_bias[None], None),
            (bias, None),
        ],
        [
            ((*group, RIDE), bf16, step_block((4 * ROWS, RIDE))),
            ((*group, RIDE), bf16, step_block((4 * ROWS, RIDE))),
            ((*group, 256), bf16, step_block((4 * ROWS, 256))),
            ((2, 8, ROWS, 256), bf16, step_block((8, ROWS, 256))),
            ((2, 2, 4 * ROWS), f32, step_block((2, 4 * ROWS))),
            ((*group, 256), bf16, step_block((4 * ROWS, 256))),
            *part_outs(MODEL_WIDTH + RIDE),
        ],
        [row_scratch, pltpu.VMEM((2, 4, ROWS, 384), bf16), w_scratch, dma(4)],
        "attention",
        9000000000,
    )
    out_sum = scatter_row(*out_parts)
    output_inner = out_sum[:, MODEL_WIDTH:].astype(bf16)
    middle = (
        input_rows
        + out_sum[:, :MODEL_WIDTH]
        + attention_output_bias.astype(f32)
        + dot(output_inner, o_out)
    )
    normed_two = layer_norm(middle, gain_two, shift_two).astype(bf16)
    place_scratch = pltpu.VMEM((4, 2 * ROWS, MODEL_WIDTH), bf16)
    feed_scratch = pltpu.VMEM((16, ROWS, 1024), bf16)
    inner_two, pre, act, *down_parts = call(
        feed_kernel,
        4,
        at,
        [
            *flat(gather_row(normed_two)),
            (feed, ANY),
            (u_in, None),
            (u_out, None),
            (d_in, None),
            (u_bias, None),
        ],
        [
            ((4, 2 * ROWS, RIDE), bf16, step_block((2 * ROWS, RIDE))),
            ((4, 2 * ROWS, 1024), f32, step_block((2 * ROWS, 1024))),
            ((4, 2 * ROWS, 1024), bf16, step_block((2 * ROWS, 1024))),
            *part_outs(MODEL_WIDTH + RIDE, True),
        ],
        [place_scratch, feed_scratch, feed_scratch, dma(6)],
        "feed",
        9500000000,
    )
    down_low = scatter_start(*down_parts)
    down_low, act = together((down_low, act))
    down_moved = (ring_x(down_low[1], -1), ring_x(down_low[2], 1), ring_x(down_low[3], 2))

    up_b, down_a, *up_parts = call(
        feed_back_kernel,
        4,
        at,
        [
            (cot_all, ANY),
            (feed, ANY),
            (pre, step_block((2 * ROWS, 1024))),
            (act, step_block((2 * ROWS, 1024))),
            (inner_two, step_block((2 * ROWS, RIDE))),
            (d_in, None),
            (u_out, None),
        ],
        [((32, 1024), f32, None), ((32, 1024), f32, None), *part_outs(MODEL_WIDTH + RIDE, True)],
        [
            pltpu.VMEM((4, 2 * ROWS, MODEL_WIDTH + RIDE), bf16),
            feed_scratch,
            feed_scratch,
            dma(6),
        ],
        "feed_back",
        9500000000,
    )
    up_parts, down_moved, up_b, down_a = together((up_parts, down_moved, up_b, down_a))
    feed_set = row_slice(jnp.concatenate([up_b, down_a], axis=1), core, (1024, 1024))
    up_far = scatter_far(*up_parts[2:])
    up_far, feed_set = together((up_far, feed_set))
    down_sum = down_low[0] + sum(part.astype(f32) for part in down_moved)
    up_sum = scatter_last(add_cores(*up_parts[:2]), *scatter_sides(up_far))
    up_back = up_sum[:, MODEL_WIDTH:].astype(bf16)
    grad_normed_two = up_sum[:, :MODEL_WIDTH] + dot(up_back, u_in)
    _, norm_two_back = jax.vjp(lambda v: layer_norm(v, gain_two, shift_two), middle)
    grad_middle = cotangent.astype(f32) + norm_two_back(grad_normed_two)[0]
    grad_branch = grad_middle.astype(bf16)

    down_inner = down_sum[:, MODEL_WIDTH:].astype(bf16)
    layer_output = (
        middle
        + down_sum[:, :MODEL_WIDTH]
        + down_projection_bias.astype(f32)
        + dot(down_inner, d_out)
    ).astype(bf16)

    branch_sides = gather_sides(grad_branch)
    middle_slices = slices_of(
        at,
        [(up_back, normed_two), (output_inner, grad_branch), (down_inner, cotangent)],
        "slices",
    )
    branch_sides, middle_slices = together((branch_sides, middle_slices))
    branch_places = gather_rest(*branch_sides)
    feed_set = jnp.concatenate(
        [
            feed_set,
            total(scatter_sequence(middle_slices)),
            jnp.full((16, RIDE), mine, jnp.int32).astype(bf16),
        ],
        axis=1,
    )
    feed_column, branch_places = together((gather_y(feed_set), branch_places))
    feed_pieces = gather_z(jnp.stack(feed_column))
    query_b, output_a, keyval_b, backs, backs_far, *query_parts = call(
        attention_back_kernel,
        2,
        at,
        [
            *flat(branch_places),
            (w, ANY),
            (inner_one, step_block((4 * ROWS, RIDE))),
            (inner_far, step_block((4 * ROWS, RIDE))),
            (query, step_block((4 * ROWS, 256))),
            (keyval_all, step_block((8, ROWS, 256))),
            (log_total, step_block((2, 4 * ROWS))),
            (attended, step_block((4 * ROWS, 256))),
            (o_out, None),
            (o_in, None),
            (q_out, None),
            (kv_out_both, None),
            (bias, None),
        ],
        [
            ((32, 256), f32, None),
            ((32, 256), f32, None),
            ((32, 256), f32, None),
            ((*group, RIDE), bf16, step_block((4 * ROWS, RIDE))),
            ((2, 32, 4 * ROWS), bf16, step_block((32, 4 * ROWS))),
            *part_outs(2688),
        ],
        [
            row_scratch,
            w_scratch,
            pltpu.VMEM((8 * ROWS, HEAD_WIDTH), f32),
            pltpu.VMEM((8 * ROWS, HEAD_WIDTH), f32),
            dma(3),
        ],
        "attention_back",
        8000000000,
    )
    query_b, output_a, keyval_b, backs, backs_far, query_parts, feed_pieces = together(
        (query_b, output_a, keyval_b, backs, backs_far, query_parts, feed_pieces)
    )
    placed = row_slice(jnp.concatenate([query_b, output_a], axis=1), core, (256, 256))
    query_far, backs_far, placed = together(
        (scatter_far(*query_parts[2:]), other_half(backs_far), placed)
    )
    all_ids = jnp.concatenate([piece[:, 0, 5632] for piece in feed_pieces]).astype(jnp.int32)
    feed_kept, feed_sent = halves_of(sum_by_adapter(feed_pieces, all_ids), core)
    query_sides = scatter_sides(query_far)
    query_near = add_cores(*query_parts[:2])
    pack_shape = (4, ADAPTER_RANK, 1152)
    late_mine, late_theirs = call(
        late_kernel,
        1,
        at,
        [
            *flat(normed_places),
            (backs, None),
            (backs_far, None),
            (keyval_b, None),
        ],
        [(pack_shape, bf16, None), (pack_shape, bf16, None)],
        [row_scratch, dma(2)],
        "late",
    )
    late_mine, late_theirs, query_near, query_sides, feed_kept, feed_sent = together(
        (late_mine, late_theirs, query_near, query_sides, feed_kept, feed_sent)
    )
    late_pack = add_cores(late_mine, late_theirs).astype(bf16)
    feed_half = add_cores(feed_kept, feed_sent).astype(bf16)
    right, left = scatter_joined(query_near, *query_sides)
    late_pack, right, left, feed_half = together((late_pack, right, left, feed_half))
    feed_sum = lax.all_gather(feed_half, ("core", "x"), axis=0).reshape(2, 4, 4, 16, 5760)
    query_moved = ring_x(right, 1), ring_x(left, -1)
    late_set = jnp.concatenate([total(scatter_sequence(late_pack)), placed], axis=-1)
    column, query_moved = together((gather_y(late_set), query_moved))
    late_pieces = gather_z(jnp.stack(column))
    query_sum = query_near[0] + sum(part.astype(f32) for part in query_moved)
    grad_keyval = (
        query_sum[:, 2048:2304] + other_half(query_sum[:, 2304:2560].astype(bf16)).astype(f32)
    ).astype(bf16)
    query_back = query_sum[:, 2560:].astype(bf16)
    keyval_back = dot_t(grad_keyval, kv_out).astype(bf16)
    grad_normed = (
        query_sum[:, :MODEL_WIDTH]
        + dot(query_back, q_in)
        + dot_t(grad_keyval, w[:, 256:512])
        + dot_t(keyval_back, kv_in)
    )
    _, norm_one_back = jax.vjp(lambda v: layer_norm(v, gain_one, shift_one), input_rows)
    grad_tokens = (grad_middle + norm_one_back(grad_normed)[0]).astype(bf16)

    late_pieces, grad_tokens = together((late_pieces, grad_tokens))
    kept, sent = halves_of(sum_by_adapter(late_pieces, all_ids), core)
    own_half = add_cores(kept, sent).astype(bf16)
    other_part = other_core(own_half)
    near = ring_by_core(jnp.concatenate([own_half, other_part], axis=0))
    far = ring_x(own_half, 2)
    feed_grads = spread_out(
        feed_spread_kernel, at, [feed_sum], (1024, 1024, 256, 256, 256), "feed_spread"
    )
    near, far, feed_grads = together((near, far, feed_grads))
    up_b, down_a, up_a, output_b, down_b = feed_grads
    query_a, keyval_a, keyval_b, query_b, output_a = spread_out(
        late_spread_kernel,
        at,
        [own_half, other_part, near, other_core(near), far, other_core(far)],
        (256, 256, 64, 256, 256),
        "late_spread",
    )
    keyval_b = keyval_b.reshape(8, 16, 2, 2, 128).sum(axis=3).reshape(8, 16, 256)

    def side_in(a):
        return jnp.swapaxes(a, 1, 2)

    return (
        layer_output,
        grad_tokens,
        side_in(query_a),
        query_b,
        side_in(keyval_a),
        keyval_b,
        side_in(output_a),
        output_b,
        side_in(up_a),
        up_b,
        side_in(down_a),
        down_b,
    )

def solution(mesh):
    fine = Mesh(mesh.devices.reshape(SIZES), AXES)
    in_specs = (
        P(AXES, None),
        P(AXES, None),
        P(),
        P(),
        P(DP, MP),
        P(MP),
        P(DP, None),
        P(),
        P(MP, DP),
        P(),
        P(),
        P(),
        P(DP, MP),
        P(MP),
        P(MP, DP),
        P(),
        P(DP, None),
        P(),
        P(None, None, MP),
        P(),
        P(),
        P(None, MP, None),
        P(),
        P(),
        P(None, None, MP),
        P(None, MP, None),
        P(),
    )
    out_specs = (P(AXES, None), P(AXES, None)) + (P(),) * 10
    return jax.shard_map(shards, mesh=fine, in_specs=in_specs, out_specs=out_specs, check_vma=False)
```

```python
import functools
import math

import jax
import jax.numpy as jnp
from jax import lax
from jax.experimental import pallas as pl
from jax.experimental.pallas import tpu as pltpu
from jax.sharding import Mesh
from jax.sharding import PartitionSpec as P

MODEL_WIDTH = 2048
H = 16
HEAD_WIDTH = 128
FEED_HIDDEN = 8192
ADAPTER_RANK = 16
ADAPTER_COUNT = 8
BLOCK = 256

AXES = ("y", "zl", "core", "zh", "x")
SIZES = (4, 2, 2, 2, 4)
DP = ("y", "zl", "core")
MP = ("zh", "x")
PLACES = (0, 3, 1, 2)
Z_RING = (0, 2, 1, 3)
ROWS = 128
RIDE = 128

f32 = jnp.float32
bf16 = jnp.bfloat16


together = lax.optimization_barrier


def ring_x(a, step):
    return lax.ppermute(a, "x", [(i, (i + step) % 4) for i in range(4)])


def ring_y(a, step):
    return lax.ppermute(a, "y", [(i, (i + step) % 4) for i in range(4)])


def ring_z(a, step):
    return lax.ppermute(a, ("zl", "zh"), [(Z_RING[i], Z_RING[(i + step) % 4]) for i in range(4)])


def other_core(a):
    return lax.ppermute(a, "core", [(0, 1), (1, 0)])


def other_half(a):
    return lax.ppermute(a, "zh", [(0, 1), (1, 0)])


def turn(a):
    return lax.ppermute(a, ("core", "zh"), [(0, 0), (1, 2), (2, 1), (3, 3)])


def plane_pairs(step, swapped):
    def index(y, z, core):
        return ((y * 2 + z % 2) * 2 + core) * 2 + z // 2

    pairs = []
    for y in range(4):
        for z in range(4):
            for core in range(2):
                if (core == 0) != swapped:
                    to = index((y + step) % 4, z, core)
                else:
                    to = index(y, (z + step) % 4, core)
                pairs.append((index(y, z, core), to))
    return pairs


def gather_cross(a, swapped):
    return [a] + [
        lax.ppermute(a, ("y", "zl", "core", "zh"), plane_pairs(-step, swapped))
        for step in (1, 2, 3)
    ]


def gather_sides(a):
    return a, ring_x(a, 1), ring_x(a, -1)


def gather_rest(a, left, right, near=None):
    half = a.shape[0] // 2
    near = other_core(a) if near is None else near
    top, bottom = ring_x(left[:half], 1), ring_x(right[half:], -1)
    return (
        (a, near),
        (left, other_core(left)),
        (right, other_core(right)),
        (top, bottom, other_core(top), other_core(bottom)),
    )


def gather_row(a):
    near = other_core(a)
    return gather_rest(*gather_sides(a), near)


def add_cores(mine, theirs):
    return mine.astype(f32) + other_core(theirs).astype(f32)


def scatter_far(far_mine, far_theirs):
    return add_cores(far_mine, far_theirs).astype(bf16)


def scatter_sides(far):
    half = far.shape[0] // 2
    return ring_x(far[:half], 1), ring_x(far[half:], -1)


def scatter_joined(near, up, down):
    half = up.shape[0]
    right = jnp.concatenate([near[2, :half] + up.astype(f32), near[2, half:]]).astype(bf16)
    left = jnp.concatenate([near[1, :half], near[1, half:] + down.astype(f32)]).astype(bf16)
    return right, left


def scatter_last(near, up, down):
    right, left = scatter_joined(near, up, down)
    return near[0] + ring_x(right, 1).astype(f32) + ring_x(left, -1).astype(f32)


def scatter_row(mine, theirs, far_mine, far_theirs):
    up, down = scatter_sides(scatter_far(far_mine, far_theirs))
    return scatter_last(add_cores(mine, theirs), up, down)


def scatter_start(mine, theirs, far_mine, far_theirs):
    far = add_cores(far_mine, far_theirs).astype(bf16)
    near = add_cores(mine, theirs)
    return near[0], near[1].astype(bf16), near[2].astype(bf16), far


def gather_y(a):
    return [a, ring_y(a, -1), ring_y(a, 2), ring_y(a, 1)]


def gather_z(a):
    return [a, ring_z(a, -1), ring_z(a, 2), ring_z(a, 1)]


def ring_by_core(a):
    pairs = [(i, (i + 1) % 4) for i in range(4)] + [(4 + i, 4 + (i + 3) % 4) for i in range(4)]
    return lax.ppermute(a, ("core", "x"), pairs)


def by_core(core, own, other):
    return jnp.where(
        core == 0, jnp.concatenate([own, other], -1), jnp.concatenate([other, own], -1)
    )


def row_slice(pair, core, widths):
    own = jnp.where(core == 0, pair[:16], pair[16:]).astype(bf16)
    other = other_core(jnp.where(core == 0, pair[16:], pair[:16]).astype(bf16))
    ends = [sum(widths[:k]) for k in range(1, len(widths))]
    pieces = zip(jnp.split(own, ends, axis=1), jnp.split(other, ends, axis=1))
    return jnp.concatenate([by_core(core, a, b) for a, b in pieces], axis=1)


def scatter_sequence(slices):
    return slices[0], ring_x(slices[1], 1), ring_x(slices[3], -1), ring_x(slices[2], 2)


def total(parts):
    return sum(part.astype(f32) for part in parts).astype(bf16)


def layer_norm(values, gain, shift):
    mean_value = jnp.mean(values, axis=-1, keepdims=True)
    centred = values - mean_value
    variance = jnp.mean(centred * centred, axis=-1, keepdims=True)
    return centred * lax.rsqrt(variance + 1e-05) * gain + shift


def gelu_tanh(values):
    inner_product = math.sqrt(2.0 / math.pi) * (values + 0.044715 * values * values * values)
    return 0.5 * values * (1.0 + jnp.tanh(inner_product))


def pick(adapter_stack, position):
    return lax.dynamic_index_in_dim(adapter_stack, position, 0, keepdims=False)


def dot(left, right):
    return jnp.dot(left, right, preferred_element_type=f32)


def dot_t(left, right):
    return lax.dot_general(left, right, (((1,), (1,)), ((), ())), preferred_element_type=f32)


def tdot(left, right):
    return lax.dot_general(left, right, (((0,), (0,)), ((), ())), preferred_element_type=f32)


def lane_owner(rows, row_core):
    lane = lax.broadcasted_iota(jnp.int32, (rows, RIDE), 1)
    owner = lax.rem(lane // ADAPTER_RANK, 2)
    return jnp.logical_and(owner == row_core, lane < 4 * ADAPTER_RANK)


def place_mask(core):
    row = lax.broadcasted_iota(jnp.int32, (2 * ROWS, RIDE), 0)
    return lane_owner(2 * ROWS, jnp.where(row < ROWS, core, 1 - core))


def copy(source, target, sem):
    pltpu.make_async_copy(source, target, sem).start()


def wait(target, sem):
    pltpu.make_async_copy(target, target, sem).wait()


def copy_place(pieces, target_mine, target_theirs, sem):
    half = ROWS // 2
    if len(pieces) == 2:
        copy(pieces[0], target_mine, sem)
        copy(pieces[1], target_theirs, sem)
    else:
        copy(pieces[0], target_mine.at[pl.ds(0, half)], sem)
        copy(pieces[1], target_mine.at[pl.ds(half, half)], sem)
        copy(pieces[2], target_theirs.at[pl.ds(0, half)], sem)
        copy(pieces[3], target_theirs.at[pl.ds(half, half)], sem)


def split_pieces(refs):
    return (refs[0:2], refs[2:4], refs[4:6], refs[6:10])


def copy_row(gathered, at, target_of, sem_of):
    core, x = at[0], at[1]
    for p in range(4):
        there = lax.rem(x + PLACES[p], 4)
        copy(gathered.at[core, there], target_of(p, 0), sem_of(p, 0))
        copy(gathered.at[1 - core, there], target_of(p, 1), sem_of(p, 1))


def assemble_kernel(at, *refs):
    pieces, (out, sem) = refs[:4], refs[4:]
    core, y, z = at[0], at[3], at[4]
    for far, piece in enumerate(pieces):
        for near in range(4):
            to_y = lax.rem(y + jnp.where(core == 0, near, far), 4)
            to_z = lax.rem(z + jnp.where(core == 0, far, near), 4)
            shard = (to_y * 2 + lax.rem(to_z, 2)) * 2 + to_z // 2
            copy(piece.at[near], out.at[pl.ds(pl.multiple_of(shard * ROWS, ROWS), ROWS)], sem)
    wait(out, sem)


def pack_kernel(at, *refs):
    first = 0
    for part in refs[:-2]:
        refs[-1][:, first : first + part.shape[1]] = part[...]
        first += part.shape[1]
    refs[-1][:, first:] = refs[-2][...].astype(f32).T.astype(bf16)


def norm_kernel(at, rows, gain, shift, out):
    values = layer_norm(
        rows[...].astype(f32), gain[...].astype(f32), shift[...].astype(f32)
    )
    out[...] = values.astype(bf16)


def select_kernel(at, *refs):
    pairs = [refs[2 * n : 2 * n + 2] for n in range(10)]
    q_bias, u_bias = refs[20:22]
    small, q_in, u_in, o_out, d_out, kv_out, bias = refs[22:]
    for out, count in ((q_in, 4), (u_in, 2), (o_out, 2), (d_out, 2)):
        out[16 * count :] = jnp.zeros((RIDE - 16 * count, MODEL_WIDTH), bf16)
    kv_out[...] = jnp.zeros_like(kv_out)
    for c in range(2):
        here, after = slice(16 * c, 16 * c + 16), slice(32 + 16 * c, 48 + 16 * c)
        q_in[here] = pairs[0][c][0]
        q_in[after] = pairs[1][c][0]
        u_in[here] = pairs[2][c][0]
        o_out[here] = pairs[3][c][0]
        d_out[here] = pairs[4][c][0]
        kv_out[after] = pairs[5][c][0]
        first = 0
        for n in range(6, 10):
            width = pairs[n][c].shape[2]
            small[here, first : first + width] = pairs[n][c][0]
            first += width
    small[32:] = jnp.zeros((16, 2560), bf16)
    small[32:33, :256] = q_bias[...]
    small[32:33, 512:1536] = u_bias[...]
    x, zh = at[2], at[3]

    def block_of(place):
        step = jnp.where(place == 0, 0, jnp.where(place == 1, 3, place - 1))
        return ((x + step) & 3) >> 1

    key = lax.broadcasted_iota(jnp.int32, (8, 4 * ROWS), 0)
    query = lax.broadcasted_iota(jnp.int32, (8, 4 * ROWS), 1) >> 7
    own = jnp.logical_and(key < 4, block_of(key) <= block_of(query))
    other = jnp.logical_and(key >= 4, zh == 1)
    bias[...] = jnp.where(jnp.logical_or(own, other), 0.0, -1e30)


def turned_kernel(at, small, q_out, o_in, u_out, d_in, q_bias, u_bias):
    first = 0
    for out in (q_out, o_in, u_out, d_in):
        width = out.shape[1]
        out[:32] = small[:32, first : first + width]
        out[32:] = jnp.zeros((RIDE - 32, width), bf16)
        first += width
    q_bias[...] = small[32:33, :256].astype(f32)
    u_bias[...] = small[32:33, 512:1536].astype(f32)


def own_keyval_kernel(at, rows, w, q_in, kv_out, kv_bias, out):
    inner = dot_t(rows[...], q_in[...])
    lane = lax.broadcasted_iota(jnp.int32, (ROWS, RIDE), 1)
    inner = jnp.where(lane // ADAPTER_RANK == 2 + at[0], inner, 0.0).astype(bf16)
    keyval = dot(rows[...], w[...]) + kv_bias[...] + dot(inner, kv_out[...])
    out[:, :256] = keyval.astype(bf16)
    out[:, 256:] = inner


def sum_kernel(at, *refs):
    pieces, (kept, sent, total) = refs[:-3], refs[-3:]
    total[...] = jnp.zeros_like(total)
    row = 1
    for piece in pieces:
        for k in range(piece.shape[0]):
            total[at[row]] += piece[k].astype(f32)
            row += 1
    kept[...] = total[pl.ds(4 * at[0], 4)].astype(bf16)
    sent[...] = total[pl.ds(4 - 4 * at[0], 4)].astype(bf16)


def slices_kernel(count, at, *refs):
    ins, out = refs[: 2 * count], refs[2 * count]
    x = at[1]
    for n in range(count):
        back, rows = ins[2 * n], ins[2 * n + 1]
        turned = back[...].astype(f32).T
        turned = (turned[:16] + turned[16:32]).astype(bf16)
        product = dot(turned, rows[...]).astype(bf16)
        for to in range(4):
            place = lax.rem(to + 4 - x, 4)
            for c in range(2):
                first = (c * 4 + to) * 256
                lanes = slice(n * 512 + c * 256, n * 512 + (c + 1) * 256)
                out[place, :, lanes] = product[:, first : first + 256]


def spread(scratch, outs, widths):
    x, c = pl.program_id(0), pl.program_id(1)
    first = 0
    for out, width in zip(outs, widths):
        if width < 128:
            out[...] = scratch[x, :, :, first : first + 128].astype(f32)
            first += 128
        else:
            here = pl.ds(pl.multiple_of(first + c * width, 128), width)
            out[...] = scratch[x, :, :, here].astype(f32)
            first += 2 * width


def feed_spread_kernel(widths, at, *refs):
    gathered, (scratch, sem) = refs[0], refs[-2:]

    @pl.when((pl.program_id(0) == 0) & (pl.program_id(1) == 0))
    def _():
        for c in range(2):
            for x in range(4):
                copy(gathered.at[c, x], scratch.at[x, pl.ds(4 * c, 4)], sem)
        wait(scratch, sem)

    spread(scratch, refs[1:-2], widths)


def late_spread_kernel(widths, at, *refs):
    own, other, near, near_other, far, far_other = refs[:6]
    scratch, sem = refs[-2:]
    core, x = at[0], at[1]

    @pl.when((pl.program_id(0) == 0) & (pl.program_id(1) == 0))
    def _():
        mine, theirs = pl.ds(4 * core, 4), pl.ds(4 * (1 - core), 4)
        side = lax.rem(x + jnp.where(core == 0, 3, 1), 4)
        other_side = lax.rem(x + jnp.where(core == 0, 1, 3), 4)
        across = lax.rem(x + 2, 4)
        copy(own, scratch.at[x, mine], sem)
        copy(other, scratch.at[x, theirs], sem)
        for part, where in ((0, mine), (1, theirs)):
            copy(near.at[pl.ds(4 * part, 4)], scratch.at[side, where], sem)
        for part, where in ((0, theirs), (1, mine)):
            copy(near_other.at[pl.ds(4 * part, 4)], scratch.at[other_side, where], sem)
        copy(far, scratch.at[across, mine], sem)
        copy(far_other, scratch.at[across, theirs], sem)
        wait(scratch, sem)

    spread(scratch, refs[6:-2], widths)


def copy_rows(rows_in, rows, sems):
    half = ROWS // 2
    for s in range(2):
        for p in range(4):
            pieces = rows_in[p]
            if len(pieces) == 2:
                copy(pieces[s], rows.at[s, pl.ds(p * ROWS, ROWS)], sems.at[s])
            else:
                for n in range(2):
                    here = pl.ds(p * ROWS + n * half, half)
                    copy(pieces[2 * s + n], rows.at[s, here], sems.at[s])


def attention_kernel(at, *refs):
    rows_in = split_pieces(refs[:10])
    kv_in = refs[10:15]
    w, q_in, q_out, kv_out, o_in, q_bias, kv_bias, bias = refs[15:23]
    inner_out, inner_far, query_out, kv_all, lse_out, att_out = refs[23:29]
    parts, far_parts = refs[29:31], refs[31:33]
    rows, kvs, ws, sems = refs[33:]
    s = pl.program_id(0)
    core = at[0]

    @pl.when(s == 0)
    def _():
        copy(w, ws, sems.at[2])
        copy_rows(rows_in, rows, sems)
        pair, near, near_other, far, far_other = kv_in
        first, second = pl.ds(0, ROWS), pl.ds(ROWS, ROWS)
        side = jnp.where(core == 0, 1, 2)
        copy(pair.at[first], kvs.at[0, 0], sems.at[3])
        copy(pair.at[second], kvs.at[1, 0], sems.at[3])
        copy(near.at[first], kvs.at[0, side], sems.at[3])
        copy(near.at[second], kvs.at[1, side], sems.at[3])
        copy(near_other.at[first], kvs.at[1, 3 - side], sems.at[3])
        copy(near_other.at[second], kvs.at[0, 3 - side], sems.at[3])
        copy(far, kvs.at[0, 3], sems.at[3])
        copy(far_other, kvs.at[1, 3], sems.at[3])
        wait(ws, sems.at[2])
        wait(kvs, sems.at[3])

    wait(rows.at[s], sems.at[s])

    owner = lane_owner(4 * ROWS, jnp.where(s == 0, core, 1 - core))
    x = rows[s]
    inner = jnp.where(owner, dot_t(x, q_in[...]), 0.0).astype(bf16)
    inner_out[0] = inner
    query = (dot(x, ws[:, :256]) + q_bias[...] + dot(inner, q_out[...])).astype(bf16)
    query_out[0] = query
    kv_own = (dot(x, ws[:, 256:512]) + kv_bias[...] + dot(inner, kv_out[...])).astype(bf16)
    inner_far[0] = kvs[s, :, :, 256:].reshape(4 * ROWS, RIDE)
    kv = jnp.concatenate([kv_own.reshape(4, ROWS, 256), kvs[s, :, :, :256]], axis=0)
    kv_all[0] = kv
    keys = kv[:, :, :HEAD_WIDTH].reshape(8 * ROWS, HEAD_WIDTH)
    values_t = kv[:, :, HEAD_WIDTH:].reshape(8 * ROWS, HEAD_WIDTH).astype(f32).T.astype(bf16)
    columns = []
    for h in range(2):
        chunks = []
        for c in range(2):
            lanes = slice(c * 256, c * 256 + 256)
            q = query[lanes, h * HEAD_WIDTH : (h + 1) * HEAD_WIDTH]
            scores = dot_t(keys, q) * (HEAD_WIDTH**-0.5)
            scores = scores.reshape(8, ROWS, 256) + bias[:, lanes][:, None, :]
            scores = scores.reshape(8 * ROWS, 256)
            top = jnp.max(scores, axis=0, keepdims=True)
            expo = jnp.exp(scores - top)
            total = jnp.sum(expo, axis=0, keepdims=True)
            probs = (expo * (1.0 / total)).astype(bf16)
            lse_out[0, h : h + 1, lanes] = top + jnp.log(total)
            chunks.append(dot(values_t, probs).T)
        columns.append(jnp.concatenate(chunks, axis=0))
    attended = jnp.concatenate(columns, axis=1).astype(bf16)
    att_out[0] = attended
    low = jnp.where(owner, dot_t(attended, o_in[...]), 0.0).astype(bf16)
    for which in range(2):

        @pl.when(s == which)
        def _(which=which):
            for p in range(4):
                here = slice(p * ROWS, (p + 1) * ROWS)
                part = parts[which].at[p] if p < 3 else far_parts[which]
                part[:, :MODEL_WIDTH] = dot_t(attended[here], ws[:, 512:]).astype(bf16)
                part[:, MODEL_WIDTH:] = low[here]


def store_parts(p, parts, far_parts, out, low):
    for which in range(2):
        here = slice(which * ROWS, (which + 1) * ROWS)

        @pl.when(p < 3)
        def _(which=which, here=here):
            parts[which][0, :, :MODEL_WIDTH] = out[here]
            parts[which][0, :, MODEL_WIDTH:] = low[here]

        @pl.when(p == 3)
        def _(which=which, here=here):
            far_parts[which][:, :MODEL_WIDTH] = out[here]
            far_parts[which][:, MODEL_WIDTH:] = low[here]


def feed_kernel(at, *refs):
    rows_in = split_pieces(refs[:10])
    cot, feed, u_in, u_out, d_in, u_bias = refs[10:16]
    up_b, down_a = refs[16:18]
    down_parts, down_far = refs[18:20], refs[20:22]
    up_parts, up_far = refs[22:24], refs[24:26]
    rows, grads, up, down, slopes, sems = refs[26:]
    p = pl.program_id(0)
    core = at[0]

    @pl.when(p == 0)
    def _():
        copy_place(rows_in[0], rows.at[0, pl.ds(0, ROWS)], rows.at[0, pl.ds(ROWS, ROWS)], sems.at[0])
        copy(feed.at[:, core, :, pl.ds(0, 1024)], up, sems.at[8])
        copy(feed.at[:, core, :, pl.ds(1024, 1024)], down, sems.at[9])
        copy_row(
            cot,
            at,
            lambda k, which: grads.at[k, pl.ds(which * ROWS, ROWS)],
            lambda k, which: sems.at[4 + k],
        )
        for k in range(1, 4):
            copy_place(
                rows_in[k], rows.at[k, pl.ds(0, ROWS)], rows.at[k, pl.ds(ROWS, ROWS)], sems.at[k]
            )
        up_b[...] = jnp.zeros_like(up_b)
        down_a[...] = jnp.zeros_like(down_a)
        wait(up, sems.at[8])

    wait(rows.at[p], sems.at[p])
    mask = place_mask(core)
    x = rows[p]
    inner = jnp.where(mask, dot_t(x, u_in[...]), 0.0)
    inner_t, inner = inner.T[:32].astype(bf16), inner.astype(bf16)
    pre = dot(x, up[...].reshape(MODEL_WIDTH, 1024)) + u_bias[...] + dot(inner, u_out[...])
    k0 = math.sqrt(2.0 / math.pi)
    square = pre * pre
    bend = jnp.tanh(k0 * (pre + 0.044715 * square * pre))
    act = (0.5 * pre * (1.0 + bend)).astype(bf16)
    slopes[...] = 0.5 * (1.0 + bend) + 0.5 * pre * (1.0 - bend * bend) * (
        k0 * (1.0 + 3.0 * 0.044715 * square)
    )

    @pl.when(p == 0)
    def _():
        wait(down, sems.at[9])

    low = jnp.where(mask, dot_t(act, d_in[...]), 0.0).astype(bf16)
    out = dot_t(act, down[...].reshape(MODEL_WIDTH, 1024)).astype(bf16)
    store_parts(p, down_parts, down_far, out, low)

    wait(grads.at[p], sems.at[4 + p])
    grad, back = grads[p, :, :MODEL_WIDTH], grads[p, :, MODEL_WIDTH:]
    down_a[...] += dot(back.astype(f32).T[:32].astype(bf16), act)
    grad_act = dot(grad, down[...].reshape(MODEL_WIDTH, 1024)) + dot(back, d_in[...])
    grad_pre = (grad_act * slopes[...]).astype(bf16)
    up_b[...] += dot(inner_t, grad_pre)
    low = jnp.where(mask, dot_t(grad_pre, u_out[...]), 0.0).astype(bf16)
    out = dot_t(grad_pre, up[...].reshape(MODEL_WIDTH, 1024)).astype(bf16)
    store_parts(p, up_parts, up_far, out, low)


def late_kernel(at, *refs):
    rows_in = split_pieces(refs[:10])
    backs, backs_far, keyval_b = refs[10:13]
    outs, (rows, sems) = refs[13:15], refs[15:]
    core, x = at[0], at[1]
    copy_rows(rows_in, rows, sems)
    product = jnp.zeros((64, MODEL_WIDTH), f32)
    for s in range(2):
        wait(rows.at[s], sems.at[s])
        back = backs[s].astype(f32).T
        back = jnp.concatenate([back[:32], back[32:64] + backs_far[s].astype(f32)], axis=0)
        product += dot(back.astype(bf16), rows[s])
    first, second = keyval_b[:16], keyval_b[16:]
    lane = lax.broadcasted_iota(jnp.int32, (ADAPTER_RANK, RIDE), 1) // 64
    for which in range(2):
        out = outs[which]
        is_first = (core == 0) if which == 0 else (core != 0)
        for n in range(2):
            both = product[32 * n : 32 * n + 32]
            picked = jnp.where(is_first, both[:16], both[16:]).astype(bf16)
            for to in range(4):
                place = lax.rem(to + 4 - x, 4)
                for c in range(2):
                    begin = (c * 4 + to) * 256
                    lanes = slice(n * 512 + c * 256, n * 512 + (c + 1) * 256)
                    out[place, :, lanes] = picked[:, begin : begin + 256]
        picked = jnp.where(is_first, first, second).astype(bf16)
        for to in range(4):
            place = lax.rem(to + 4 - x, 4)
            part = picked[:, (to // 2) * 128 : (to // 2) * 128 + 128]
            out[place, :, 1024:1152] = jnp.where(lane == to % 2, part, jnp.zeros_like(part))


def attention_back_kernel(at, *refs):
    branch, w, inner_in, inner_far, query_in, kv_in, lse_in, att_in = refs[:8]
    o_out, o_in, q_out, kv_out, bias = refs[8:13]
    query_b, output_a, keyval_b, backs, backs_far = refs[13:18]
    parts, far_parts = refs[18:20], refs[20:22]
    rows, ws, grad_k, grad_v, sems = refs[22:]
    s = pl.program_id(0)
    core = at[0]

    @pl.when(s == 0)
    def _():
        copy(w, ws, sems.at[2])
        copy_row(
            branch,
            at,
            lambda p, which: rows.at[which, pl.ds(p * ROWS, ROWS)],
            lambda p, which: sems.at[which],
        )
        query_b[...] = jnp.zeros_like(query_b)
        output_a[...] = jnp.zeros_like(output_a)
        keyval_b[...] = jnp.zeros_like(keyval_b)
        wait(ws, sems.at[2])

    wait(rows.at[s], sems.at[s])

    owner = lane_owner(4 * ROWS, jnp.where(s == 0, core, 1 - core))
    scale = HEAD_WIDTH**-0.5
    x = rows[s]
    back = jnp.where(owner, dot_t(x, o_out[...]), 0.0)
    output_a[...] += dot(back.T[:32].astype(bf16), att_in[0])
    grad_att = (dot(x, ws[:, 512:]) + dot(back.astype(bf16), o_in[...])).astype(bf16)
    query = query_in[0]
    kv = kv_in[0]
    keys = kv[:, :, :HEAD_WIDTH].reshape(8 * ROWS, HEAD_WIDTH)
    values = kv[:, :, HEAD_WIDTH:].reshape(8 * ROWS, HEAD_WIDTH)
    keys_t = keys.astype(f32).T.astype(bf16)
    columns = []
    for h in range(2):
        chunks = []
        for c in range(2):
            lanes = slice(c * 256, c * 256 + 256)
            head = slice(h * HEAD_WIDTH, (h + 1) * HEAD_WIDTH)
            q, g = query[lanes, head], grad_att[lanes, head]
            scores = dot_t(keys, q) * scale
            scores = scores.reshape(8, ROWS, 256) + bias[:, lanes][:, None, :]
            probs = jnp.exp(scores.reshape(8 * ROWS, 256) - lse_in[0, h : h + 1, lanes])
            grad_probs = dot_t(values, g)
            delta = jnp.sum(probs * grad_probs, axis=0, keepdims=True)
            grad_scores = (probs * (grad_probs - delta)).astype(bf16)
            chunks.append((dot(keys_t, grad_scores) * scale).T)
            more_k = dot(grad_scores, q) * scale
            more_v = dot(probs.astype(bf16), g)
            if h == 0 and c == 0:
                grad_k[...] = more_k
                grad_v[...] = more_v
            else:
                grad_k[...] += more_k
                grad_v[...] += more_v
        columns.append(jnp.concatenate(chunks, axis=0))
    grad_query = jnp.concatenate(columns, axis=1).astype(bf16)
    inner_t = inner_in[0].astype(f32).T
    query_b[...] += dot(inner_t[:32].astype(bf16), grad_query)
    low = jnp.where(owner, dot_t(grad_query, q_out[...]), 0.0).astype(bf16)
    grad_kv = jnp.concatenate([grad_k[...], grad_v[...]], axis=1).astype(bf16)
    own_kv, far_kv = grad_kv[: 4 * ROWS], grad_kv[4 * ROWS :]
    keyval_b[...] += dot(inner_t[32:64].astype(bf16), own_kv)
    keyval_b[...] += dot(inner_far[0].astype(f32).T[32:64].astype(bf16), far_kv)
    backs[0] = low + jnp.where(owner, dot_t(own_kv, kv_out[...]), 0.0).astype(bf16)
    backs_far[0] = jnp.where(owner, dot_t(far_kv, kv_out[...]), 0.0).T[32:64].astype(bf16)
    for which in range(2):

        @pl.when(s == which)
        def _(which=which):
            for p in range(4):
                here = slice(p * ROWS, (p + 1) * ROWS)
                part = parts[which].at[p] if p < 3 else far_parts[which]
                part[:, :2048] = dot_t(grad_query[here], ws[:, :256]).astype(bf16)
                part[:, 2048:2304] = own_kv[here]
                part[:, 2304:2560] = far_kv[here]
                part[:, 2560:] = low[here]


VMEM_LIMIT = 56 * 1024 * 1024
ANY = pl.BlockSpec(memory_space=pl.ANY)


def whole_block(shape):
    return pl.BlockSpec(shape, lambda i, at: (0,) * len(shape))


def step_block(shape):
    return pl.BlockSpec((1, *shape), lambda i, at: (i,) + (0,) * len(shape))


def call(kernel, steps, at, ins, outs, scratch, name, flops=0):
    arrays = [a for a, _ in ins]
    in_specs = [whole_block(a.shape) if b is None else b for a, b in ins]
    out_specs = [whole_block(s) if b is None else b for s, _, b in outs]
    return pl.pallas_call(
        kernel,
        out_shape=[jax.ShapeDtypeStruct(s, d) for s, d, _ in outs],
        grid_spec=pltpu.PrefetchScalarGridSpec(
            num_scalar_prefetch=1,
            grid=(steps,),
            in_specs=in_specs,
            out_specs=out_specs,
            scratch_shapes=scratch,
        ),
        compiler_params=pltpu.CompilerParams(vmem_limit_bytes=VMEM_LIMIT),
        cost_estimate=pl.CostEstimate(
            flops=flops,
            bytes_accessed=sum(a.size * a.dtype.itemsize for a in arrays)
            + sum(math.prod(s) * 4 for s, _, _ in outs),
            transcendentals=0,
        ),
        name=name,
    )(at, *arrays)


def flat(places):
    return [(piece, ANY) for place in places for piece in place]


def part_outs(width, steps=False):
    block = pl.BlockSpec((1, ROWS, width), lambda i, at: (jnp.minimum(i, 2), 0, 0))
    near = ((3, ROWS, width), bf16, block if steps else None)
    return [near, near, ((ROWS, width), bf16, None), ((ROWS, width), bf16, None)]


def dma(n):
    return pltpu.SemaphoreType.DMA((n,))


def sum_by_adapter(pieces, core, ids):
    width = pieces[0].shape[-1]
    block = max(w for w in range(128, 3713, 128) if width % w == 0)
    half = (ADAPTER_COUNT // 2, ADAPTER_RANK)
    return pl.pallas_call(
        sum_kernel,
        out_shape=[jax.ShapeDtypeStruct((*half, width), bf16)] * 2,
        grid_spec=pltpu.PrefetchScalarGridSpec(
            num_scalar_prefetch=1,
            grid=(width // block,),
            in_specs=[
                pl.BlockSpec((p.shape[0], ADAPTER_RANK, block), lambda i, at: (0, 0, i))
                for p in pieces
            ],
            out_specs=[pl.BlockSpec((*half, block), lambda i, at: (0, 0, i))] * 2,
            scratch_shapes=[pltpu.VMEM((ADAPTER_COUNT, ADAPTER_RANK, block), f32)],
        ),
        compiler_params=pltpu.CompilerParams(vmem_limit_bytes=VMEM_LIMIT),
        name="sum_by_adapter",
    )(jnp.concatenate([jnp.reshape(core, (1,)), ids]).astype(jnp.int32), *pieces)


def spread_out(kernel, at, pieces, widths, name):
    total = pieces[0].shape[-1]
    wide = [(w, lambda i, j, at: (0, 0, j * 4 + i)) for w in widths]
    blocks = [b if b[0] >= 128 else (128, lambda i, j, at: (0, 0, i)) for b in wide]
    return pl.pallas_call(
        functools.partial(kernel, widths),
        out_shape=[
            jax.ShapeDtypeStruct((ADAPTER_COUNT, ADAPTER_RANK, 8 * w if w >= 128 else 512), f32)
            for w in widths
        ],
        grid_spec=pltpu.PrefetchScalarGridSpec(
            num_scalar_prefetch=1,
            grid=(4, 2),
            in_specs=[ANY] * len(pieces),
            out_specs=[pl.BlockSpec((ADAPTER_COUNT, ADAPTER_RANK, w), m) for w, m in blocks],
            scratch_shapes=[
                pltpu.VMEM((4, ADAPTER_COUNT, ADAPTER_RANK, total), bf16),
                pltpu.SemaphoreType.DMA,
            ],
        ),
        compiler_params=pltpu.CompilerParams(vmem_limit_bytes=VMEM_LIMIT),
        name=name,
    )(at, *pieces)


def slices_of(at, pairs, name):
    shape = (4, ADAPTER_RANK, 512 * len(pairs))
    ins = [(a, None) for pair in pairs for a in pair]
    kernel = functools.partial(slices_kernel, len(pairs))
    return call(kernel, 1, at, ins, [(shape, bf16, None)], [], name)[0]


def shards(
    tokens,
    cotangent,
    attention_norm_scale,
    attention_norm_bias,
    query_projection,
    query_projection_bias,
    keyvalue_projection,
    value_projection_bias,
    attention_output_weight,
    attention_output_bias,
    feedforward_norm_scale,
    feedforward_norm_bias,
    up_projection_weight,
    up_projection_bias,
    down_projection_weight,
    down_projection_bias,
    sequence_adapter,
    query_adapter_input,
    query_adapter_output,
    keyvalue_adapter_input,
    keyvalue_adapter_output,
    output_adapter_input,
    output_adapter_output,
    up_adapter_input,
    up_adapter_output,
    down_adapter_input,
    down_adapter_output,
):
    y, core, zl, zh, x = (lax.axis_index(n) for n in ("y", "core", "zl", "zh", "x"))
    z = zh * 2 + zl
    at = jnp.stack([core, x, zh, y, z]).astype(jnp.int32)
    gain_one, shift_one = attention_norm_scale.astype(f32), attention_norm_bias.astype(f32)
    gain_two, shift_two = feedforward_norm_scale.astype(f32), feedforward_norm_bias.astype(f32)

    def pack(*parts):
        width = sum(part.shape[1] for part in parts[:-1]) + parts[-1].shape[0]
        ins = [(part, None) for part in parts]
        return call(pack_kernel, 1, at, ins, [((ROWS, width), bf16, None)], [], "pack")[0]

    mine = sequence_adapter[0, 0]
    theirs = other_core(sequence_adapter)[0, 0]
    attention_shard = pack(query_projection, keyvalue_projection, attention_output_weight)
    attention_shard, cotangent = together((attention_shard, cotangent))
    down_back = dot_t(cotangent, pick(down_adapter_output, mine)).astype(bf16)
    down_back = jnp.pad(down_back, ((0, 0), (0, RIDE - 16)))
    down_back = jnp.where(core == 0, down_back, jnp.roll(down_back, 16, axis=1))
    cot_all = jnp.concatenate([cotangent, down_back], axis=1)
    cot_all = lax.all_gather(cot_all, ("core", "x"), axis=0, tiled=True)
    cot_all = cot_all.reshape(2, 4, ROWS, MODEL_WIDTH + RIDE)

    attention_shard = turn(attention_shard)
    feed_shard = pack(up_projection_weight, down_projection_weight)
    rows_shape = ((ROWS, MODEL_WIDTH), bf16, None)
    normed = call(
        norm_kernel,
        1,
        at,
        [(tokens, None), (attention_norm_scale[None], None), (attention_norm_bias[None], None)],
        [rows_shape],
        [],
        "norm",
    )[0]
    attention_shard, normed, feed_shard, mine, theirs = together(
        (attention_shard, normed, feed_shard, mine, theirs)
    )
    column, mine, theirs = together((gather_cross(attention_shard, False), mine, theirs))
    plane = gather_cross(jnp.stack(column), True)
    normed_sides = gather_sides(normed)

    low = jnp.where(core == 0, mine, theirs)
    high = jnp.where(core == 0, theirs, mine)
    stacks = (
        jnp.swapaxes(query_adapter_input, 1, 2),
        jnp.swapaxes(keyvalue_adapter_input, 1, 2),
        jnp.swapaxes(up_adapter_input, 1, 2),
        output_adapter_output,
        down_adapter_output,
        keyvalue_adapter_output,
        query_adapter_output,
        jnp.swapaxes(output_adapter_input, 1, 2),
        up_adapter_output,
        jnp.swapaxes(down_adapter_input, 1, 2),
    )
    chosen = []
    for stack in stacks:
        block = (1, ADAPTER_RANK, stack.shape[2])
        chosen.append((stack, pl.BlockSpec(block, lambda i, at: (at[0], 0, 0))))
        chosen.append((stack, pl.BlockSpec(block, lambda i, at: (at[1], 0, 0))))
    wide = ((RIDE, MODEL_WIDTH), bf16, None)
    small, q_in, u_in, o_out, d_out, kv_out, bias = call(
        select_kernel,
        1,
        jnp.stack([low, high, x, zh]).astype(jnp.int32),
        [*chosen, (query_projection_bias[None], None), (up_projection_bias[None], None)],
        [
            ((48, 2560), bf16, None),
            wide,
            wide,
            wide,
            wide,
            ((RIDE, 256), bf16, None),
            ((8, 4 * ROWS), f32, None),
        ],
        [],
        "select",
    )
    keyval_bias = jnp.concatenate(
        [jnp.zeros((1, HEAD_WIDTH), f32), value_projection_bias.astype(f32)[None]], axis=1
    )
    prepared = (q_in, u_in, o_out, d_out, kv_out, bias, keyval_bias, small)
    plane, normed_sides, prepared = together((plane, normed_sides, prepared))
    q_in, u_in, o_out, d_out, kv_out, bias, keyval_bias, small = prepared
    normed_places = gather_rest(*normed_sides)
    (w,) = call(
        assemble_kernel,
        1,
        at,
        [(piece, ANY) for piece in plane],
        [((MODEL_WIDTH, 768), bf16, None)],
        [pltpu.SemaphoreType.DMA],
        "assemble",
    )
    feed_shard, w, cot_all = together((feed_shard, w, cot_all))
    feed = lax.all_gather(feed_shard, DP + ("zh",), axis=0, tiled=True)
    feed = feed.reshape(16, 2, ROWS, 2048)

    w_keyval = pl.BlockSpec((MODEL_WIDTH, 256), lambda i, at: (0, 1))
    keyval = call(
        own_keyval_kernel,
        1,
        at,
        [(normed, None), (w, w_keyval), (q_in, None), (kv_out, None), (keyval_bias, None)],
        [((ROWS, 384), bf16, None)],
        [],
        "own_keyval",
    )[0]
    keyval = other_half(keyval)
    keyval_far = ring_x(keyval, 2)
    keyval = jnp.concatenate([keyval, other_core(keyval)], axis=0)
    keyval_near = ring_by_core(keyval)
    keyval_pieces = (keyval, keyval_near, other_core(keyval_near))
    keyval_pieces += (keyval_far, other_core(keyval_far))
    q_out, o_in, u_out, d_in, q_bias, u_bias = call(
        turned_kernel,
        1,
        at,
        [(turn(small), None)],
        [
            ((RIDE, 256), bf16, None),
            ((RIDE, 256), bf16, None),
            ((RIDE, 1024), bf16, None),
            ((RIDE, 1024), bf16, None),
            ((1, 256), f32, None),
            ((1, 1024), f32, None),
        ],
        [],
        "turned",
    )
    input_rows = tokens.astype(f32)

    group = (2, 4 * ROWS)
    row_scratch = pltpu.VMEM((2, 4 * ROWS, MODEL_WIDTH), bf16)
    w_scratch = pltpu.VMEM((MODEL_WIDTH, 768), bf16)
    inner_one, inner_far, query, keyval_all, log_total, attended, *out_parts = call(
        attention_kernel,
        2,
        at,
        [
            *flat(normed_places),
            *[(piece, ANY) for piece in keyval_pieces],
            (w, ANY),
            (q_in, None),
            (q_out, None),
            (kv_out, None),
            (o_in, None),
            (q_bias, None),
            (keyval_bias, None),
            (bias, None),
        ],
        [
            ((*group, RIDE), bf16, step_block((4 * ROWS, RIDE))),
            ((*group, RIDE), bf16, step_block((4 * ROWS, RIDE))),
            ((*group, 256), bf16, step_block((4 * ROWS, 256))),
            ((2, 8, ROWS, 256), bf16, step_block((8, ROWS, 256))),
            ((2, 2, 4 * ROWS), f32, step_block((2, 4 * ROWS))),
            ((*group, 256), bf16, step_block((4 * ROWS, 256))),
            *part_outs(MODEL_WIDTH + RIDE),
        ],
        [row_scratch, pltpu.VMEM((2, 4, ROWS, 384), bf16), w_scratch, dma(4)],
        "attention",
        9000000000,
    )
    out_sum = scatter_row(*out_parts)
    output_inner = out_sum[:, MODEL_WIDTH:].astype(bf16)
    middle = (
        input_rows
        + out_sum[:, :MODEL_WIDTH]
        + attention_output_bias.astype(f32)
        + dot(output_inner, o_out)
    )
    normed_two = layer_norm(middle, gain_two, shift_two).astype(bf16)
    place_scratch = pltpu.VMEM((4, 2 * ROWS, MODEL_WIDTH), bf16)
    feed_scratch = pltpu.VMEM((16, ROWS, 1024), bf16)
    up_b, down_a, *feed_parts = call(
        feed_kernel,
        4,
        at,
        [
            *flat(gather_row(normed_two)),
            (cot_all, ANY),
            (feed, ANY),
            (u_in, None),
            (u_out, None),
            (d_in, None),
            (u_bias, None),
        ],
        [
            ((32, 1024), f32, None),
            ((32, 1024), f32, None),
            *part_outs(MODEL_WIDTH + RIDE, True),
            *part_outs(MODEL_WIDTH + RIDE, True),
        ],
        [
            place_scratch,
            pltpu.VMEM((4, 2 * ROWS, MODEL_WIDTH + RIDE), bf16),
            feed_scratch,
            feed_scratch,
            pltpu.VMEM((2 * ROWS, 1024), f32),
            dma(10),
        ],
        "feed",
        19000000000,
    )
    down_parts, up_parts = feed_parts[:4], feed_parts[4:]
    up_parts, down_parts, up_b, down_a = together((up_parts, down_parts, up_b, down_a))
    up_far = scatter_far(*up_parts[2:])
    up_far, up_b, down_a, down_parts = together((up_far, up_b, down_a, down_parts))
    feed_set = row_slice(jnp.concatenate([up_b, down_a], axis=1), core, (1024, 1024))
    up_sides, up_near, feed_set = together(
        (scatter_sides(up_far), add_cores(*up_parts[:2]), feed_set)
    )
    right, left = scatter_joined(up_near, *up_sides)
    right, left, down_parts = together((right, left, down_parts))
    up_moved = ring_x(right, 1), ring_x(left, -1)
    down_far, down_near = scatter_far(*down_parts[2:]), add_cores(*down_parts[:2])
    up_moved, down_far, down_near = together((up_moved, down_far, down_near))
    up_sum = up_near[0] + sum(part.astype(f32) for part in up_moved)
    up_back = up_sum[:, MODEL_WIDTH:].astype(bf16)
    grad_normed_two = up_sum[:, :MODEL_WIDTH] + dot(up_back, u_in)
    _, norm_two_back = jax.vjp(lambda v: layer_norm(v, gain_two, shift_two), middle)
    grad_middle = cotangent.astype(f32) + norm_two_back(grad_normed_two)[0]
    grad_branch = grad_middle.astype(bf16)

    branch_all = lax.all_gather(grad_branch, ("core", "x"), axis=0, tiled=True)
    branch_all = branch_all.reshape(2, 4, ROWS, MODEL_WIDTH)
    middle_slices = slices_of(
        at,
        [(up_back, normed_two), (output_inner, grad_branch)],
        "slices",
    )
    feed_set = jnp.concatenate(
        [
            feed_set,
            total(scatter_sequence(middle_slices)),
            jnp.full((16, 2 * RIDE), mine, jnp.int32).astype(bf16),
        ],
        axis=1,
    )
    down_sides = scatter_sides(down_far)
    feed_column, branch_all, down_sides = together((gather_y(feed_set), branch_all, down_sides))
    right, left = scatter_joined(down_near, *down_sides)
    right, left, branch_all, feed_column = together(
        (right, left, branch_all, jnp.stack(feed_column))
    )
    down_moved = ring_x(right, 1), ring_x(left, -1)
    feed_pieces = gather_z(feed_column)
    query_b, output_a, keyval_b, backs, backs_far, *query_parts = call(
        attention_back_kernel,
        2,
        at,
        [
            (branch_all, ANY),
            (w, ANY),
            (inner_one, step_block((4 * ROWS, RIDE))),
            (inner_far, step_block((4 * ROWS, RIDE))),
            (query, step_block((4 * ROWS, 256))),
            (keyval_all, step_block((8, ROWS, 256))),
            (log_total, step_block((2, 4 * ROWS))),
            (attended, step_block((4 * ROWS, 256))),
            (o_out, None),
            (o_in, None),
            (q_out, None),
            (kv_out, None),
            (bias, None),
        ],
        [
            ((32, 256), f32, None),
            ((32, 256), f32, None),
            ((32, 256), f32, None),
            ((*group, RIDE), bf16, step_block((4 * ROWS, RIDE))),
            ((2, 32, 4 * ROWS), bf16, step_block((32, 4 * ROWS))),
            *part_outs(2688),
        ],
        [
            row_scratch,
            w_scratch,
            pltpu.VMEM((8 * ROWS, HEAD_WIDTH), f32),
            pltpu.VMEM((8 * ROWS, HEAD_WIDTH), f32),
            dma(3),
        ],
        "attention_back",
        8000000000,
    )
    query_b, output_a, keyval_b, backs, backs_far, query_parts, down_moved, feed_pieces = together(
        (query_b, output_a, keyval_b, backs, backs_far, query_parts, down_moved, feed_pieces)
    )
    placed = row_slice(jnp.concatenate([query_b, output_a], axis=1), core, (256, 256))
    query_far, backs_far, placed, down_moved = together(
        (scatter_far(*query_parts[2:]), other_half(backs_far), placed, down_moved)
    )
    down_sum = down_near[0] + sum(part.astype(f32) for part in down_moved)
    down_inner = down_sum[:, MODEL_WIDTH:].astype(bf16)
    layer_output = (
        middle
        + down_sum[:, :MODEL_WIDTH]
        + down_projection_bias.astype(f32)
        + dot(down_inner, d_out)
    ).astype(bf16)
    down_slices = slices_of(at, [(down_inner, cotangent)], "down_slices")
    query_sides = scatter_sides(query_far)
    query_near = add_cores(*query_parts[:2])
    pack_shape = (4, ADAPTER_RANK, 1152)
    late_mine, late_theirs = call(
        late_kernel,
        1,
        at,
        [
            *flat(normed_places),
            (backs, None),
            (backs_far, None),
            (keyval_b, None),
        ],
        [(pack_shape, bf16, None), (pack_shape, bf16, None)],
        [row_scratch, dma(2)],
        "late",
    )
    late_mine, late_theirs, query_near, query_sides, down_slices = together(
        (late_mine, late_theirs, query_near, query_sides, down_slices)
    )
    late_pack = jnp.concatenate(
        [add_cores(late_mine, late_theirs).astype(bf16), down_slices], axis=-1
    )
    right, left = scatter_joined(query_near, *query_sides)
    late_pack, right, left = together((late_pack, right, left))
    query_moved = ring_x(right, 1), ring_x(left, -1)
    late_parts, feed_pieces = together((scatter_sequence(late_pack), feed_pieces))
    late_set = jnp.concatenate([total(late_parts), placed], axis=-1)
    all_ids = jnp.concatenate([piece[:, 0, 5120] for piece in feed_pieces]).astype(jnp.int32)
    feed_kept, feed_sent = sum_by_adapter(feed_pieces, core, all_ids)
    column = gather_y(late_set)
    feed_half = add_cores(feed_kept, feed_sent).astype(bf16)
    column, query_moved, feed_half = together((column, query_moved, feed_half))
    feed_sum = lax.all_gather(feed_half, ("core", "x"), axis=0).reshape(2, 4, 4, 16, 5376)
    late_pieces = gather_z(jnp.stack(column))
    query_sum = query_near[0] + sum(part.astype(f32) for part in query_moved)
    grad_keyval = (
        query_sum[:, 2048:2304] + other_half(query_sum[:, 2304:2560].astype(bf16)).astype(f32)
    ).astype(bf16)
    keyval_back = dot_t(grad_keyval, kv_out)
    keyval_back = jnp.where(jnp.arange(RIDE) // ADAPTER_RANK == 2 + core, keyval_back, 0.0)
    back = (query_sum[:, 2560:] + keyval_back).astype(bf16)
    grad_normed = (
        query_sum[:, :MODEL_WIDTH] + dot(back, q_in) + dot_t(grad_keyval, w[:, 256:512])
    )
    _, norm_one_back = jax.vjp(lambda v: layer_norm(v, gain_one, shift_one), input_rows)
    grad_tokens = (grad_middle + norm_one_back(grad_normed)[0]).astype(bf16)

    late_pieces, grad_tokens = together((late_pieces, grad_tokens))
    kept, sent = sum_by_adapter(late_pieces, core, all_ids)
    own_half = add_cores(kept, sent).astype(bf16)
    other_part = other_core(own_half)
    near = ring_by_core(jnp.concatenate([own_half, other_part], axis=0))
    far = ring_x(own_half, 2)
    feed_grads = spread_out(
        feed_spread_kernel, at, [feed_sum], (1024, 1024, 256, 256), "feed_spread"
    )
    near, far, feed_grads = together((near, far, feed_grads))
    up_b, down_a, up_a, output_b = feed_grads
    query_a, keyval_a, keyval_b, down_b, query_b, output_a = spread_out(
        late_spread_kernel,
        at,
        [own_half, other_part, near, other_core(near), far, other_core(far)],
        (256, 256, 64, 256, 256, 256),
        "late_spread",
    )
    keyval_b = keyval_b.reshape(8, 16, 2, 2, 128).sum(axis=3).reshape(8, 16, 256)

    def side_in(a):
        return jnp.swapaxes(a, 1, 2)

    return (
        layer_output,
        grad_tokens,
        side_in(query_a),
        query_b,
        side_in(keyval_a),
        keyval_b,
        side_in(output_a),
        output_b,
        side_in(up_a),
        up_b,
        side_in(down_a),
        down_b,
    )

def solution(mesh):
    fine = Mesh(mesh.devices.reshape(SIZES), AXES)
    in_specs = (
        P(AXES, None),
        P(AXES, None),
        P(),
        P(),
        P(DP, MP),
        P(MP),
        P(DP, None),
        P(),
        P(MP, DP),
        P(),
        P(),
        P(),
        P(DP, MP),
        P(MP),
        P(MP, DP),
        P(),
        P(DP, None),
        P(),
        P(None, None, MP),
        P(),
        P(),
        P(None, MP, None),
        P(),
        P(),
        P(None, None, MP),
        P(None, MP, None),
        P(),
    )
    out_specs = (P(AXES, None), P(AXES, None)) + (P(),) * 10
    return jax.shard_map(shards, mesh=fine, in_specs=in_specs, out_specs=out_specs, check_vma=False)
```

```python
import functools
import math

import jax
import jax.numpy as jnp
from jax import lax
from jax.experimental import pallas as pl
from jax.experimental.pallas import tpu as pltpu
from jax.sharding import Mesh
from jax.sharding import PartitionSpec as P

MODEL_WIDTH = 2048
H = 16
HEAD_WIDTH = 128
FEED_HIDDEN = 8192
ADAPTER_RANK = 16
ADAPTER_COUNT = 8
BLOCK = 256

AXES = ("y", "zl", "core", "zh", "x")
SIZES = (4, 2, 2, 2, 4)
DP = ("y", "zl", "core")
MP = ("zh", "x")
PLACES = (0, 3, 1, 2)
Z_RING = (0, 2, 1, 3)
ROWS = 128
RIDE = 128

f32 = jnp.float32
bf16 = jnp.bfloat16


together = lax.optimization_barrier


def ring_x(a, step):
    return lax.ppermute(a, "x", [(i, (i + step) % 4) for i in range(4)])


def ring_y(a, step):
    return lax.ppermute(a, "y", [(i, (i + step) % 4) for i in range(4)])


def ring_z(a, step):
    return lax.ppermute(a, ("zl", "zh"), [(Z_RING[i], Z_RING[(i + step) % 4]) for i in range(4)])


def other_core(a):
    return lax.ppermute(a, "core", [(0, 1), (1, 0)])


def other_half(a):
    return lax.ppermute(a, "zh", [(0, 1), (1, 0)])


def turn(a):
    return lax.ppermute(a, ("core", "zh"), [(0, 0), (1, 2), (2, 1), (3, 3)])


def plane_pairs(step, swapped):
    def index(y, z, core):
        return ((y * 2 + z % 2) * 2 + core) * 2 + z // 2

    pairs = []
    for y in range(4):
        for z in range(4):
            for core in range(2):
                if (core == 0) != swapped:
                    to = index((y + step) % 4, z, core)
                else:
                    to = index(y, (z + step) % 4, core)
                pairs.append((index(y, z, core), to))
    return pairs


def gather_cross(a, swapped):
    return [a] + [
        lax.ppermute(a, ("y", "zl", "core", "zh"), plane_pairs(-step, swapped))
        for step in (1, 2, 3)
    ]


def gather_sides(a):
    return a, ring_x(a, 1), ring_x(a, -1)


def gather_rest(a, left, right, near=None):
    half = a.shape[0] // 2
    near = other_core(a) if near is None else near
    top, bottom = ring_x(left[:half], 1), ring_x(right[half:], -1)
    return (
        (a, near),
        (left, other_core(left)),
        (right, other_core(right)),
        (top, bottom, other_core(top), other_core(bottom)),
    )


def gather_row(a):
    near = other_core(a)
    return gather_rest(*gather_sides(a), near)


def add_cores(mine, theirs):
    return mine.astype(f32) + other_core(theirs).astype(f32)


def scatter_far(far_mine, far_theirs):
    return add_cores(far_mine, far_theirs).astype(bf16)


def scatter_sides(far):
    half = far.shape[0] // 2
    return ring_x(far[:half], 1), ring_x(far[half:], -1)


def scatter_joined(near, up, down):
    half = up.shape[0]
    right = jnp.concatenate([near[2, :half] + up.astype(f32), near[2, half:]]).astype(bf16)
    left = jnp.concatenate([near[1, :half], near[1, half:] + down.astype(f32)]).astype(bf16)
    return right, left


def scatter_last(near, up, down):
    right, left = scatter_joined(near, up, down)
    return near[0] + ring_x(right, 1).astype(f32) + ring_x(left, -1).astype(f32)


def scatter_row(mine, theirs, far_mine, far_theirs):
    up, down = scatter_sides(scatter_far(far_mine, far_theirs))
    return scatter_last(add_cores(mine, theirs), up, down)


def scatter_start(mine, theirs, far_mine, far_theirs):
    far = add_cores(far_mine, far_theirs).astype(bf16)
    near = add_cores(mine, theirs)
    return near[0], near[1].astype(bf16), near[2].astype(bf16), far


def gather_y(a):
    return [a, ring_y(a, -1), ring_y(a, 2), ring_y(a, 1)]


def gather_z(a):
    return [a, ring_z(a, -1), ring_z(a, 2), ring_z(a, 1)]


def ring_by_core(a):
    pairs = [(i, (i + 1) % 4) for i in range(4)] + [(4 + i, 4 + (i + 3) % 4) for i in range(4)]
    return lax.ppermute(a, ("core", "x"), pairs)


def by_core(core, own, other):
    return jnp.where(
        core == 0, jnp.concatenate([own, other], -1), jnp.concatenate([other, own], -1)
    )


def row_slice(pair, core, widths):
    own = jnp.where(core == 0, pair[:16], pair[16:]).astype(bf16)
    other = other_core(jnp.where(core == 0, pair[16:], pair[:16]).astype(bf16))
    ends = [sum(widths[:k]) for k in range(1, len(widths))]
    pieces = zip(jnp.split(own, ends, axis=1), jnp.split(other, ends, axis=1))
    return jnp.concatenate([by_core(core, a, b) for a, b in pieces], axis=1)


def scatter_sequence(slices):
    return slices[0], ring_x(slices[1], 1), ring_x(slices[3], -1), ring_x(slices[2], 2)


def total(parts):
    return sum(part.astype(f32) for part in parts).astype(bf16)


def layer_norm(values, gain, shift):
    mean_value = jnp.mean(values, axis=-1, keepdims=True)
    centred = values - mean_value
    variance = jnp.mean(centred * centred, axis=-1, keepdims=True)
    return centred * lax.rsqrt(variance + 1e-05) * gain + shift


def gelu_tanh(values):
    inner_product = math.sqrt(2.0 / math.pi) * (values + 0.044715 * values * values * values)
    return 0.5 * values * (1.0 + jnp.tanh(inner_product))


def pick(adapter_stack, position):
    return lax.dynamic_index_in_dim(adapter_stack, position, 0, keepdims=False)


def dot(left, right):
    return jnp.dot(left, right, preferred_element_type=f32)


def dot_t(left, right):
    return lax.dot_general(left, right, (((1,), (1,)), ((), ())), preferred_element_type=f32)


def tdot(left, right):
    return lax.dot_general(left, right, (((0,), (0,)), ((), ())), preferred_element_type=f32)


def lane_owner(rows, row_core):
    lane = lax.broadcasted_iota(jnp.int32, (rows, RIDE), 1)
    owner = lax.rem(lane // ADAPTER_RANK, 2)
    return jnp.logical_and(owner == row_core, lane < 4 * ADAPTER_RANK)


def place_mask(core):
    row = lax.broadcasted_iota(jnp.int32, (2 * ROWS, RIDE), 0)
    return lane_owner(2 * ROWS, jnp.where(row < ROWS, core, 1 - core))


def copy(source, target, sem):
    pltpu.make_async_copy(source, target, sem).start()


def wait(target, sem):
    pltpu.make_async_copy(target, target, sem).wait()


def copy_place(pieces, target_mine, target_theirs, sem):
    half = ROWS // 2
    if len(pieces) == 2:
        copy(pieces[0], target_mine, sem)
        copy(pieces[1], target_theirs, sem)
    else:
        copy(pieces[0], target_mine.at[pl.ds(0, half)], sem)
        copy(pieces[1], target_mine.at[pl.ds(half, half)], sem)
        copy(pieces[2], target_theirs.at[pl.ds(0, half)], sem)
        copy(pieces[3], target_theirs.at[pl.ds(half, half)], sem)


def split_pieces(refs):
    return (refs[0:2], refs[2:4], refs[4:6], refs[6:10])


def copy_row(gathered, at, target_of, sem_of):
    core, x = at[0], at[1]
    for p in range(4):
        there = lax.rem(x + PLACES[p], 4)
        copy(gathered.at[core, there], target_of(p, 0), sem_of(p, 0))
        copy(gathered.at[1 - core, there], target_of(p, 1), sem_of(p, 1))


def assemble_kernel(at, *refs):
    pieces, (out, sem) = refs[:4], refs[4:]
    core, y, z = at[0], at[3], at[4]
    for far, piece in enumerate(pieces):
        for near in range(4):
            to_y = lax.rem(y + jnp.where(core == 0, near, far), 4)
            to_z = lax.rem(z + jnp.where(core == 0, far, near), 4)
            shard = (to_y * 2 + lax.rem(to_z, 2)) * 2 + to_z // 2
            copy(piece.at[near], out.at[pl.ds(pl.multiple_of(shard * ROWS, ROWS), ROWS)], sem)
    wait(out, sem)


def pack_kernel(at, *refs):
    first = 0
    for part in refs[:-2]:
        refs[-1][:, first : first + part.shape[1]] = part[...]
        first += part.shape[1]
    refs[-1][:, first:] = refs[-2][...].astype(f32).T.astype(bf16)


def norm_kernel(at, rows, gain, shift, out):
    values = layer_norm(
        rows[...].astype(f32), gain[...].astype(f32), shift[...].astype(f32)
    )
    out[...] = values.astype(bf16)


def select_kernel(at, *refs):
    pairs = [refs[2 * n : 2 * n + 2] for n in range(10)]
    q_bias, u_bias = refs[20:22]
    small, q_in, u_in, o_out, d_out, kv_out, bias = refs[22:]
    for out, count in ((q_in, 4), (u_in, 2), (o_out, 2), (d_out, 2)):
        out[16 * count :] = jnp.zeros((RIDE - 16 * count, MODEL_WIDTH), bf16)
    kv_out[...] = jnp.zeros_like(kv_out)
    for c in range(2):
        here, after = slice(16 * c, 16 * c + 16), slice(32 + 16 * c, 48 + 16 * c)
        q_in[here] = pairs[0][c][0]
        q_in[after] = pairs[1][c][0]
        u_in[here] = pairs[2][c][0]
        o_out[here] = pairs[3][c][0]
        d_out[here] = pairs[4][c][0]
        kv_out[after] = pairs[5][c][0]
        first = 0
        for n in range(6, 10):
            width = pairs[n][c].shape[2]
            small[here, first : first + width] = pairs[n][c][0]
            first += width
    small[32:] = jnp.zeros((16, 2560), bf16)
    small[32:33, :256] = q_bias[...]
    small[32:33, 512:1536] = u_bias[...]
    x, zh = at[2], at[3]

    def block_of(place):
        step = jnp.where(place == 0, 0, jnp.where(place == 1, 3, place - 1))
        return ((x + step) & 3) >> 1

    key = lax.broadcasted_iota(jnp.int32, (8, 4 * ROWS), 0)
    query = lax.broadcasted_iota(jnp.int32, (8, 4 * ROWS), 1) >> 7
    own = jnp.logical_and(key < 4, block_of(key) <= block_of(query))
    other = jnp.logical_and(key >= 4, zh == 1)
    bias[...] = jnp.where(jnp.logical_or(own, other), 0.0, -1e30)


def turned_kernel(at, small, q_out, o_in, u_out, d_in, q_bias, u_bias):
    first = 0
    for out in (q_out, o_in, u_out, d_in):
        width = out.shape[1]
        out[:32] = small[:32, first : first + width]
        out[32:] = jnp.zeros((RIDE - 32, width), bf16)
        first += width
    q_bias[...] = small[32:33, :256].astype(f32)
    u_bias[...] = small[32:33, 512:1536].astype(f32)


def own_keyval_kernel(at, rows, w, q_in, kv_out, kv_bias, out):
    inner = dot_t(rows[...], q_in[...])
    lane = lax.broadcasted_iota(jnp.int32, (ROWS, RIDE), 1)
    inner = jnp.where(lane // ADAPTER_RANK == 2 + at[0], inner, 0.0).astype(bf16)
    keyval = dot(rows[...], w[...]) + kv_bias[...] + dot(inner, kv_out[...])
    out[:, :256] = keyval.astype(bf16)
    out[:, 256:] = inner


def sum_kernel(at, *refs):
    pieces, (kept, sent, total) = refs[:-3], refs[-3:]
    total[...] = jnp.zeros_like(total)
    row = 1
    for piece in pieces:
        for k in range(piece.shape[0]):
            total[at[row]] += piece[k].astype(f32)
            row += 1
    kept[...] = total[pl.ds(4 * at[0], 4)].astype(bf16)
    sent[...] = total[pl.ds(4 - 4 * at[0], 4)].astype(bf16)


def slices_kernel(count, at, *refs):
    ins, out = refs[: 2 * count], refs[2 * count]
    x = at[1]
    for n in range(count):
        back, rows = ins[2 * n], ins[2 * n + 1]
        turned = back[...].astype(f32).T
        turned = (turned[:16] + turned[16:32]).astype(bf16)
        product = dot(turned, rows[...]).astype(bf16)
        for to in range(4):
            place = lax.rem(to + 4 - x, 4)
            for c in range(2):
                first = (c * 4 + to) * 256
                lanes = slice(n * 512 + c * 256, n * 512 + (c + 1) * 256)
                out[place, :, lanes] = product[:, first : first + 256]


def spread(scratch, outs, widths):
    x, c = pl.program_id(0), pl.program_id(1)
    first = 0
    for out, width in zip(outs, widths):
        if width < 128:
            part = scratch[x, :, :, first : first + 128].astype(f32)

            @pl.when(jnp.logical_and(c == 0, x % 2 == 0))
            def _(out=out, part=part):
                out[...] = part

            @pl.when(jnp.logical_and(c == 0, x % 2 == 1))
            def _(out=out, part=part):
                out[...] += part

            first += 128
        else:
            here = pl.ds(pl.multiple_of(first + c * width, 128), width)
            out[...] = scratch[x, :, :, here].astype(f32)
            first += 2 * width


def feed_spread_kernel(widths, at, *refs):
    gathered, (scratch, sem) = refs[0], refs[-2:]

    @pl.when((pl.program_id(0) == 0) & (pl.program_id(1) == 0))
    def _():
        for c in range(2):
            for x in range(4):
                copy(gathered.at[c, x], scratch.at[x, pl.ds(4 * c, 4)], sem)
        wait(scratch, sem)

    spread(scratch, refs[1:-2], widths)


def late_spread_kernel(widths, at, *refs):
    own, other, near, near_other, far, far_other = refs[:6]
    scratch, sem = refs[-2:]
    core, x = at[0], at[1]

    @pl.when((pl.program_id(0) == 0) & (pl.program_id(1) == 0))
    def _():
        mine, theirs = pl.ds(4 * core, 4), pl.ds(4 * (1 - core), 4)
        side = lax.rem(x + jnp.where(core == 0, 3, 1), 4)
        other_side = lax.rem(x + jnp.where(core == 0, 1, 3), 4)
        across = lax.rem(x + 2, 4)
        copy(own, scratch.at[x, mine], sem)
        copy(other, scratch.at[x, theirs], sem)
        for part, where in ((0, mine), (1, theirs)):
            copy(near.at[pl.ds(4 * part, 4)], scratch.at[side, where], sem)
        for part, where in ((0, theirs), (1, mine)):
            copy(near_other.at[pl.ds(4 * part, 4)], scratch.at[other_side, where], sem)
        copy(far, scratch.at[across, mine], sem)
        copy(far_other, scratch.at[across, theirs], sem)
        wait(scratch, sem)

    spread(scratch, refs[6:-2], widths)


def copy_rows(rows_in, rows, sems):
    half = ROWS // 2
    for s in range(2):
        for p in range(4):
            pieces = rows_in[p]
            if len(pieces) == 2:
                copy(pieces[s], rows.at[s, pl.ds(p * ROWS, ROWS)], sems.at[s])
            else:
                for n in range(2):
                    here = pl.ds(p * ROWS + n * half, half)
                    copy(pieces[2 * s + n], rows.at[s, here], sems.at[s])


def attention_kernel(at, *refs):
    rows_in = split_pieces(refs[:10])
    kv_in = refs[10:15]
    w, q_in, q_out, kv_out, o_in, q_bias, kv_bias, bias = refs[15:23]
    inner_out, inner_far, query_out, kv_all, lse_out, att_out = refs[23:29]
    parts, far_parts = refs[29:31], refs[31:33]
    rows, kvs, ws, sems = refs[33:]
    s = pl.program_id(0)
    core = at[0]

    @pl.when(s == 0)
    def _():
        copy(w, ws, sems.at[2])
        copy_rows(rows_in, rows, sems)
        pair, near, near_other, far, far_other = kv_in
        first, second = pl.ds(0, ROWS), pl.ds(ROWS, ROWS)
        side = jnp.where(core == 0, 1, 2)
        copy(pair.at[first], kvs.at[0, 0], sems.at[3])
        copy(pair.at[second], kvs.at[1, 0], sems.at[3])
        copy(near.at[first], kvs.at[0, side], sems.at[3])
        copy(near.at[second], kvs.at[1, side], sems.at[3])
        copy(near_other.at[first], kvs.at[1, 3 - side], sems.at[3])
        copy(near_other.at[second], kvs.at[0, 3 - side], sems.at[3])
        copy(far, kvs.at[0, 3], sems.at[3])
        copy(far_other, kvs.at[1, 3], sems.at[3])
        wait(ws, sems.at[2])
        wait(kvs, sems.at[3])

    wait(rows.at[s], sems.at[s])

    owner = lane_owner(4 * ROWS, jnp.where(s == 0, core, 1 - core))
    x = rows[s]
    inner = jnp.where(owner, dot_t(x, q_in[...]), 0.0).astype(bf16)
    inner_out[0] = inner
    query = (dot(x, ws[:, :256]) + q_bias[...] + dot(inner, q_out[...])).astype(bf16)
    query_out[0] = query
    kv_own = (dot(x, ws[:, 256:512]) + kv_bias[...] + dot(inner, kv_out[...])).astype(bf16)
    inner_far[0] = kvs[s, :, :, 256:].reshape(4 * ROWS, RIDE)
    kv = jnp.concatenate([kv_own.reshape(4, ROWS, 256), kvs[s, :, :, :256]], axis=0)
    kv_all[0] = kv
    keys = kv[:, :, :HEAD_WIDTH].reshape(8 * ROWS, HEAD_WIDTH)
    values_t = kv[:, :, HEAD_WIDTH:].reshape(8 * ROWS, HEAD_WIDTH).astype(f32).T.astype(bf16)
    columns = []
    for h in range(2):
        chunks = []
        for c in range(2):
            lanes = slice(c * 256, c * 256 + 256)
            q = query[lanes, h * HEAD_WIDTH : (h + 1) * HEAD_WIDTH]
            scores = dot_t(keys, q) * (HEAD_WIDTH**-0.5)
            scores = scores.reshape(8, ROWS, 256) + bias[:, lanes][:, None, :]
            scores = scores.reshape(8 * ROWS, 256)
            top = jnp.max(scores, axis=0, keepdims=True)
            expo = jnp.exp(scores - top)
            total = jnp.sum(expo, axis=0, keepdims=True)
            probs = (expo * (1.0 / total)).astype(bf16)
            lse_out[0, h : h + 1, lanes] = top + jnp.log(total)
            chunks.append(dot(values_t, probs).T)
        columns.append(jnp.concatenate(chunks, axis=0))
    attended = jnp.concatenate(columns, axis=1).astype(bf16)
    att_out[0] = attended
    low = jnp.where(owner, dot_t(attended, o_in[...]), 0.0).astype(bf16)
    for which in range(2):

        @pl.when(s == which)
        def _(which=which):
            for p in range(4):
                here = slice(p * ROWS, (p + 1) * ROWS)
                part = parts[which].at[p] if p < 3 else far_parts[which]
                part[:, :MODEL_WIDTH] = dot_t(attended[here], ws[:, 512:]).astype(bf16)
                part[:, MODEL_WIDTH:] = low[here]


def store_parts(p, parts, far_parts, out, low):
    for which in range(2):
        here = slice(which * ROWS, (which + 1) * ROWS)

        @pl.when(p < 3)
        def _(which=which, here=here):
            parts[which][0, :, :MODEL_WIDTH] = out[here]
            parts[which][0, :, MODEL_WIDTH:] = low[here]

        @pl.when(p == 3)
        def _(which=which, here=here):
            far_parts[which][:, :MODEL_WIDTH] = out[here]
            far_parts[which][:, MODEL_WIDTH:] = low[here]


def feed_kernel(at, *refs):
    rows_in = split_pieces(refs[:10])
    cot, feed, u_in, u_out, d_in, u_bias = refs[10:16]
    placed = refs[16]
    up_b, down_a = placed.at[:, pl.ds(0, 1024)], placed.at[:, pl.ds(1024, 1024)]
    down_parts, down_far = refs[17:19], refs[19:21]
    up_parts, up_far = refs[21:23], refs[23:25]
    rows, grads, up, down, slopes, sems = refs[25:]
    p = pl.program_id(0)
    core = at[0]

    @pl.when(p == 0)
    def _():
        copy_place(rows_in[0], rows.at[0, pl.ds(0, ROWS)], rows.at[0, pl.ds(ROWS, ROWS)], sems.at[0])
        copy(feed.at[:, core, :, pl.ds(0, 1024)], up, sems.at[8])
        copy(feed.at[:, core, :, pl.ds(1024, 1024)], down, sems.at[9])
        copy_row(
            cot,
            at,
            lambda k, which: grads.at[k, pl.ds(which * ROWS, ROWS)],
            lambda k, which: sems.at[4 + k],
        )
        for k in range(1, 4):
            copy_place(
                rows_in[k], rows.at[k, pl.ds(0, ROWS)], rows.at[k, pl.ds(ROWS, ROWS)], sems.at[k]
            )
        placed[...] = jnp.zeros_like(placed)
        wait(up, sems.at[8])

    wait(rows.at[p], sems.at[p])
    mask = place_mask(core)
    x = rows[p]
    inner = jnp.where(mask, dot_t(x, u_in[...]), 0.0)
    inner_t, inner = inner.T[:32].astype(bf16), inner.astype(bf16)
    pre = dot(x, up[...].reshape(MODEL_WIDTH, 1024)) + u_bias[...] + dot(inner, u_out[...])
    k0 = math.sqrt(2.0 / math.pi)
    square = pre * pre
    bend = jnp.tanh(k0 * (pre + 0.044715 * square * pre))
    act = (0.5 * pre * (1.0 + bend)).astype(bf16)
    slopes[...] = 0.5 * (1.0 + bend) + 0.5 * pre * (1.0 - bend * bend) * (
        k0 * (1.0 + 3.0 * 0.044715 * square)
    )

    @pl.when(p == 0)
    def _():
        wait(down, sems.at[9])

    low = jnp.where(mask, dot_t(act, d_in[...]), 0.0).astype(bf16)
    out = dot_t(act, down[...].reshape(MODEL_WIDTH, 1024)).astype(bf16)
    store_parts(p, down_parts, down_far, out, low)

    wait(grads.at[p], sems.at[4 + p])
    grad, back = grads[p, :, :MODEL_WIDTH], grads[p, :, MODEL_WIDTH:]
    down_a[...] += dot(back.astype(f32).T[:32].astype(bf16), act)
    grad_act = dot(grad, down[...].reshape(MODEL_WIDTH, 1024)) + dot(back, d_in[...])
    grad_pre = (grad_act * slopes[...]).astype(bf16)
    up_b[...] += dot(inner_t, grad_pre)
    low = jnp.where(mask, dot_t(grad_pre, u_out[...]), 0.0).astype(bf16)
    out = dot_t(grad_pre, up[...].reshape(MODEL_WIDTH, 1024)).astype(bf16)
    store_parts(p, up_parts, up_far, out, low)


def late_kernel(at, *refs):
    rows_in = split_pieces(refs[:10])
    backs, backs_far, keyval_b, cotangent = refs[10:14]
    down_parts = refs[14:18]
    outs, (rows, sems) = refs[18:20], refs[20:]
    core, x = at[0], at[1]
    copy_rows(rows_in, rows, sems)
    inner = sum(part[...].astype(f32) for part in down_parts).T
    inner = (inner[:16] + inner[16:32]).astype(bf16)
    down_b = dot(inner, cotangent[...]).astype(bf16)
    for to in range(4):
        place = lax.rem(to + 4 - x, 4)
        for c in range(2):
            begin = (c * 4 + to) * 256
            lanes = slice(1152 + c * 256, 1152 + (c + 1) * 256)
            outs[0][place, :, lanes] = down_b[:, begin : begin + 256]
    product = jnp.zeros((64, MODEL_WIDTH), f32)
    for s in range(2):
        wait(rows.at[s], sems.at[s])
        back = backs[s].astype(f32).T
        back = jnp.concatenate([back[:32], back[32:64] + backs_far[s].astype(f32)], axis=0)
        product += dot(back.astype(bf16), rows[s])
    first, second = keyval_b[:16], keyval_b[16:]
    lane = lax.broadcasted_iota(jnp.int32, (ADAPTER_RANK, RIDE), 1) // 64
    for which in range(2):
        out = outs[which]
        is_first = (core == 0) if which == 0 else (core != 0)
        for n in range(2):
            both = product[32 * n : 32 * n + 32]
            picked = jnp.where(is_first, both[:16], both[16:]).astype(bf16)
            for to in range(4):
                place = lax.rem(to + 4 - x, 4)
                for c in range(2):
                    begin = (c * 4 + to) * 256
                    lanes = slice(n * 512 + c * 256, n * 512 + (c + 1) * 256)
                    out[place, :, lanes] = picked[:, begin : begin + 256]
        picked = jnp.where(is_first, first, second).astype(bf16)
        for to in range(4):
            place = lax.rem(to + 4 - x, 4)
            part = picked[:, (to // 2) * 128 : (to // 2) * 128 + 128]
            out[place, :, 1024:1152] = jnp.where(lane == to % 2, part, jnp.zeros_like(part))


def attention_back_kernel(at, *refs):
    branch, w, inner_in, inner_far, query_in, kv_in, lse_in, att_in = refs[:8]
    o_out, o_in, q_out, kv_out, bias = refs[8:13]
    placed, keyval_b, backs, backs_far = refs[13:17]
    query_b, output_a = placed.at[:, pl.ds(0, 256)], placed.at[:, pl.ds(256, 256)]
    parts, far_parts = refs[17:19], refs[19:21]
    rows, ws, grad_k, grad_v, sems = refs[21:]
    s = pl.program_id(0)
    core = at[0]

    @pl.when(s == 0)
    def _():
        copy(w, ws, sems.at[2])
        copy_row(
            branch,
            at,
            lambda p, which: rows.at[which, pl.ds(p * ROWS, ROWS)],
            lambda p, which: sems.at[which],
        )
        placed[...] = jnp.zeros_like(placed)
        keyval_b[...] = jnp.zeros_like(keyval_b)
        wait(ws, sems.at[2])

    wait(rows.at[s], sems.at[s])

    owner = lane_owner(4 * ROWS, jnp.where(s == 0, core, 1 - core))
    scale = HEAD_WIDTH**-0.5
    x = rows[s]
    back = jnp.where(owner, dot_t(x, o_out[...]), 0.0)
    output_a[...] += dot(back.T[:32].astype(bf16), att_in[0])
    grad_att = (dot(x, ws[:, 512:]) + dot(back.astype(bf16), o_in[...])).astype(bf16)
    query = query_in[0]
    kv = kv_in[0]
    keys = kv[:, :, :HEAD_WIDTH].reshape(8 * ROWS, HEAD_WIDTH)
    values = kv[:, :, HEAD_WIDTH:].reshape(8 * ROWS, HEAD_WIDTH)
    keys_t = keys.astype(f32).T.astype(bf16)
    columns = []
    for h in range(2):
        chunks = []
        for c in range(2):
            lanes = slice(c * 256, c * 256 + 256)
            head = slice(h * HEAD_WIDTH, (h + 1) * HEAD_WIDTH)
            q, g = query[lanes, head], grad_att[lanes, head]
            scores = dot_t(keys, q) * scale
            scores = scores.reshape(8, ROWS, 256) + bias[:, lanes][:, None, :]
            probs = jnp.exp(scores.reshape(8 * ROWS, 256) - lse_in[0, h : h + 1, lanes])
            grad_probs = dot_t(values, g)
            delta = jnp.sum(probs * grad_probs, axis=0, keepdims=True)
            grad_scores = (probs * (grad_probs - delta)).astype(bf16)
            chunks.append((dot(keys_t, grad_scores) * scale).T)
            more_k = dot(grad_scores, q) * scale
            more_v = dot(probs.astype(bf16), g)
            if h == 0 and c == 0:
                grad_k[...] = more_k
                grad_v[...] = more_v
            else:
                grad_k[...] += more_k
                grad_v[...] += more_v
        columns.append(jnp.concatenate(chunks, axis=0))
    grad_query = jnp.concatenate(columns, axis=1).astype(bf16)
    inner_t = inner_in[0].astype(f32).T
    query_b[...] += dot(inner_t[:32].astype(bf16), grad_query)
    low = jnp.where(owner, dot_t(grad_query, q_out[...]), 0.0).astype(bf16)
    grad_kv = jnp.concatenate([grad_k[...], grad_v[...]], axis=1).astype(bf16)
    own_kv, far_kv = grad_kv[: 4 * ROWS], grad_kv[4 * ROWS :]
    keyval_b[...] += dot(inner_t[32:64].astype(bf16), own_kv)
    keyval_b[...] += dot(inner_far[0].astype(f32).T[32:64].astype(bf16), far_kv)
    backs[0] = low + jnp.where(owner, dot_t(own_kv, kv_out[...]), 0.0).astype(bf16)
    backs_far[0] = jnp.where(owner, dot_t(far_kv, kv_out[...]), 0.0).T[32:64].astype(bf16)
    for which in range(2):

        @pl.when(s == which)
        def _(which=which):
            for p in range(4):
                here = slice(p * ROWS, (p + 1) * ROWS)
                part = parts[which].at[p] if p < 3 else far_parts[which]
                part[:, :2048] = dot_t(grad_query[here], ws[:, :256]).astype(bf16)
                part[:, 2048:2304] = own_kv[here]
                part[:, 2304:2560] = far_kv[here]
                part[:, 2560:] = low[here]


VMEM_LIMIT = 56 * 1024 * 1024
ANY = pl.BlockSpec(memory_space=pl.ANY)


def whole_block(shape):
    return pl.BlockSpec(shape, lambda i, at: (0,) * len(shape))


def step_block(shape):
    return pl.BlockSpec((1, *shape), lambda i, at: (i,) + (0,) * len(shape))


def call(kernel, steps, at, ins, outs, scratch, name, flops=0, short=False):
    arrays = [a for a, _ in ins]
    in_specs = [whole_block(a.shape) if b is None else b for a, b in ins]
    out_specs = [whole_block(s) if b is None else b for s, _, b in outs]
    return pl.pallas_call(
        kernel,
        out_shape=[jax.ShapeDtypeStruct(s, d) for s, d, _ in outs],
        grid_spec=pltpu.PrefetchScalarGridSpec(
            num_scalar_prefetch=1,
            grid=(steps,),
            in_specs=in_specs,
            out_specs=out_specs,
            scratch_shapes=scratch,
        ),
        compiler_params=pltpu.CompilerParams(vmem_limit_bytes=VMEM_LIMIT),
        cost_estimate=pl.CostEstimate(
            flops=0 if short else flops,
            bytes_accessed=0
            if short
            else sum(a.size * a.dtype.itemsize for a in arrays)
            + sum(math.prod(s) * 4 for s, _, _ in outs),
            transcendentals=0,
        ),
        name=name,
    )(at, *arrays)


def flat(places):
    return [(piece, ANY) for place in places for piece in place]


def part_outs(width, steps=False):
    block = pl.BlockSpec((1, ROWS, width), lambda i, at: (jnp.minimum(i, 2), 0, 0))
    near = ((3, ROWS, width), bf16, block if steps else None)
    return [near, near, ((ROWS, width), bf16, None), ((ROWS, width), bf16, None)]


def dma(n):
    return pltpu.SemaphoreType.DMA((n,))


def sum_by_adapter(pieces, core, ids):
    width = pieces[0].shape[-1]
    block = max(w for w in range(128, 3713, 128) if width % w == 0)
    half = (ADAPTER_COUNT // 2, ADAPTER_RANK)
    return pl.pallas_call(
        sum_kernel,
        out_shape=[jax.ShapeDtypeStruct((*half, width), bf16)] * 2,
        grid_spec=pltpu.PrefetchScalarGridSpec(
            num_scalar_prefetch=1,
            grid=(width // block,),
            in_specs=[
                pl.BlockSpec((p.shape[0], ADAPTER_RANK, block), lambda i, at: (0, 0, i))
                for p in pieces
            ],
            out_specs=[pl.BlockSpec((*half, block), lambda i, at: (0, 0, i))] * 2,
            scratch_shapes=[pltpu.VMEM((ADAPTER_COUNT, ADAPTER_RANK, block), f32)],
        ),
        compiler_params=pltpu.CompilerParams(vmem_limit_bytes=VMEM_LIMIT),
        name="sum_by_adapter",
    )(jnp.concatenate([jnp.reshape(core, (1,)), ids]).astype(jnp.int32), *pieces)


def spread_out(kernel, at, pieces, widths, name):
    total = pieces[0].shape[-1]
    blocks = [
        (w, lambda i, j, at: (0, 0, j * 4 + i)) if w >= 128 else (128, lambda i, j, at: (0, 0, i // 2))
        for w in widths
    ]
    return pl.pallas_call(
        functools.partial(kernel, widths),
        out_shape=[
            jax.ShapeDtypeStruct((ADAPTER_COUNT, ADAPTER_RANK, 8 * w if w >= 128 else 256), f32)
            for w in widths
        ],
        grid_spec=pltpu.PrefetchScalarGridSpec(
            num_scalar_prefetch=1,
            grid=(4, 2),
            in_specs=[ANY] * len(pieces),
            out_specs=[pl.BlockSpec((ADAPTER_COUNT, ADAPTER_RANK, w), m) for w, m in blocks],
            scratch_shapes=[
                pltpu.VMEM((4, ADAPTER_COUNT, ADAPTER_RANK, total), bf16),
                pltpu.SemaphoreType.DMA,
            ],
        ),
        compiler_params=pltpu.CompilerParams(vmem_limit_bytes=VMEM_LIMIT),
        name=name,
    )(at, *pieces)


def slices_of(at, pairs, name):
    shape = (4, ADAPTER_RANK, 512 * len(pairs))
    ins = [(a, None) for pair in pairs for a in pair]
    kernel = functools.partial(slices_kernel, len(pairs))
    return call(kernel, 1, at, ins, [(shape, bf16, None)], [], name)[0]


def shards(
    tokens,
    cotangent,
    attention_norm_scale,
    attention_norm_bias,
    query_projection,
    query_projection_bias,
    keyvalue_projection,
    value_projection_bias,
    attention_output_weight,
    attention_output_bias,
    feedforward_norm_scale,
    feedforward_norm_bias,
    up_projection_weight,
    up_projection_bias,
    down_projection_weight,
    down_projection_bias,
    sequence_adapter,
    query_adapter_input,
    query_adapter_output,
    keyvalue_adapter_input,
    keyvalue_adapter_output,
    output_adapter_input,
    output_adapter_output,
    up_adapter_input,
    up_adapter_output,
    down_adapter_input,
    down_adapter_output,
):
    y, core, zl, zh, x = (lax.axis_index(n) for n in ("y", "core", "zl", "zh", "x"))
    z = zh * 2 + zl
    at = jnp.stack([core, x, zh, y, z]).astype(jnp.int32)
    gain_one, shift_one = attention_norm_scale.astype(f32), attention_norm_bias.astype(f32)
    gain_two, shift_two = feedforward_norm_scale.astype(f32), feedforward_norm_bias.astype(f32)

    def pack(*parts):
        width = sum(part.shape[1] for part in parts[:-1]) + parts[-1].shape[0]
        ins = [(part, None) for part in parts]
        return call(pack_kernel, 1, at, ins, [((ROWS, width), bf16, None)], [], "pack")[0]

    mine = sequence_adapter[0, 0]
    attention_shard = pack(query_projection, keyvalue_projection, attention_output_weight)
    attention_shard, cotangent = together((attention_shard, cotangent))
    down_back = dot_t(cotangent, pick(down_adapter_output, mine)).astype(bf16)
    down_back = jnp.pad(down_back, ((0, 0), (0, RIDE - 16)))
    down_back = jnp.where(core == 0, down_back, jnp.roll(down_back, 16, axis=1))
    cot_all = jnp.concatenate([cotangent, down_back], axis=1)
    cot_all = lax.all_gather(cot_all, ("core", "x"), axis=0, tiled=True)
    cot_all = cot_all.reshape(2, 4, ROWS, MODEL_WIDTH + RIDE)

    attention_shard = turn(attention_shard)
    feed_shard = pack(up_projection_weight, down_projection_weight)
    attention_shard, feed_shard, sequence_adapter, tokens = together(
        (attention_shard, feed_shard, sequence_adapter, tokens)
    )
    theirs = other_core(sequence_adapter)[0, 0]
    rows_shape = ((ROWS, MODEL_WIDTH), bf16, None)
    normed = call(
        norm_kernel,
        1,
        at,
        [(tokens, None), (attention_norm_scale[None], None), (attention_norm_bias[None], None)],
        [rows_shape],
        [],
        "norm",
    )[0]
    column, mine, theirs, normed = together(
        (gather_cross(attention_shard, False), mine, theirs, normed)
    )
    plane = gather_cross(jnp.stack(column), True)
    normed_sides = gather_sides(normed)

    low = jnp.where(core == 0, mine, theirs)
    high = jnp.where(core == 0, theirs, mine)
    stacks = (
        jnp.swapaxes(query_adapter_input, 1, 2),
        jnp.swapaxes(keyvalue_adapter_input, 1, 2),
        jnp.swapaxes(up_adapter_input, 1, 2),
        output_adapter_output,
        down_adapter_output,
        keyvalue_adapter_output,
        query_adapter_output,
        jnp.swapaxes(output_adapter_input, 1, 2),
        up_adapter_output,
        jnp.swapaxes(down_adapter_input, 1, 2),
    )
    chosen = []
    for stack in stacks:
        block = (1, ADAPTER_RANK, stack.shape[2])
        chosen.append((stack, pl.BlockSpec(block, lambda i, at: (at[0], 0, 0))))
        chosen.append((stack, pl.BlockSpec(block, lambda i, at: (at[1], 0, 0))))
    wide = ((RIDE, MODEL_WIDTH), bf16, None)
    small, q_in, u_in, o_out, d_out, kv_out, bias = call(
        select_kernel,
        1,
        jnp.stack([low, high, x, zh]).astype(jnp.int32),
        [*chosen, (query_projection_bias[None], None), (up_projection_bias[None], None)],
        [
            ((48, 2560), bf16, None),
            wide,
            wide,
            wide,
            wide,
            ((RIDE, 256), bf16, None),
            ((8, 4 * ROWS), f32, None),
        ],
        [],
        "select",
    )
    keyval_bias = jnp.concatenate(
        [jnp.zeros((1, HEAD_WIDTH), f32), value_projection_bias.astype(f32)[None]], axis=1
    )
    prepared = (q_in, u_in, o_out, d_out, kv_out, bias, keyval_bias, small)
    plane, normed_sides, prepared = together((plane, normed_sides, prepared))
    q_in, u_in, o_out, d_out, kv_out, bias, keyval_bias, small = prepared
    normed_places = gather_rest(*normed_sides)
    (w,) = call(
        assemble_kernel,
        1,
        at,
        [(piece, ANY) for piece in plane],
        [((MODEL_WIDTH, 768), bf16, None)],
        [pltpu.SemaphoreType.DMA],
        "assemble",
    )
    feed_shard, w, cot_all = together((feed_shard, w, cot_all))
    feed = lax.all_gather(feed_shard, DP + ("zh",), axis=0, tiled=True)
    feed = feed.reshape(16, 2, ROWS, 2048)

    w_keyval = pl.BlockSpec((MODEL_WIDTH, 256), lambda i, at: (0, 1))
    keyval = call(
        own_keyval_kernel,
        1,
        at,
        [(normed, None), (w, w_keyval), (q_in, None), (kv_out, None), (keyval_bias, None)],
        [((ROWS, 384), bf16, None)],
        [],
        "own_keyval",
    )[0]
    keyval = other_half(keyval)
    keyval_far = ring_x(keyval, 2)
    turned = call(
        turned_kernel,
        1,
        at,
        [(turn(small), None)],
        [
            ((RIDE, 256), bf16, None),
            ((RIDE, 256), bf16, None),
            ((RIDE, 1024), bf16, None),
            ((RIDE, 1024), bf16, None),
            ((1, 256), f32, None),
            ((1, 1024), f32, None),
        ],
        [],
        "turned",
    )
    keyval_pair = jnp.concatenate([keyval, other_core(keyval)], axis=0)
    keyval_pair, turned = together((keyval_pair, turned))
    q_out, o_in, u_out, d_in, q_bias, u_bias = turned
    keyval = keyval_pair
    keyval_near = ring_by_core(keyval)
    keyval_pieces = (keyval, keyval_near, other_core(keyval_near))
    keyval_pieces += (keyval_far, other_core(keyval_far))
    input_rows = tokens.astype(f32)

    group = (2, 4 * ROWS)
    row_scratch = pltpu.VMEM((2, 4 * ROWS, MODEL_WIDTH), bf16)
    w_scratch = pltpu.VMEM((MODEL_WIDTH, 768), bf16)
    inner_one, inner_far, query, keyval_all, log_total, attended, *out_parts = call(
        attention_kernel,
        2,
        at,
        [
            *flat(normed_places),
            *[(piece, ANY) for piece in keyval_pieces],
            (w, ANY),
            (q_in, None),
            (q_out, None),
            (kv_out, None),
            (o_in, None),
            (q_bias, None),
            (keyval_bias, None),
            (bias, None),
        ],
        [
            ((*group, RIDE), bf16, step_block((4 * ROWS, RIDE))),
            ((*group, RIDE), bf16, step_block((4 * ROWS, RIDE))),
            ((*group, 256), bf16, step_block((4 * ROWS, 256))),
            ((2, 8, ROWS, 256), bf16, step_block((8, ROWS, 256))),
            ((2, 2, 4 * ROWS), f32, step_block((2, 4 * ROWS))),
            ((*group, 256), bf16, step_block((4 * ROWS, 256))),
            *part_outs(MODEL_WIDTH + RIDE),
        ],
        [row_scratch, pltpu.VMEM((2, 4, ROWS, 384), bf16), w_scratch, dma(4)],
        "attention",
        9000000000,
    )
    out_sum = scatter_row(*out_parts)
    output_inner = out_sum[:, MODEL_WIDTH:].astype(bf16)
    middle = (
        input_rows
        + out_sum[:, :MODEL_WIDTH]
        + attention_output_bias.astype(f32)
        + dot(output_inner, o_out)
    )
    normed_two = layer_norm(middle, gain_two, shift_two).astype(bf16)
    place_scratch = pltpu.VMEM((4, 2 * ROWS, MODEL_WIDTH), bf16)
    feed_scratch = pltpu.VMEM((16, ROWS, 1024), bf16)
    feed_placed, *feed_parts = call(
        feed_kernel,
        4,
        at,
        [
            *flat(gather_row(normed_two)),
            (cot_all, ANY),
            (feed, ANY),
            (u_in, None),
            (u_out, None),
            (d_in, None),
            (u_bias, None),
        ],
        [
            ((32, 2048), f32, None),
            *part_outs(MODEL_WIDTH + RIDE, True),
            *part_outs(MODEL_WIDTH + RIDE, True),
        ],
        [
            place_scratch,
            pltpu.VMEM((4, 2 * ROWS, MODEL_WIDTH + RIDE), bf16),
            feed_scratch,
            feed_scratch,
            pltpu.VMEM((2 * ROWS, 1024), f32),
            dma(10),
        ],
        "feed",
        19000000000,
    )
    down_parts, up_parts = feed_parts[:4], feed_parts[4:]
    up_parts, down_parts, feed_placed = together((up_parts, down_parts, feed_placed))
    up_far = scatter_far(*up_parts[2:])
    up_far, feed_placed, down_parts = together((up_far, feed_placed, down_parts))
    feed_set = row_slice(feed_placed, core, (1024, 1024))
    up_sides, up_near, feed_set = together(
        (scatter_sides(up_far), add_cores(*up_parts[:2]), feed_set)
    )
    right, left = scatter_joined(up_near, *up_sides)
    right, left, down_parts = together((right, left, down_parts))
    up_moved = ring_x(right, 1), ring_x(left, -1)
    down_low = scatter_start(*down_parts)
    up_moved, down_low = together((up_moved, down_low))
    up_sum = up_near[0] + sum(part.astype(f32) for part in up_moved)
    up_back = up_sum[:, MODEL_WIDTH:].astype(bf16)
    grad_normed_two = up_sum[:, :MODEL_WIDTH] + dot(up_back, u_in)
    _, norm_two_back = jax.vjp(lambda v: layer_norm(v, gain_two, shift_two), middle)
    grad_middle = cotangent.astype(f32) + norm_two_back(grad_normed_two)[0]
    grad_branch = grad_middle.astype(bf16)

    branch_all = lax.all_gather(grad_branch, ("core", "x"), axis=0, tiled=True)
    branch_all = branch_all.reshape(2, 4, ROWS, MODEL_WIDTH)
    middle_slices = slices_of(
        at,
        [(up_back, normed_two), (output_inner, grad_branch)],
        "slices",
    )
    feed_set = jnp.concatenate(
        [
            feed_set,
            total(scatter_sequence(middle_slices)),
            jnp.full((16, 2 * RIDE), mine, jnp.int32).astype(bf16),
        ],
        axis=1,
    )
    feed_column, down_low = together((gather_y(feed_set), down_low))
    feed_column = jnp.stack(feed_column)
    feed_sides = ring_z(feed_column, -1), ring_z(feed_column, 1)
    down_moved = (ring_x(down_low[1], -1), ring_x(down_low[2], 1), ring_x(down_low[3], 2))
    placed, keyval_b, backs, backs_far, *query_parts = call(
        attention_back_kernel,
        2,
        at,
        [
            (branch_all, ANY),
            (w, ANY),
            (inner_one, step_block((4 * ROWS, RIDE))),
            (inner_far, step_block((4 * ROWS, RIDE))),
            (query, step_block((4 * ROWS, 256))),
            (keyval_all, step_block((8, ROWS, 256))),
            (log_total, step_block((2, 4 * ROWS))),
            (attended, step_block((4 * ROWS, 256))),
            (o_out, None),
            (o_in, None),
            (q_out, None),
            (kv_out, None),
            (bias, None),
        ],
        [
            ((32, 512), f32, None),
            ((32, 256), f32, None),
            ((*group, RIDE), bf16, step_block((4 * ROWS, RIDE))),
            ((2, 32, 4 * ROWS), bf16, step_block((32, 4 * ROWS))),
            *part_outs(2688),
        ],
        [
            row_scratch,
            w_scratch,
            pltpu.VMEM((8 * ROWS, HEAD_WIDTH), f32),
            pltpu.VMEM((8 * ROWS, HEAD_WIDTH), f32),
            dma(3),
        ],
        "attention_back",
        short=True,
    )
    placed, keyval_b, backs, backs_far, query_parts, down_moved, feed_sides = together(
        (placed, keyval_b, backs, backs_far, query_parts, down_moved, feed_sides)
    )
    query_far, backs_far, placed, feed_column = together(
        (scatter_far(*query_parts[2:]), other_half(backs_far), placed, feed_column)
    )
    feed_far = ring_z(feed_column, 2)
    query_sides = scatter_sides(query_far)
    query_near = add_cores(*query_parts[:2])
    pack_shape = (4, ADAPTER_RANK, 1152)
    ride_block = pl.BlockSpec((ROWS, RIDE), lambda i, at: (0, MODEL_WIDTH // RIDE))
    late_mine, late_theirs = call(
        late_kernel,
        1,
        at,
        [
            *flat(normed_places),
            (backs, None),
            (backs_far, None),
            (keyval_b, None),
            (cotangent, None),
            *[(part, ride_block) for part in (down_low[0], *down_moved)],
        ],
        [((4, ADAPTER_RANK, 1664), bf16, None), (pack_shape, bf16, None)],
        [row_scratch, dma(2)],
        "late",
    )
    late_mine, late_theirs, query_near, query_sides = together(
        (late_mine, late_theirs, query_near, query_sides)
    )
    late_pack = add_cores(late_mine[..., :1152], late_theirs).astype(bf16)
    late_pack = jnp.concatenate([late_pack, late_mine[..., 1152:]], axis=-1)
    right, left = scatter_joined(query_near, *query_sides)
    late_pack, right, left = together((late_pack, right, left))
    query_moved = ring_x(right, 1), ring_x(left, -1)
    late_parts, feed_far, feed_column, feed_sides, down_moved = together(
        (scatter_sequence(late_pack), feed_far, feed_column, feed_sides, down_moved)
    )
    down_sum = down_low[0] + sum(part.astype(f32) for part in down_moved)
    placed = row_slice(placed, core, (256, 256))
    down_inner = down_sum[:, MODEL_WIDTH:].astype(bf16)
    layer_output = (
        middle
        + down_sum[:, :MODEL_WIDTH]
        + down_projection_bias.astype(f32)
        + dot(down_inner, d_out)
    ).astype(bf16)
    feed_pieces = [feed_column, feed_sides[0], feed_far, feed_sides[1]]
    late_set = jnp.concatenate([total(late_parts), placed], axis=-1)
    names = together(jnp.concatenate([piece[:, :1, 5120:5248] for piece in feed_pieces]))
    all_ids = names[:, 0, 0].astype(jnp.int32)
    feed_kept, feed_sent = sum_by_adapter(feed_pieces, core, all_ids)
    column = gather_y(late_set)
    feed_half = add_cores(feed_kept, feed_sent).astype(bf16)
    column, query_moved, feed_half = together((column, query_moved, feed_half))
    feed_sum = lax.all_gather(feed_half, ("core", "x"), axis=0).reshape(2, 4, 4, 16, 5376)
    late_pieces = gather_z(jnp.stack(column))
    query_sum = query_near[0] + sum(part.astype(f32) for part in query_moved)
    grad_keyval = (
        query_sum[:, 2048:2304] + other_half(query_sum[:, 2304:2560].astype(bf16)).astype(f32)
    ).astype(bf16)
    keyval_back = dot_t(grad_keyval, kv_out)
    keyval_back = jnp.where(jnp.arange(RIDE) // ADAPTER_RANK == 2 + core, keyval_back, 0.0)
    back = (query_sum[:, 2560:] + keyval_back).astype(bf16)
    grad_normed = (
        query_sum[:, :MODEL_WIDTH] + dot(back, q_in) + dot_t(grad_keyval, w[:, 256:512])
    )
    _, norm_one_back = jax.vjp(lambda v: layer_norm(v, gain_one, shift_one), input_rows)
    grad_tokens = (grad_middle + norm_one_back(grad_normed)[0]).astype(bf16)

    late_pieces, grad_tokens = together((late_pieces, grad_tokens))
    kept, sent = sum_by_adapter(late_pieces, core, all_ids)
    own_half = add_cores(kept, sent).astype(bf16)
    other_part = other_core(own_half)
    near = ring_by_core(jnp.concatenate([own_half, other_part], axis=0))
    far = ring_x(own_half, 2)
    feed_grads = spread_out(
        feed_spread_kernel, at, [feed_sum], (1024, 1024, 256, 256), "feed_spread"
    )
    near, far, feed_grads, layer_output = together((near, far, feed_grads, layer_output))
    up_b, down_a, up_a, output_b = feed_grads
    query_a, keyval_a, keyval_b, down_b, query_b, output_a = spread_out(
        late_spread_kernel,
        at,
        [own_half, other_part, near, other_core(near), far, other_core(far)],
        (256, 256, 64, 256, 256, 256),
        "late_spread",
    )

    def side_in(a):
        return jnp.swapaxes(a, 1, 2)

    return (
        layer_output,
        grad_tokens,
        side_in(query_a),
        query_b,
        side_in(keyval_a),
        keyval_b,
        side_in(output_a),
        output_b,
        side_in(up_a),
        up_b,
        side_in(down_a),
        down_b,
    )

def solution(mesh):
    fine = Mesh(mesh.devices.reshape(SIZES), AXES)
    in_specs = (
        P(AXES, None),
        P(AXES, None),
        P(),
        P(),
        P(DP, MP),
        P(MP),
        P(DP, None),
        P(),
        P(MP, DP),
        P(),
        P(),
        P(),
        P(DP, MP),
        P(MP),
        P(MP, DP),
        P(),
        P(DP, None),
        P(),
        P(None, None, MP),
        P(),
        P(),
        P(None, MP, None),
        P(),
        P(),
        P(None, None, MP),
        P(None, MP, None),
        P(),
    )
    out_specs = (P(AXES, None), P(AXES, None)) + (P(),) * 10
    return jax.shard_map(shards, mesh=fine, in_specs=in_specs, out_specs=out_specs, check_vma=False)
```

```python
import functools
import math

import jax
import jax.numpy as jnp
from jax import lax
from jax.experimental import pallas as pl
from jax.experimental.pallas import tpu as pltpu
from jax.sharding import Mesh
from jax.sharding import PartitionSpec as P

MODEL_WIDTH = 2048
H = 16
HEAD_WIDTH = 128
FEED_HIDDEN = 8192
ADAPTER_RANK = 16
ADAPTER_COUNT = 8
BLOCK = 256

AXES = ("y", "zl", "core", "zh", "x")
SIZES = (4, 2, 2, 2, 4)
DP = ("y", "zl", "core")
MP = ("zh", "x")
PLACES = (0, 3, 1, 2)
Z_RING = (0, 2, 1, 3)
ROWS = 128
RIDE = 128

f32 = jnp.float32
bf16 = jnp.bfloat16


together = lax.optimization_barrier


def ring_x(a, step):
    return lax.ppermute(a, "x", [(i, (i + step) % 4) for i in range(4)])


def ring_y(a, step):
    return lax.ppermute(a, "y", [(i, (i + step) % 4) for i in range(4)])


def ring_z(a, step):
    return lax.ppermute(a, ("zl", "zh"), [(Z_RING[i], Z_RING[(i + step) % 4]) for i in range(4)])


def other_core(a):
    return lax.ppermute(a, "core", [(0, 1), (1, 0)])


def other_half(a):
    return lax.ppermute(a, "zh", [(0, 1), (1, 0)])


def turn(a):
    return lax.ppermute(a, ("core", "zh"), [(0, 0), (1, 2), (2, 1), (3, 3)])


def plane_pairs(step, swapped):
    def index(y, z, core):
        return ((y * 2 + z % 2) * 2 + core) * 2 + z // 2

    pairs = []
    for y in range(4):
        for z in range(4):
            for core in range(2):
                if (core == 0) != swapped:
                    to = index((y + step) % 4, z, core)
                else:
                    to = index(y, (z + step) % 4, core)
                pairs.append((index(y, z, core), to))
    return pairs


def gather_cross(a, swapped):
    return [a] + [
        lax.ppermute(a, ("y", "zl", "core", "zh"), plane_pairs(-step, swapped))
        for step in (1, 2, 3)
    ]


def gather_sides(a):
    return a, ring_x(a, 1), ring_x(a, -1)


def gather_rest(a, left, right, near=None):
    half = a.shape[0] // 2
    near = other_core(a) if near is None else near
    top, bottom = ring_x(left[:half], 1), ring_x(right[half:], -1)
    return (
        (a, near),
        (left, other_core(left)),
        (right, other_core(right)),
        (top, bottom, other_core(top), other_core(bottom)),
    )


def gather_row(a):
    near = other_core(a)
    return gather_rest(*gather_sides(a), near)


def add_cores(mine, theirs):
    return mine.astype(f32) + other_core(theirs).astype(f32)


def scatter_far(far_mine, far_theirs):
    return add_cores(far_mine, far_theirs).astype(bf16)


def scatter_sides(far):
    half = far.shape[0] // 2
    return ring_x(far[:half], 1), ring_x(far[half:], -1)


def scatter_joined(near, up, down):
    half = up.shape[0]
    right = jnp.concatenate([near[2, :half] + up.astype(f32), near[2, half:]]).astype(bf16)
    left = jnp.concatenate([near[1, :half], near[1, half:] + down.astype(f32)]).astype(bf16)
    return right, left


def scatter_last(near, up, down):
    right, left = scatter_joined(near, up, down)
    return near[0] + ring_x(right, 1).astype(f32) + ring_x(left, -1).astype(f32)


def scatter_row(mine, theirs, far_mine, far_theirs):
    up, down = scatter_sides(scatter_far(far_mine, far_theirs))
    return scatter_last(add_cores(mine, theirs), up, down)


def scatter_start(mine, theirs, far_mine, far_theirs):
    far = add_cores(far_mine, far_theirs).astype(bf16)
    near = add_cores(mine, theirs)
    return near[0], near[1].astype(bf16), near[2].astype(bf16), far


def gather_y(a):
    return [a, ring_y(a, -1), ring_y(a, 2), ring_y(a, 1)]


def gather_z(a):
    return [a, ring_z(a, -1), ring_z(a, 2), ring_z(a, 1)]


def ring_by_core(a):
    pairs = [(i, (i + 1) % 4) for i in range(4)] + [(4 + i, 4 + (i + 3) % 4) for i in range(4)]
    return lax.ppermute(a, ("core", "x"), pairs)


def by_core(core, own, other):
    return jnp.where(
        core == 0, jnp.concatenate([own, other], -1), jnp.concatenate([other, own], -1)
    )


def row_slice(pair, core, widths):
    own = jnp.where(core == 0, pair[:16], pair[16:]).astype(bf16)
    other = other_core(jnp.where(core == 0, pair[16:], pair[:16]).astype(bf16))
    ends = [sum(widths[:k]) for k in range(1, len(widths))]
    pieces = zip(jnp.split(own, ends, axis=1), jnp.split(other, ends, axis=1))
    return jnp.concatenate([by_core(core, a, b) for a, b in pieces], axis=1)


def scatter_sequence(slices):
    return slices[0], ring_x(slices[1], 1), ring_x(slices[3], -1), ring_x(slices[2], 2)


def total(parts):
    return sum(part.astype(f32) for part in parts).astype(bf16)


def layer_norm(values, gain, shift):
    mean_value = jnp.mean(values, axis=-1, keepdims=True)
    centred = values - mean_value
    variance = jnp.mean(centred * centred, axis=-1, keepdims=True)
    return centred * lax.rsqrt(variance + 1e-05) * gain + shift


def gelu_tanh(values):
    inner_product = math.sqrt(2.0 / math.pi) * (values + 0.044715 * values * values * values)
    return 0.5 * values * (1.0 + jnp.tanh(inner_product))


def pick(adapter_stack, position):
    return lax.dynamic_index_in_dim(adapter_stack, position, 0, keepdims=False)


def dot(left, right):
    return jnp.dot(left, right, preferred_element_type=f32)


def dot_t(left, right):
    return lax.dot_general(left, right, (((1,), (1,)), ((), ())), preferred_element_type=f32)


def tdot(left, right):
    return lax.dot_general(left, right, (((0,), (0,)), ((), ())), preferred_element_type=f32)


def lane_owner(rows, row_core):
    lane = lax.broadcasted_iota(jnp.int32, (rows, RIDE), 1)
    owner = lax.rem(lane // ADAPTER_RANK, 2)
    return jnp.logical_and(owner == row_core, lane < 4 * ADAPTER_RANK)


def place_mask(core):
    row = lax.broadcasted_iota(jnp.int32, (2 * ROWS, RIDE), 0)
    return lane_owner(2 * ROWS, jnp.where(row < ROWS, core, 1 - core))


def copy(source, target, sem):
    pltpu.make_async_copy(source, target, sem).start()


def wait(target, sem):
    pltpu.make_async_copy(target, target, sem).wait()


def copy_place(pieces, target_mine, target_theirs, sem):
    half = ROWS // 2
    if len(pieces) == 2:
        copy(pieces[0], target_mine, sem)
        copy(pieces[1], target_theirs, sem)
    else:
        copy(pieces[0], target_mine.at[pl.ds(0, half)], sem)
        copy(pieces[1], target_mine.at[pl.ds(half, half)], sem)
        copy(pieces[2], target_theirs.at[pl.ds(0, half)], sem)
        copy(pieces[3], target_theirs.at[pl.ds(half, half)], sem)


def split_pieces(refs):
    return (refs[0:2], refs[2:4], refs[4:6], refs[6:10])


def copy_row(gathered, at, target_of, sem_of):
    core, x = at[0], at[1]
    for p in range(4):
        there = lax.rem(x + PLACES[p], 4)
        copy(gathered.at[core, there], target_of(p, 0), sem_of(p, 0))
        copy(gathered.at[1 - core, there], target_of(p, 1), sem_of(p, 1))


def assemble_kernel(at, *refs):
    pieces, (out, sem) = refs[:4], refs[4:]
    core, y, z = at[0], at[3], at[4]
    for far, piece in enumerate(pieces):
        for near in range(4):
            to_y = lax.rem(y + jnp.where(core == 0, near, far), 4)
            to_z = lax.rem(z + jnp.where(core == 0, far, near), 4)
            shard = (to_y * 2 + lax.rem(to_z, 2)) * 2 + to_z // 2
            copy(piece.at[near], out.at[pl.ds(pl.multiple_of(shard * ROWS, ROWS), ROWS)], sem)
    wait(out, sem)


def pack_kernel(at, *refs):
    first = 0
    for part in refs[:-2]:
        refs[-1][:, first : first + part.shape[1]] = part[...]
        first += part.shape[1]
    refs[-1][:, first:] = refs[-2][...].astype(f32).T.astype(bf16)


def norm_kernel(at, rows, gain, shift, out):
    values = layer_norm(
        rows[...].astype(f32), gain[...].astype(f32), shift[...].astype(f32)
    )
    out[...] = values.astype(bf16)


def select_kernel(at, *refs):
    pairs = [refs[2 * n : 2 * n + 2] for n in range(10)]
    q_bias, u_bias = refs[20:22]
    small, q_in, u_in, o_out, d_out, kv_out, bias = refs[22:]
    for out, count in ((q_in, 4), (u_in, 2), (o_out, 2), (d_out, 2)):
        out[16 * count :] = jnp.zeros((RIDE - 16 * count, MODEL_WIDTH), bf16)
    kv_out[...] = jnp.zeros_like(kv_out)
    for c in range(2):
        here, after = slice(16 * c, 16 * c + 16), slice(32 + 16 * c, 48 + 16 * c)
        q_in[here] = pairs[0][c][0]
        q_in[after] = pairs[1][c][0]
        u_in[here] = pairs[2][c][0]
        o_out[here] = pairs[3][c][0]
        d_out[here] = pairs[4][c][0]
        kv_out[after] = pairs[5][c][0]
        first = 0
        for n in range(6, 10):
            width = pairs[n][c].shape[2]
            small[here, first : first + width] = pairs[n][c][0]
            first += width
    small[32:] = jnp.zeros((16, 2560), bf16)
    small[32:33, :256] = q_bias[...]
    small[32:33, 512:1536] = u_bias[...]
    x, zh = at[2], at[3]

    def block_of(place):
        step = jnp.where(place == 0, 0, jnp.where(place == 1, 3, place - 1))
        return ((x + step) & 3) >> 1

    key = lax.broadcasted_iota(jnp.int32, (8, 4 * ROWS), 0)
    query = lax.broadcasted_iota(jnp.int32, (8, 4 * ROWS), 1) >> 7
    own = jnp.logical_and(key < 4, block_of(key) <= block_of(query))
    other = jnp.logical_and(key >= 4, zh == 1)
    bias[...] = jnp.where(jnp.logical_or(own, other), 0.0, -1e30)


def turned_kernel(at, small, q_out, o_in, u_out, d_in, q_bias, u_bias):
    first = 0
    for out in (q_out, o_in, u_out, d_in):
        width = out.shape[1]
        out[:32] = small[:32, first : first + width]
        out[32:] = jnp.zeros((RIDE - 32, width), bf16)
        first += width
    q_bias[...] = small[32:33, :256].astype(f32)
    u_bias[...] = small[32:33, 512:1536].astype(f32)


def own_keyval_kernel(at, rows, w, q_in, kv_out, kv_bias, out):
    inner = dot_t(rows[...], q_in[...])
    lane = lax.broadcasted_iota(jnp.int32, (ROWS, RIDE), 1)
    inner = jnp.where(lane // ADAPTER_RANK == 2 + at[0], inner, 0.0).astype(bf16)
    keyval = dot(rows[...], w[...]) + kv_bias[...] + dot(inner, kv_out[...])
    out[:, :256] = keyval.astype(bf16)
    out[:, 256:] = inner


def sum_kernel(at, *refs):
    pieces, (kept, sent, total) = refs[:-3], refs[-3:]
    total[...] = jnp.zeros_like(total)
    row = 1
    for piece in pieces:
        for k in range(piece.shape[0]):
            total[at[row]] += piece[k].astype(f32)
            row += 1
    kept[...] = total[pl.ds(4 * at[0], 4)].astype(bf16)
    sent[...] = total[pl.ds(4 - 4 * at[0], 4)].astype(bf16)


def slices_kernel(count, at, *refs):
    ins, out = refs[: 2 * count], refs[2 * count]
    x = at[1]
    for n in range(count):
        back, rows = ins[2 * n], ins[2 * n + 1]
        turned = back[...].astype(f32).T
        turned = (turned[:16] + turned[16:32]).astype(bf16)
        product = dot(turned, rows[...]).astype(bf16)
        for to in range(4):
            place = lax.rem(to + 4 - x, 4)
            for c in range(2):
                first = (c * 4 + to) * 256
                lanes = slice(n * 512 + c * 256, n * 512 + (c + 1) * 256)
                out[place, :, lanes] = product[:, first : first + 256]


def spread(scratch, outs, widths):
    x, c = pl.program_id(0), pl.program_id(1)
    first = 0
    for out, width in zip(outs, widths):
        here = pl.ds(pl.multiple_of(first + c * width, 128), width)
        out[...] = scratch[x, :, :, here].astype(f32)
        first += 2 * width


def feed_spread_kernel(widths, at, *refs):
    gathered, (scratch, sem) = refs[0], refs[-2:]

    @pl.when((pl.program_id(0) == 0) & (pl.program_id(1) == 0))
    def _():
        for c in range(2):
            for x in range(4):
                copy(gathered.at[c, x], scratch.at[x, pl.ds(4 * c, 4)], sem)
        wait(scratch, sem)

    spread(scratch, refs[1:-2], widths)


def late_spread_kernel(widths, at, *refs):
    own, other, near, near_other, far, far_other = refs[:6]
    outs, (scratch, sem) = refs[6:-2], refs[-2:]
    core, x = at[0], at[1]
    mine, theirs = pl.ds(4 * core, 4), pl.ds(4 * (1 - core), 4)
    side = lax.rem(x + jnp.where(core == 0, 3, 1), 4)
    other_side = lax.rem(x + jnp.where(core == 0, 1, 3), 4)
    across = lax.rem(x + 2, 4)
    copy(own, scratch.at[x, mine], sem)
    copy(other, scratch.at[x, theirs], sem)
    for part, where in ((0, mine), (1, theirs)):
        copy(near.at[pl.ds(4 * part, 4)], scratch.at[side, where], sem)
    for part, where in ((0, theirs), (1, mine)):
        copy(near_other.at[pl.ds(4 * part, 4)], scratch.at[other_side, where], sem)
    copy(far, scratch.at[across, mine], sem)
    copy(far_other, scratch.at[across, theirs], sem)
    wait(scratch, sem)
    first = 0
    for out, width in zip(outs, widths):
        if width < 128:
            for g in range(2):
                pair = scratch[2 * g, :, :, first : first + 128].astype(f32)
                pair += scratch[2 * g + 1, :, :, first : first + 128].astype(f32)
                out[:, :, g * 128 : g * 128 + 128] = pair
            first += 128
            continue
        for c in range(2):
            for to in range(4):
                here = slice((c * 4 + to) * width, (c * 4 + to + 1) * width)
                out[:, :, here] = scratch[to, :, :, first : first + width].astype(f32)
            first += width


def copy_rows(rows_in, rows, sems):
    half = ROWS // 2
    for s in range(2):
        for p in range(4):
            pieces = rows_in[p]
            if len(pieces) == 2:
                copy(pieces[s], rows.at[s, pl.ds(p * ROWS, ROWS)], sems.at[s])
            else:
                for n in range(2):
                    here = pl.ds(p * ROWS + n * half, half)
                    copy(pieces[2 * s + n], rows.at[s, here], sems.at[s])


def attend(query, kv, bias, lanes, lse_out):
    keys = kv[:, :, :HEAD_WIDTH].reshape(8 * ROWS, HEAD_WIDTH)
    values_t = kv[:, :, HEAD_WIDTH:].reshape(8 * ROWS, HEAD_WIDTH).astype(f32).T.astype(bf16)
    columns = []
    for h in range(2):
        q = query[:, h * HEAD_WIDTH : (h + 1) * HEAD_WIDTH]
        scores = dot_t(keys, q) * (HEAD_WIDTH**-0.5)
        scores = scores.reshape(8, ROWS, 256) + bias[:, lanes][:, None, :]
        scores = scores.reshape(8 * ROWS, 256)
        top = jnp.max(scores, axis=0, keepdims=True)
        expo = jnp.exp(scores - top)
        total = jnp.sum(expo, axis=0, keepdims=True)
        probs = (expo * (1.0 / total)).astype(bf16)
        lse_out[0, h : h + 1] = top + jnp.log(total)
        columns.append(dot(values_t, probs).T)
    return jnp.concatenate(columns, axis=1).astype(bf16)


def attention_kernel(at, *refs):
    rows_in = split_pieces(refs[:10])
    kv_in = refs[10:15]
    w, q_in, q_out, kv_out, o_in, q_bias, kv_bias, bias = refs[15:23]
    inner_out, inner_far, query_out, kv_all, lse_out, att_out = refs[23:29]
    parts, far_parts = refs[29:31], refs[31:33]
    rows, kvs, ws, sems = refs[33:]
    s = pl.program_id(0)
    core = at[0]

    @pl.when(s == 0)
    def _():
        copy(w, ws, sems.at[2])
        copy_rows(rows_in, rows, sems)
        pair, near, near_other, far, far_other = kv_in
        first, second = pl.ds(0, ROWS), pl.ds(ROWS, ROWS)
        side = jnp.where(core == 0, 1, 2)
        copy(pair.at[first], kvs.at[0, 0], sems.at[3])
        copy(pair.at[second], kvs.at[1, 0], sems.at[3])
        copy(near.at[first], kvs.at[0, side], sems.at[3])
        copy(near.at[second], kvs.at[1, side], sems.at[3])
        copy(near_other.at[first], kvs.at[1, 3 - side], sems.at[3])
        copy(near_other.at[second], kvs.at[0, 3 - side], sems.at[3])
        copy(far, kvs.at[0, 3], sems.at[3])
        copy(far_other, kvs.at[1, 3], sems.at[3])
        wait(ws, sems.at[2])
        wait(kvs, sems.at[3])

    wait(rows.at[s], sems.at[s])
    owner = lane_owner(4 * ROWS, jnp.where(s == 0, core, 1 - core))
    x = rows[s]
    inner = jnp.where(owner, dot_t(x, q_in[...]), 0.0).astype(bf16)
    inner_out[0] = inner
    query = (dot(x, ws[:, :256]) + q_bias[...] + dot(inner, q_out[...])).astype(bf16)
    query_out[0] = query
    kv_own = (dot(x, ws[:, 256:512]) + kv_bias[...] + dot(inner, kv_out[...])).astype(bf16)
    inner_far[0] = kvs[s, :, :, 256:].reshape(4 * ROWS, RIDE)
    kv = jnp.concatenate([kv_own.reshape(4, ROWS, 256), kvs[s, :, :, :256]], axis=0)
    kv_all[0] = kv
    attended = attend(query[2 * ROWS :], kv, bias, slice(2 * ROWS, 4 * ROWS), lse_out)
    att_out[0] = attended
    low = jnp.where(owner[2 * ROWS :], dot_t(attended, o_in[...]), 0.0).astype(bf16)
    out = dot_t(attended, ws[:, 512:]).astype(bf16)
    for which in range(2):

        @pl.when(s == which)
        def _(which=which):
            for n, part in enumerate((parts[which], far_parts[which])):
                here = slice(n * ROWS, (n + 1) * ROWS)
                part[:, :MODEL_WIDTH] = out[here]
                part[:, MODEL_WIDTH:] = low[here]


def attention_rest_kernel(at, query_in, kv_in, w, o_in, bias, lse_out, att_out, mine, theirs):
    s = pl.program_id(0)
    owner = lane_owner(2 * ROWS, jnp.where(s == 0, at[0], 1 - at[0]))
    attended = attend(query_in[0, : 2 * ROWS], kv_in[0], bias, slice(0, 2 * ROWS), lse_out)
    att_out[0] = attended
    low = jnp.where(owner, dot_t(attended, o_in[...]), 0.0).astype(bf16)
    out = dot_t(attended, w[...]).astype(bf16)
    for which, part in enumerate((mine, theirs)):

        @pl.when(s == which)
        def _(part=part):
            for n in range(2):
                here = slice(n * ROWS, (n + 1) * ROWS)
                part[n, :, :MODEL_WIDTH] = out[here]
                part[n, :, MODEL_WIDTH:] = low[here]


def store_parts(p, parts, far_parts, out, low):
    for which in range(2):
        here = slice(which * ROWS, (which + 1) * ROWS)

        @pl.when(p < 3)
        def _(which=which, here=here):
            parts[which][0, :, :MODEL_WIDTH] = out[here]
            parts[which][0, :, MODEL_WIDTH:] = low[here]

        @pl.when(p == 3)
        def _(which=which, here=here):
            far_parts[which][:, :MODEL_WIDTH] = out[here]
            far_parts[which][:, MODEL_WIDTH:] = low[here]


def feed_kernel(at, *refs):
    rows_in = split_pieces(refs[:10])
    cot, feed, u_in, u_out, d_in, u_bias = refs[10:16]
    placed = refs[16]
    up_b, down_a = placed.at[:, pl.ds(0, 1024)], placed.at[:, pl.ds(1024, 1024)]
    down_parts, down_far = refs[17:19], refs[19:21]
    up_parts, up_far = refs[21:23], refs[23:25]
    rows, grads, up, down, slopes, sems = refs[25:]
    p = pl.program_id(0)
    core = at[0]

    @pl.when(p == 0)
    def _():
        copy_place(rows_in[0], rows.at[0, pl.ds(0, ROWS)], rows.at[0, pl.ds(ROWS, ROWS)], sems.at[0])
        copy(feed.at[:, core, :, pl.ds(0, 1024)], up, sems.at[8])
        copy(feed.at[:, core, :, pl.ds(1024, 1024)], down, sems.at[9])
        copy_row(
            cot,
            at,
            lambda k, which: grads.at[k, pl.ds(which * ROWS, ROWS)],
            lambda k, which: sems.at[4 + k],
        )
        for k in range(1, 4):
            copy_place(
                rows_in[k], rows.at[k, pl.ds(0, ROWS)], rows.at[k, pl.ds(ROWS, ROWS)], sems.at[k]
            )
        placed[...] = jnp.zeros_like(placed)
        wait(up, sems.at[8])

    wait(rows.at[p], sems.at[p])
    mask = place_mask(core)
    x = rows[p]
    inner = jnp.where(mask, dot_t(x, u_in[...]), 0.0)
    inner_t, inner = inner.T[:32].astype(bf16), inner.astype(bf16)
    pre = dot(x, up[...].reshape(MODEL_WIDTH, 1024)) + u_bias[...] + dot(inner, u_out[...])
    k0 = math.sqrt(2.0 / math.pi)
    square = pre * pre
    bend = jnp.tanh(k0 * (pre + 0.044715 * square * pre))
    act = (0.5 * pre * (1.0 + bend)).astype(bf16)
    slopes[...] = 0.5 * (1.0 + bend) + 0.5 * pre * (1.0 - bend * bend) * (
        k0 * (1.0 + 3.0 * 0.044715 * square)
    )

    @pl.when(p == 0)
    def _():
        wait(down, sems.at[9])

    low = jnp.where(mask, dot_t(act, d_in[...]), 0.0).astype(bf16)
    out = dot_t(act, down[...].reshape(MODEL_WIDTH, 1024)).astype(bf16)
    store_parts(p, down_parts, down_far, out, low)

    wait(grads.at[p], sems.at[4 + p])
    grad, back = grads[p, :, :MODEL_WIDTH], grads[p, :, MODEL_WIDTH:]
    down_a[...] += dot(back.astype(f32).T[:32].astype(bf16), act)
    grad_act = dot(grad, down[...].reshape(MODEL_WIDTH, 1024)) + dot(back, d_in[...])
    grad_pre = (grad_act * slopes[...]).astype(bf16)
    up_b[...] += dot(inner_t, grad_pre)
    low = jnp.where(mask, dot_t(grad_pre, u_out[...]), 0.0).astype(bf16)
    out = dot_t(grad_pre, up[...].reshape(MODEL_WIDTH, 1024)).astype(bf16)
    store_parts(p, up_parts, up_far, out, low)


def late_kernel(at, *refs):
    rows_in = split_pieces(refs[:10])
    backs, backs_far, keyval_b, cotangent = refs[10:14]
    down_parts = refs[14:18]
    outs, (rows, sems) = refs[18:20], refs[20:]
    core, x = at[0], at[1]
    copy_rows(rows_in, rows, sems)
    inner = sum(part[...].astype(f32) for part in down_parts).T
    inner = (inner[:16] + inner[16:32]).astype(bf16)
    down_b = dot(inner, cotangent[...]).astype(bf16)
    for to in range(4):
        place = lax.rem(to + 4 - x, 4)
        for c in range(2):
            begin = (c * 4 + to) * 256
            lanes = slice(1152 + c * 256, 1152 + (c + 1) * 256)
            outs[0][place, :, lanes] = down_b[:, begin : begin + 256]
    product = jnp.zeros((64, MODEL_WIDTH), f32)
    for s in range(2):
        wait(rows.at[s], sems.at[s])
        back = backs[s].astype(f32).T
        back = jnp.concatenate([back[:32], back[32:64] + backs_far[s].astype(f32)], axis=0)
        product += dot(back.astype(bf16), rows[s])
    first, second = keyval_b[:16], keyval_b[16:]
    lane = lax.broadcasted_iota(jnp.int32, (ADAPTER_RANK, RIDE), 1) // 64
    for which in range(2):
        out = outs[which]
        is_first = (core == 0) if which == 0 else (core != 0)
        for n in range(2):
            both = product[32 * n : 32 * n + 32]
            picked = jnp.where(is_first, both[:16], both[16:]).astype(bf16)
            for to in range(4):
                place = lax.rem(to + 4 - x, 4)
                for c in range(2):
                    begin = (c * 4 + to) * 256
                    lanes = slice(n * 512 + c * 256, n * 512 + (c + 1) * 256)
                    out[place, :, lanes] = picked[:, begin : begin + 256]
        picked = jnp.where(is_first, first, second).astype(bf16)
        for to in range(4):
            place = lax.rem(to + 4 - x, 4)
            part = picked[:, (to // 2) * 128 : (to // 2) * 128 + 128]
            out[place, :, 1024:1152] = jnp.where(lane == to % 2, part, jnp.zeros_like(part))


def attention_back_kernel(at, *refs):
    branch, w, inner_in, inner_far, query_in, kv_in = refs[:6]
    lse_in, att_in = refs[6:8], refs[8:10]
    o_out, o_in, q_out, kv_out, bias = refs[10:15]
    placed, keyval_b, backs, backs_far = refs[15:19]
    query_b, output_a = placed.at[:, pl.ds(0, 256)], placed.at[:, pl.ds(256, 256)]
    parts, far_parts = refs[19:21], refs[21:23]
    rows, ws, grad_k, grad_v, sems = refs[23:]
    s = pl.program_id(0)
    core = at[0]

    @pl.when(s == 0)
    def _():
        copy(w, ws, sems.at[2])
        copy_row(
            branch,
            at,
            lambda p, which: rows.at[which, pl.ds(p * ROWS, ROWS)],
            lambda p, which: sems.at[which],
        )
        placed[...] = jnp.zeros_like(placed)
        keyval_b[...] = jnp.zeros_like(keyval_b)
        wait(ws, sems.at[2])

    wait(rows.at[s], sems.at[s])

    owner = lane_owner(4 * ROWS, jnp.where(s == 0, core, 1 - core))
    scale = HEAD_WIDTH**-0.5
    x = rows[s]
    back = jnp.where(owner, dot_t(x, o_out[...]), 0.0)
    output_a[...] += dot(
        back.T[:32].astype(bf16), jnp.concatenate([att_in[0][0], att_in[1][0]], axis=0)
    )
    grad_att = (dot(x, ws[:, 512:]) + dot(back.astype(bf16), o_in[...])).astype(bf16)
    query = query_in[0]
    kv = kv_in[0]
    keys = kv[:, :, :HEAD_WIDTH].reshape(8 * ROWS, HEAD_WIDTH)
    values = kv[:, :, HEAD_WIDTH:].reshape(8 * ROWS, HEAD_WIDTH)
    keys_t = keys.astype(f32).T.astype(bf16)
    columns = []
    for h in range(2):
        chunks = []
        for c in range(2):
            lanes = slice(c * 256, c * 256 + 256)
            head = slice(h * HEAD_WIDTH, (h + 1) * HEAD_WIDTH)
            q, g = query[lanes, head], grad_att[lanes, head]
            scores = dot_t(keys, q) * scale
            scores = scores.reshape(8, ROWS, 256) + bias[:, lanes][:, None, :]
            probs = jnp.exp(scores.reshape(8 * ROWS, 256) - lse_in[c][0, h : h + 1])
            grad_probs = dot_t(values, g)
            delta = jnp.sum(probs * grad_probs, axis=0, keepdims=True)
            grad_scores = (probs * (grad_probs - delta)).astype(bf16)
            chunks.append((dot(keys_t, grad_scores) * scale).T)
            more_k = dot(grad_scores, q) * scale
            more_v = dot(probs.astype(bf16), g)
            if h == 0 and c == 0:
                grad_k[...] = more_k
                grad_v[...] = more_v
            else:
                grad_k[...] += more_k
                grad_v[...] += more_v
        columns.append(jnp.concatenate(chunks, axis=0))
    grad_query = jnp.concatenate(columns, axis=1).astype(bf16)
    inner_t = inner_in[0].astype(f32).T
    query_b[...] += dot(inner_t[:32].astype(bf16), grad_query)
    low = jnp.where(owner, dot_t(grad_query, q_out[...]), 0.0).astype(bf16)
    grad_kv = jnp.concatenate([grad_k[...], grad_v[...]], axis=1).astype(bf16)
    own_kv, far_kv = grad_kv[: 4 * ROWS], grad_kv[4 * ROWS :]
    keyval_b[...] += dot(inner_t[32:64].astype(bf16), own_kv)
    keyval_b[...] += dot(inner_far[0].astype(f32).T[32:64].astype(bf16), far_kv)
    backs[0] = low + jnp.where(owner, dot_t(own_kv, kv_out[...]), 0.0).astype(bf16)
    backs_far[0] = jnp.where(owner, dot_t(far_kv, kv_out[...]), 0.0).T[32:64].astype(bf16)
    for which in range(2):

        @pl.when(s == which)
        def _(which=which):
            for p in range(4):
                here = slice(p * ROWS, (p + 1) * ROWS)
                part = parts[which].at[p] if p < 3 else far_parts[which]
                part[:, :2048] = dot_t(grad_query[here], ws[:, :256]).astype(bf16)
                part[:, 2048:2304] = own_kv[here]
                part[:, 2304:2560] = far_kv[here]
                part[:, 2560:] = low[here]


VMEM_LIMIT = 56 * 1024 * 1024
ANY = pl.BlockSpec(memory_space=pl.ANY)


def whole_block(shape):
    return pl.BlockSpec(shape, lambda i, at: (0,) * len(shape))


def step_block(shape):
    return pl.BlockSpec((1, *shape), lambda i, at: (i,) + (0,) * len(shape))


def call(kernel, steps, at, ins, outs, scratch, name, flops=0, short=False):
    arrays = [a for a, _ in ins]
    in_specs = [whole_block(a.shape) if b is None else b for a, b in ins]
    out_specs = [whole_block(s) if b is None else b for s, _, b in outs]
    return pl.pallas_call(
        kernel,
        out_shape=[jax.ShapeDtypeStruct(s, d) for s, d, _ in outs],
        grid_spec=pltpu.PrefetchScalarGridSpec(
            num_scalar_prefetch=1,
            grid=(steps,),
            in_specs=in_specs,
            out_specs=out_specs,
            scratch_shapes=scratch,
        ),
        compiler_params=pltpu.CompilerParams(vmem_limit_bytes=VMEM_LIMIT),
        cost_estimate=pl.CostEstimate(
            flops=0 if short else flops,
            bytes_accessed=0
            if short
            else sum(a.size * a.dtype.itemsize for a in arrays)
            + sum(math.prod(s) * 4 for s, _, _ in outs),
            transcendentals=0,
        ),
        name=name,
    )(at, *arrays)


def flat(places):
    return [(piece, ANY) for place in places for piece in place]


def part_outs(width, steps=False):
    block = pl.BlockSpec((1, ROWS, width), lambda i, at: (jnp.minimum(i, 2), 0, 0))
    near = ((3, ROWS, width), bf16, block if steps else None)
    return [near, near, ((ROWS, width), bf16, None), ((ROWS, width), bf16, None)]


def dma(n):
    return pltpu.SemaphoreType.DMA((n,))


def sum_by_adapter(pieces, core, ids):
    width = pieces[0].shape[-1]
    block = max(w for w in range(128, 3713, 128) if width % w == 0)
    half = (ADAPTER_COUNT // 2, ADAPTER_RANK)
    return pl.pallas_call(
        sum_kernel,
        out_shape=[jax.ShapeDtypeStruct((*half, width), bf16)] * 2,
        grid_spec=pltpu.PrefetchScalarGridSpec(
            num_scalar_prefetch=1,
            grid=(width // block,),
            in_specs=[
                pl.BlockSpec((p.shape[0], ADAPTER_RANK, block), lambda i, at: (0, 0, i))
                for p in pieces
            ],
            out_specs=[pl.BlockSpec((*half, block), lambda i, at: (0, 0, i))] * 2,
            scratch_shapes=[pltpu.VMEM((ADAPTER_COUNT, ADAPTER_RANK, block), f32)],
        ),
        compiler_params=pltpu.CompilerParams(vmem_limit_bytes=VMEM_LIMIT),
        name="sum_by_adapter",
    )(jnp.concatenate([jnp.reshape(core, (1,)), ids]).astype(jnp.int32), *pieces)


def spread_out(kernel, at, pieces, widths, name, steps=True):
    total = pieces[0].shape[-1]
    full = [8 * w if w >= 128 else 256 for w in widths]
    rows = (ADAPTER_COUNT, ADAPTER_RANK)
    if steps:
        grid = (4, 2)
        out_specs = [pl.BlockSpec((*rows, w), lambda i, j, at: (0, 0, j * 4 + i)) for w in widths]
    else:
        grid = (1,)
        out_specs = [pl.BlockSpec((*rows, w), lambda i, at: (0, 0, 0)) for w in full]
    return pl.pallas_call(
        functools.partial(kernel, widths),
        out_shape=[jax.ShapeDtypeStruct((*rows, w), f32) for w in full],
        grid_spec=pltpu.PrefetchScalarGridSpec(
            num_scalar_prefetch=1,
            grid=grid,
            in_specs=[ANY] * len(pieces),
            out_specs=out_specs,
            scratch_shapes=[pltpu.VMEM((4, *rows, total), bf16), pltpu.SemaphoreType.DMA],
        ),
        compiler_params=pltpu.CompilerParams(vmem_limit_bytes=VMEM_LIMIT),
        name=name,
    )(at, *pieces)


def slices_of(at, pairs, name):
    shape = (4, ADAPTER_RANK, 512 * len(pairs))
    ins = [(a, None) for pair in pairs for a in pair]
    kernel = functools.partial(slices_kernel, len(pairs))
    return call(kernel, 1, at, ins, [(shape, bf16, None)], [], name)[0]


def shards(
    tokens,
    cotangent,
    attention_norm_scale,
    attention_norm_bias,
    query_projection,
    query_projection_bias,
    keyvalue_projection,
    value_projection_bias,
    attention_output_weight,
    attention_output_bias,
    feedforward_norm_scale,
    feedforward_norm_bias,
    up_projection_weight,
    up_projection_bias,
    down_projection_weight,
    down_projection_bias,
    sequence_adapter,
    query_adapter_input,
    query_adapter_output,
    keyvalue_adapter_input,
    keyvalue_adapter_output,
    output_adapter_input,
    output_adapter_output,
    up_adapter_input,
    up_adapter_output,
    down_adapter_input,
    down_adapter_output,
):
    y, core, zl, zh, x = (lax.axis_index(n) for n in ("y", "core", "zl", "zh", "x"))
    z = zh * 2 + zl
    at = jnp.stack([core, x, zh, y, z]).astype(jnp.int32)
    gain_one, shift_one = attention_norm_scale.astype(f32), attention_norm_bias.astype(f32)
    gain_two, shift_two = feedforward_norm_scale.astype(f32), feedforward_norm_bias.astype(f32)

    def pack(*parts):
        width = sum(part.shape[1] for part in parts[:-1]) + parts[-1].shape[0]
        ins = [(part, None) for part in parts]
        return call(pack_kernel, 1, at, ins, [((ROWS, width), bf16, None)], [], "pack")[0]

    mine = sequence_adapter[0, 0]
    attention_shard = pack(query_projection, keyvalue_projection, attention_output_weight)
    attention_shard, cotangent = together((attention_shard, cotangent))
    down_back = dot_t(cotangent, pick(down_adapter_output, mine)).astype(bf16)
    down_back = jnp.pad(down_back, ((0, 0), (0, RIDE - 16)))
    down_back = jnp.where(core == 0, down_back, jnp.roll(down_back, 16, axis=1))
    cot_all = jnp.concatenate([cotangent, down_back], axis=1)
    cot_all = lax.all_gather(cot_all, ("core", "x"), axis=0, tiled=True)
    cot_all = cot_all.reshape(2, 4, ROWS, MODEL_WIDTH + RIDE)

    attention_shard = turn(attention_shard)
    feed_shard = pack(up_projection_weight, down_projection_weight)
    attention_shard, feed_shard, sequence_adapter, tokens = together(
        (attention_shard, feed_shard, sequence_adapter, tokens)
    )
    theirs = other_core(sequence_adapter)[0, 0]
    rows_shape = ((ROWS, MODEL_WIDTH), bf16, None)
    normed = call(
        norm_kernel,
        1,
        at,
        [(tokens, None), (attention_norm_scale[None], None), (attention_norm_bias[None], None)],
        [rows_shape],
        [],
        "norm",
    )[0]
    column, mine, theirs, normed = together(
        (gather_cross(attention_shard, False), mine, theirs, normed)
    )
    plane = gather_cross(jnp.stack(column), True)
    normed_sides = gather_sides(normed)

    low = jnp.where(core == 0, mine, theirs)
    high = jnp.where(core == 0, theirs, mine)
    stacks = (
        jnp.swapaxes(query_adapter_input, 1, 2),
        jnp.swapaxes(keyvalue_adapter_input, 1, 2),
        jnp.swapaxes(up_adapter_input, 1, 2),
        output_adapter_output,
        down_adapter_output,
        keyvalue_adapter_output,
        query_adapter_output,
        jnp.swapaxes(output_adapter_input, 1, 2),
        up_adapter_output,
        jnp.swapaxes(down_adapter_input, 1, 2),
    )
    chosen = []
    for stack in stacks:
        block = (1, ADAPTER_RANK, stack.shape[2])
        chosen.append((stack, pl.BlockSpec(block, lambda i, at: (at[0], 0, 0))))
        chosen.append((stack, pl.BlockSpec(block, lambda i, at: (at[1], 0, 0))))
    wide = ((RIDE, MODEL_WIDTH), bf16, None)
    small, q_in, u_in, o_out, d_out, kv_out, bias = call(
        select_kernel,
        1,
        jnp.stack([low, high, x, zh]).astype(jnp.int32),
        [*chosen, (query_projection_bias[None], None), (up_projection_bias[None], None)],
        [
            ((48, 2560), bf16, None),
            wide,
            wide,
            wide,
            wide,
            ((RIDE, 256), bf16, None),
            ((8, 4 * ROWS), f32, None),
        ],
        [],
        "select",
    )
    keyval_bias = jnp.concatenate(
        [jnp.zeros((1, HEAD_WIDTH), f32), value_projection_bias.astype(f32)[None]], axis=1
    )
    prepared = (q_in, u_in, o_out, d_out, kv_out, bias, keyval_bias, small)
    plane, normed_sides, prepared, feed_shard, cot_all = together(
        (plane, normed_sides, prepared, feed_shard, cot_all)
    )
    q_in, u_in, o_out, d_out, kv_out, bias, keyval_bias, small = prepared
    normed_places = gather_rest(*normed_sides)
    (w,) = call(
        assemble_kernel,
        1,
        at,
        [(piece, ANY) for piece in plane],
        [((MODEL_WIDTH, 768), bf16, None)],
        [pltpu.SemaphoreType.DMA],
        "assemble",
    )
    feed = lax.all_gather(feed_shard, DP + ("zh",), axis=0, tiled=True)
    feed = feed.reshape(16, 2, ROWS, 2048)

    w, keyval_bias = together((w, keyval_bias))
    w_keyval = pl.BlockSpec((MODEL_WIDTH, 256), lambda i, at: (0, 1))
    keyval = call(
        own_keyval_kernel,
        1,
        at,
        [(normed, None), (w, w_keyval), (q_in, None), (kv_out, None), (keyval_bias, None)],
        [((ROWS, 384), bf16, None)],
        [],
        "own_keyval",
    )[0]
    keyval = other_half(keyval)
    keyval_far = ring_x(keyval, 2)
    turned = call(
        turned_kernel,
        1,
        at,
        [(turn(small), None)],
        [
            ((RIDE, 256), bf16, None),
            ((RIDE, 256), bf16, None),
            ((RIDE, 1024), bf16, None),
            ((RIDE, 1024), bf16, None),
            ((1, 256), f32, None),
            ((1, 1024), f32, None),
        ],
        [],
        "turned",
    )
    keyval_pair = jnp.concatenate([keyval, other_core(keyval)], axis=0)
    keyval_pair, turned = together((keyval_pair, turned))
    q_out, o_in, u_out, d_in, q_bias, u_bias = turned
    keyval = keyval_pair
    keyval_near = ring_by_core(keyval)
    keyval_pieces = (keyval, keyval_near, other_core(keyval_near))
    keyval_pieces += (keyval_far, other_core(keyval_far))
    input_rows = tokens.astype(f32)

    group = (2, 4 * ROWS)
    row_scratch = pltpu.VMEM((2, 4 * ROWS, MODEL_WIDTH), bf16)
    w_scratch = pltpu.VMEM((MODEL_WIDTH, 768), bf16)
    inner_one, inner_far, query, keyval_all, lse_high, att_high, *out_parts = call(
        attention_kernel,
        2,
        at,
        [
            *flat(normed_places),
            *[(piece, ANY) for piece in keyval_pieces],
            (w, ANY),
            (q_in, None),
            (q_out, None),
            (kv_out, None),
            (o_in, None),
            (q_bias, None),
            (keyval_bias, None),
            (bias, None),
        ],
        [
            ((*group, RIDE), bf16, step_block((4 * ROWS, RIDE))),
            ((*group, RIDE), bf16, step_block((4 * ROWS, RIDE))),
            ((*group, 256), bf16, step_block((4 * ROWS, 256))),
            ((2, 8, ROWS, 256), bf16, step_block((8, ROWS, 256))),
            ((2, 2, 2 * ROWS), f32, step_block((2, 2 * ROWS))),
            ((2, 2 * ROWS, 256), bf16, step_block((2 * ROWS, 256))),
            *[((ROWS, MODEL_WIDTH + RIDE), bf16, None)] * 4,
        ],
        [row_scratch, pltpu.VMEM((2, 4, ROWS, 384), bf16), w_scratch, dma(4)],
        "attention",
        9000000000,
    )
    out_far, query = together((scatter_far(*out_parts[2:]), query))
    out_sides = scatter_sides(out_far)
    out_right = add_cores(*out_parts[:2])
    lse_low, att_low, out_mine, out_theirs = call(
        attention_rest_kernel,
        2,
        at,
        [
            (query, step_block((4 * ROWS, 256))),
            (keyval_all, step_block((8, ROWS, 256))),
            (w, pl.BlockSpec((MODEL_WIDTH, 256), lambda i, at: (0, 2))),
            (o_in, None),
            (bias, None),
        ],
        [
            ((2, 2, 2 * ROWS), f32, step_block((2, 2 * ROWS))),
            ((2, 2 * ROWS, 256), bf16, step_block((2 * ROWS, 256))),
            ((2, ROWS, MODEL_WIDTH + RIDE), bf16, None),
            ((2, ROWS, MODEL_WIDTH + RIDE), bf16, None),
        ],
        [],
        "attention_rest",
        short=True,
    )
    out_mine, out_theirs, out_sides, out_right = together(
        (out_mine, out_theirs, out_sides, out_right)
    )
    out_near = add_cores(out_mine, out_theirs)
    out_sum = scatter_last(jnp.concatenate([out_near, out_right[None]]), *out_sides)
    output_inner = out_sum[:, MODEL_WIDTH:].astype(bf16)
    middle = (
        input_rows
        + out_sum[:, :MODEL_WIDTH]
        + attention_output_bias.astype(f32)
        + dot(output_inner, o_out)
    )
    normed_two = layer_norm(middle, gain_two, shift_two).astype(bf16)
    place_scratch = pltpu.VMEM((4, 2 * ROWS, MODEL_WIDTH), bf16)
    feed_scratch = pltpu.VMEM((16, ROWS, 1024), bf16)
    feed_placed, *feed_parts = call(
        feed_kernel,
        4,
        at,
        [
            *flat(gather_row(normed_two)),
            (cot_all, ANY),
            (feed, ANY),
            (u_in, None),
            (u_out, None),
            (d_in, None),
            (u_bias, None),
        ],
        [
            ((32, 2048), f32, None),
            *part_outs(MODEL_WIDTH + RIDE, True),
            *part_outs(MODEL_WIDTH + RIDE, True),
        ],
        [
            place_scratch,
            pltpu.VMEM((4, 2 * ROWS, MODEL_WIDTH + RIDE), bf16),
            feed_scratch,
            feed_scratch,
            pltpu.VMEM((2 * ROWS, 1024), f32),
            dma(10),
        ],
        "feed",
        19000000000,
    )
    down_parts, up_parts = feed_parts[:4], feed_parts[4:]
    up_parts, down_parts, feed_placed = together((up_parts, down_parts, feed_placed))
    up_far = scatter_far(*up_parts[2:])
    up_far, feed_placed, down_parts = together((up_far, feed_placed, down_parts))
    feed_set = row_slice(feed_placed, core, (1024, 1024))
    up_sides, up_near, feed_set = together(
        (scatter_sides(up_far), add_cores(*up_parts[:2]), feed_set)
    )
    right, left = scatter_joined(up_near, *up_sides)
    right, left, down_parts = together((right, left, down_parts))
    up_moved = ring_x(right, 1), ring_x(left, -1)
    down_low = scatter_start(*down_parts)
    up_moved, down_low = together((up_moved, down_low))
    up_sum = up_near[0] + sum(part.astype(f32) for part in up_moved)
    up_back = up_sum[:, MODEL_WIDTH:].astype(bf16)
    grad_normed_two = up_sum[:, :MODEL_WIDTH] + dot(up_back, u_in)
    _, norm_two_back = jax.vjp(lambda v: layer_norm(v, gain_two, shift_two), middle)
    grad_middle = cotangent.astype(f32) + norm_two_back(grad_normed_two)[0]
    grad_branch = grad_middle.astype(bf16)

    branch_all = lax.all_gather(grad_branch, ("core", "x"), axis=0, tiled=True)
    branch_all = branch_all.reshape(2, 4, ROWS, MODEL_WIDTH)
    middle_slices = slices_of(
        at,
        [(up_back, normed_two), (output_inner, grad_branch)],
        "slices",
    )
    feed_set = jnp.concatenate(
        [
            feed_set,
            total(scatter_sequence(middle_slices)),
            jnp.full((16, 2 * RIDE), mine, jnp.int32).astype(bf16),
        ],
        axis=1,
    )
    feed_column, down_low = together((gather_y(feed_set), down_low))
    feed_column = jnp.stack(feed_column)
    feed_sides = ring_z(feed_column, -1), ring_z(feed_column, 1)
    down_moved = (ring_x(down_low[1], -1), ring_x(down_low[2], 1), ring_x(down_low[3], 2))
    placed, keyval_b, backs, backs_far, *query_parts = call(
        attention_back_kernel,
        2,
        at,
        [
            (branch_all, ANY),
            (w, ANY),
            (inner_one, step_block((4 * ROWS, RIDE))),
            (inner_far, step_block((4 * ROWS, RIDE))),
            (query, step_block((4 * ROWS, 256))),
            (keyval_all, step_block((8, ROWS, 256))),
            (lse_low, step_block((2, 2 * ROWS))),
            (lse_high, step_block((2, 2 * ROWS))),
            (att_low, step_block((2 * ROWS, 256))),
            (att_high, step_block((2 * ROWS, 256))),
            (o_out, None),
            (o_in, None),
            (q_out, None),
            (kv_out, None),
            (bias, None),
        ],
        [
            ((32, 512), f32, None),
            ((32, 256), f32, None),
            ((*group, RIDE), bf16, step_block((4 * ROWS, RIDE))),
            ((2, 32, 4 * ROWS), bf16, step_block((32, 4 * ROWS))),
            *part_outs(2688),
        ],
        [
            row_scratch,
            w_scratch,
            pltpu.VMEM((8 * ROWS, HEAD_WIDTH), f32),
            pltpu.VMEM((8 * ROWS, HEAD_WIDTH), f32),
            dma(3),
        ],
        "attention_back",
        short=True,
    )
    placed, keyval_b, backs, backs_far, query_parts, down_moved, feed_sides = together(
        (placed, keyval_b, backs, backs_far, query_parts, down_moved, feed_sides)
    )
    query_far, backs_far, placed, feed_column = together(
        (scatter_far(*query_parts[2:]), other_half(backs_far), placed, feed_column)
    )
    feed_far = ring_z(feed_column, 2)
    query_sides = scatter_sides(query_far)
    query_near = add_cores(*query_parts[:2])
    pack_shape = (4, ADAPTER_RANK, 1152)
    ride_block = pl.BlockSpec((ROWS, RIDE), lambda i, at: (0, MODEL_WIDTH // RIDE))
    late_mine, late_theirs = call(
        late_kernel,
        1,
        at,
        [
            *flat(normed_places),
            (backs, None),
            (backs_far, None),
            (keyval_b, None),
            (cotangent, None),
            *[(part, ride_block) for part in (down_low[0], *down_moved)],
        ],
        [((4, ADAPTER_RANK, 1664), bf16, None), (pack_shape, bf16, None)],
        [row_scratch, dma(2)],
        "late",
    )
    late_mine, late_theirs, query_near, query_sides = together(
        (late_mine, late_theirs, query_near, query_sides)
    )
    late_pack = add_cores(late_mine[..., :1152], late_theirs).astype(bf16)
    late_pack = jnp.concatenate([late_pack, late_mine[..., 1152:]], axis=-1)
    right, left = scatter_joined(query_near, *query_sides)
    late_pack, right, left = together((late_pack, right, left))
    query_moved = ring_x(right, 1), ring_x(left, -1)
    late_parts, feed_far, feed_column, feed_sides, down_moved = together(
        (scatter_sequence(late_pack), feed_far, feed_column, feed_sides, down_moved)
    )
    down_sum = down_low[0] + sum(part.astype(f32) for part in down_moved)
    placed = row_slice(placed, core, (256, 256))
    down_inner = down_sum[:, MODEL_WIDTH:].astype(bf16)
    layer_output = (
        middle
        + down_sum[:, :MODEL_WIDTH]
        + down_projection_bias.astype(f32)
        + dot(down_inner, d_out)
    ).astype(bf16)
    feed_pieces = [feed_column, feed_sides[0], feed_far, feed_sides[1]]
    late_set = jnp.concatenate([total(late_parts), placed], axis=-1)
    names = together(jnp.concatenate([piece[:, :1, 5120:5248] for piece in feed_pieces]))
    all_ids = names[:, 0, 0].astype(jnp.int32)
    feed_kept, feed_sent = sum_by_adapter(feed_pieces, core, all_ids)
    column = gather_y(late_set)
    feed_half = add_cores(feed_kept, feed_sent).astype(bf16)
    column, query_moved, feed_half = together((column, query_moved, feed_half))
    feed_sum = lax.all_gather(feed_half, ("core", "x"), axis=0).reshape(2, 4, 4, 16, 5376)
    late_pieces = gather_z(jnp.stack(column))
    query_sum = query_near[0] + sum(part.astype(f32) for part in query_moved)
    grad_keyval = (
        query_sum[:, 2048:2304] + other_half(query_sum[:, 2304:2560].astype(bf16)).astype(f32)
    ).astype(bf16)
    keyval_back = dot_t(grad_keyval, kv_out)
    keyval_back = jnp.where(jnp.arange(RIDE) // ADAPTER_RANK == 2 + core, keyval_back, 0.0)
    back = (query_sum[:, 2560:] + keyval_back).astype(bf16)
    grad_normed = (
        query_sum[:, :MODEL_WIDTH] + dot(back, q_in) + dot_t(grad_keyval, w[:, 256:512])
    )
    _, norm_one_back = jax.vjp(lambda v: layer_norm(v, gain_one, shift_one), input_rows)
    grad_tokens = (grad_middle + norm_one_back(grad_normed)[0]).astype(bf16)

    late_pieces, grad_tokens = together((late_pieces, grad_tokens))
    kept, sent = sum_by_adapter(late_pieces, core, all_ids)
    own_half = add_cores(kept, sent).astype(bf16)
    other_part = other_core(own_half)
    near = ring_by_core(jnp.concatenate([own_half, other_part], axis=0))
    far = ring_x(own_half, 2)
    feed_grads = spread_out(
        feed_spread_kernel, at, [feed_sum], (1024, 1024, 256, 256), "feed_spread"
    )
    near, far, feed_grads, layer_output = together((near, far, feed_grads, layer_output))
    up_b, down_a, up_a, output_b = feed_grads
    query_a, keyval_a, keyval_b, down_b, query_b, output_a = spread_out(
        late_spread_kernel,
        at,
        [own_half, other_part, near, other_core(near), far, other_core(far)],
        (256, 256, 64, 256, 256, 256),
        "late_spread",
        False,
    )

    def side_in(a):
        return jnp.swapaxes(a, 1, 2)

    return (
        layer_output,
        grad_tokens,
        side_in(query_a),
        query_b,
        side_in(keyval_a),
        keyval_b,
        side_in(output_a),
        output_b,
        side_in(up_a),
        up_b,
        side_in(down_a),
        down_b,
    )

def solution(mesh):
    fine = Mesh(mesh.devices.reshape(SIZES), AXES)
    in_specs = (
        P(AXES, None),
        P(AXES, None),
        P(),
        P(),
        P(DP, MP),
        P(MP),
        P(DP, None),
        P(),
        P(MP, DP),
        P(),
        P(),
        P(),
        P(DP, MP),
        P(MP),
        P(MP, DP),
        P(),
        P(DP, None),
        P(),
        P(None, None, MP),
        P(),
        P(),
        P(None, MP, None),
        P(),
        P(),
        P(None, None, MP),
        P(None, MP, None),
        P(),
    )
    out_specs = (P(AXES, None), P(AXES, None)) + (P(),) * 10
    return jax.shard_map(shards, mesh=fine, in_specs=in_specs, out_specs=out_specs, check_vma=False)
```
